512 devices in a mesh: dp: 32 (over x, y, core), vocab: 16 (over z).
Axes of the slice: x: 4, y: 4, z: 16, core: 2. Of those that a mesh axis runs over, the one named last changes fastest.
Arguments:
- query_hidden: bfloat16 [64, 32, 4096], P('dp'), may hold values from -6 to 6
- passage_hidden: bfloat16 [64, 96, 4096], P('dp'), may hold values from -6 to 6
- query_logits: float32 [64, 32, 16384], P('dp', None, 'vocab'), may hold values from -12 to 6
- passage_logits: float32 [64, 96, 16384], P('dp', None, 'vocab'), may hold values from -12 to 6
- head_weight: bfloat16 [16384, 4096], P('vocab', 'dp'), may hold values from -0.1875 to 0.1875
- query_mask: int32 [64, 32], P('dp'), may hold values from 0 to 1, as said below
- passage_mask: int32 [64, 96], P('dp'), may hold values from 0 to 1, as said below
- positive: int32 [64], replicated, may hold values from 0 to 63, as said below
- score_scale: float32 [1], replicated, may hold values from 256 to 768
Outputs:
- grad_query_hidden: bfloat16 [64, 32, 4096], P('dp', None, 'vocab')
- grad_passage_hidden: bfloat16 [64, 96, 4096], P('dp', None, 'vocab')
- grad_weight: float32 [16384, 4096], P('vocab', 'dp')
The draws below stay inside these ranges and needn't reach their ends.
Inputs may be any that keep to these rules, and one draw needn't show every extreme that they name: `query_mask`: each row is 1 on its first positions, at least 8 of them, and 0 after them. `passage_mask`: each row is 1 on its first positions, at least 24 of them, and 0 after them. The positive passage of query i is one of the 2 passages of its own group, from 2 * (i // 2) to 2 * (i // 2) + 1.
All inputs are finite; a program needn't handle non-finite values.
Results may differ from the reference program's by a relative error of at most 0.023.
Values may be sent and summed in bfloat16 or wider, within the bound.
A program may use at most 64 MiB of HBM per device.

```python
import math
import jax
import jax.numpy as jnp
from jax import lax

D = 4096
V_DEV = 1024
LQ = 32
LP = 96
NQ_G = 2
NP_G = 2
QUERIES = 64
PASSAGES = 64
VOCAB = 16384


def column_shift(key, incline):
    jitter = jax.random.uniform(jax.random.fold_in(key, 202), (VOCAB,), jnp.float32, -0.3, 0.3)
    return incline * (2.0 * jnp.arange(VOCAB, dtype=jnp.float32) / max(VOCAB - 1, 1) - 1.0) + jitter


def sequence_logits(key, row_count, length, column, incline):
    key_noise, key_shift = jax.random.split(key)
    jitter = jax.random.normal(key_noise, (row_count, length, VOCAB), jnp.float32)
    threshold = math.sqrt(2.0) * lax.erf_inv(jnp.float32(2.0 * 0.4 ** (1.0 / length) - 1.0))
    row_rank = jnp.arange(row_count, dtype=jnp.float32) / max(row_count - 1, 1)
    row_shift = incline * (2.0 * row_rank - 1.0) + jax.random.uniform(key_shift, (row_count,), jnp.float32, -0.3, 0.3)
    values = 1.5 * (jitter - threshold) + row_shift[:, None, None] + column[None, None, :]
    return jnp.clip(values, -12.0, 6.0)


def draw_query_logits(key, part):
    column = column_shift(key, 0.6)
    key = jax.random.fold_in(key, 1)
    return sequence_logits(key, QUERIES, LQ, column, 0.6)


def draw_passage_logits(key, part):
    column = column_shift(key, 0.6)
    key = jax.random.fold_in(key, 2)
    return sequence_logits(key, PASSAGES, LP, column, 0.6)


def draw_query_mask(key, part):
    key = jax.random.fold_in(key, 3)
    lengths = jax.random.randint(key, (QUERIES,), max(LQ // 4, 1), LQ + 1)
    return (jnp.arange(LQ)[None, :] < lengths[:, None]).astype(jnp.int32)


def draw_passage_mask(key, part):
    key = jax.random.fold_in(key, 4)
    lengths = jax.random.randint(key, (PASSAGES,), max(LP // 4, 1), LP + 1)
    return (jnp.arange(LP)[None, :] < lengths[:, None]).astype(jnp.int32)


def draw_positive(key, part):
    key = jax.random.fold_in(key, 5)
    within = jax.random.randint(key, (QUERIES,), 0, NP_G)
    return (jnp.arange(QUERIES) // NQ_G * NP_G + within).astype(jnp.int32)


def raised(entries, rng, source, target, parts, factor):
    def block_of(axis_at):
        return (jnp.arange(entries.shape[axis_at]) // (entries.shape[axis_at] // parts)).reshape((-1,) + (1,) * (entries.ndim - 1 - axis_at))

    first = jax.random.permutation(rng, parts)[block_of(target)]
    other_side = (block_of(target) + parts // 2) % parts
    return jnp.where((block_of(source) == first) | (block_of(source) == other_side), factor * entries, entries)


def block_scale(own_key, dims, cuts, low, high):
    level, own = 1.0, jax.random.fold_in(own_key, 6)
    for dim, parts in cuts:
        heights = jnp.exp(jax.random.uniform(jax.random.fold_in(own, dim), (parts,), jnp.float32, low / len(cuts), high / len(cuts)))
        level = level * jnp.repeat(heights, dims[dim] // parts).reshape([-1 if axis == dim else 1 for axis in range(len(dims))])
    return level


def gaussian(stream_key, shape, scale, most, cuts=(), kind=jnp.bfloat16):
    level = block_scale(stream_key, shape, cuts, -0.22, 0.18) if cuts else 1.0
    result = jax.random.normal(stream_key, shape, jnp.float32) * scale * level
    return jnp.minimum(jnp.maximum(result, -most), most).astype(kind)


def noise_with(own_key, extent, spread, limit, cuts, heavy, held_as=jnp.bfloat16):
    result = spread * jax.random.normal(own_key, extent, jnp.float32)
    if cuts:
        result = result * block_scale(own_key, extent, cuts, -0.22, 0.18)
    return jnp.clip(raised(result, jax.random.fold_in(own_key, 3), *heavy), -limit, limit).astype(held_as)


def setup_inputs(seed: int = 0) -> dict:
    arg_keys = jax.random.split(jax.random.key(seed), 10)
    query_hidden = gaussian(arg_keys[0], (QUERIES, LQ, D), 1.0, 6.0, ((0, 32),))
    passage_hidden = gaussian(arg_keys[1], (PASSAGES, LP, D), 1.0, 6.0, ((0, 32),))
    query_logits = draw_query_logits(jax.random.fold_in(arg_keys[9], 71), 0)
    passage_logits = draw_passage_logits(jax.random.fold_in(arg_keys[9], 71), 0)
    head_weight = noise_with(arg_keys[4], (VOCAB, D), D ** -0.5, 0.1875, ((0, 16), (1, 32)), (0, 1, 32, 2.75))
    query_mask = draw_query_mask(jax.random.fold_in(arg_keys[9], 71), 0)
    passage_mask = draw_passage_mask(jax.random.fold_in(arg_keys[9], 71), 0)
    positive = draw_positive(jax.random.fold_in(arg_keys[9], 71), 0)
    score_scale = jnp.clip(jax.random.uniform(arg_keys[8], (1,), jnp.float32, 256.0, 768.0), 256.0, 768.0)
    return {"query_hidden": query_hidden, "passage_hidden": passage_hidden, "query_logits": query_logits, "passage_logits": passage_logits, "head_weight": head_weight, "query_mask": query_mask, "passage_mask": passage_mask, "positive": positive, "score_scale": score_scale}


loss_scale = 256.0
query_weight = 3.0
passage_weight = 1.0
highest = lax.Precision.HIGHEST


def pooling(logits, padding):
    masked = jnp.where(padding[:, :, None] > 0, logits, -jnp.inf)
    return jnp.max(masked, axis=1), jnp.argmax(masked, axis=1).astype(jnp.int32)


def activate(pooled):
    return jnp.log1p(jnp.maximum(pooled, 0.0))


def slopes(pooled):
    return jnp.where(pooled > 0.0, 1.0 / (1.0 + jnp.maximum(pooled, 0.0)), 0.0)


def softmax_excess(scores, positive):
    largest = jnp.max(scores, axis=1, keepdims=True)
    weights = jnp.exp(scores - largest)
    target = (jnp.arange(scores.shape[1], dtype=jnp.int32)[None, :] == positive[:, None]).astype(jnp.float32)
    return weights / jnp.sum(weights, axis=1, keepdims=True) - target


def sequence_terms(hidden, where_max, push_rows, head_weight):
    sequences = hidden.shape[0]
    length = hidden.shape[1]
    shards = VOCAB // V_DEV
    positions = jnp.arange(length, dtype=jnp.int32)
    flat_hidden = hidden.reshape(sequences * length, D).astype(jnp.float32)
    spot_blocks = where_max.reshape(sequences, shards, V_DEV).transpose(1, 0, 2)
    push_blocks = push_rows.reshape(sequences, shards, V_DEV).transpose(1, 0, 2)
    weight_blocks = head_weight.reshape(shards, V_DEV, D)

    def accumulate(running, item_block):
        spot_block, push_block, weight_block = item_block
        table = jnp.where(positions[None, :, None] == spot_block[:, None, :], push_block[:, None, :].astype(jnp.float32), jnp.float32(0.0))
        table = table.reshape(sequences * length, V_DEV)
        section = jnp.dot(table, weight_block.astype(jnp.float32), preferred_element_type=jnp.float32).astype(jnp.bfloat16)
        section = lax.optimization_barrier(section)
        weight_part = lax.dot_general(table, flat_hidden, (((0,), (0,)), ((), ())), preferred_element_type=jnp.float32)
        return running + section.astype(jnp.float32), weight_part

    initial = jnp.zeros((sequences * length, D), jnp.float32)
    running, weight_parts = lax.scan(accumulate, initial, (spot_blocks, push_blocks, weight_blocks))
    return running.astype(jnp.bfloat16).reshape(sequences, length, D), weight_parts.reshape(VOCAB, D)


def reference(query_hidden, passage_hidden, query_logits, passage_logits, head_weight, query_mask, passage_mask, positive, score_scale):
    query_pool, query_where = pooling(query_logits, query_mask)
    passage_pool, passage_where = pooling(passage_logits, passage_mask)
    query_rep = activate(query_pool)
    passage_rep = activate(passage_pool)
    factor = score_scale[0] / VOCAB
    scores = jnp.dot(query_rep, passage_rep.T, precision=highest) * factor
    excess = softmax_excess(scores, positive)
    query_mean = jnp.sum(query_rep, axis=0) / QUERIES
    passage_mean = jnp.sum(passage_rep, axis=0) / PASSAGES
    query_grad = loss_scale * (factor * jnp.dot(excess, passage_rep, precision=highest) + (2.0 * query_weight / QUERIES) * query_mean[None, :])
    passage_grad = loss_scale * (factor * jnp.dot(excess.T, query_rep, precision=highest) + (2.0 * passage_weight / PASSAGES) * passage_mean[None, :])
    query_push = (query_grad * slopes(query_pool)).astype(jnp.bfloat16)
    passage_push = (passage_grad * slopes(passage_pool)).astype(jnp.bfloat16)
    query_out, query_weight_grad = sequence_terms(query_hidden, query_where, query_push, head_weight)
    passage_out, passage_weight_grad = sequence_terms(passage_hidden, passage_where, passage_push, head_weight)
    return (query_out, passage_out, query_weight_grad + passage_weight_grad)
```

```python
import functools

import jax
import jax.numpy as jnp
from jax import lax
from jax.experimental import pallas as pl
from jax.experimental.pallas import tpu as pltpu
from jax.sharding import PartitionSpec as P

MESH = pl.DeviceIdType.MESH
HIGHEST = lax.Precision.HIGHEST
LOSS_SCALE = 256.0
QUERY_WEIGHT = 3.0
PASSAGE_WEIGHT = 1.0
TURN = 3
F32 = jnp.float32
BF16 = jnp.bfloat16


def pooled(logits, length):
    spots = lax.broadcasted_iota(jnp.int32, logits.shape, 0).astype(F32)
    masked = jnp.where(spots < length, logits, -jnp.inf)
    largest = jnp.max(masked, axis=0, keepdims=True)
    where = jnp.min(jnp.where(masked == largest, spots, 1e9), axis=0, keepdims=True)
    return largest, where


def kernel(
    groups,
    planes,
    inverse,
    query_hidden,
    passage_hidden,
    query_logits,
    passage_logits,
    weight,
    query_mask,
    passage_mask,
    positive,
    scale,
    grad_query,
    grad_passage,
    grad_weight,
    pools,
    rep,
    push,
    part_out,
    part_in,
    part_sum,
    hidden,
    tables,
    partials,
    stage,
    inbox,
    last,
    total,
    pool_send,
    pool_recv,
    twin_send,
    twin_recv,
    one_send,
    one_recv,
    two_send,
    two_recv,
    hidden_send,
    hidden_recv,
    ring_send,
    ring_recv,
    last_send,
    last_recv,
):
    chips = groups // 2
    half = planes // 2
    query_length = query_logits.shape[1]
    passage_length = passage_logits.shape[1]
    vocab_local = query_logits.shape[2]
    query_rows = 2 * query_length
    rows = query_rows + 2 * passage_length
    width = weight.shape[1]
    queries = 2 * groups
    me = lax.axis_index("dp")
    z = lax.axis_index("vocab")
    column = lax.div(me, 2)
    core = lax.rem(me, 2)
    twin = 2 * column + 1 - core

    def ring(value, size):
        return lax.rem(value + 4 * size, size)

    def chunk_of(owner):
        return ring(column + (TURN + 1) * planes - TURN * owner, planes)

    own_chunk = chunk_of(z)
    source_plane = ring(inverse * ring(z - column, planes), planes)
    self_last = jnp.logical_and(z == column, own_chunk == column)

    barrier = pltpu.get_barrier_semaphore()

    def greet(dp_index, plane):
        pl.semaphore_signal(barrier, inc=1, device_id=(dp_index, plane), device_id_type=MESH)

    @pl.loop(1, groups)
    def _(i):
        greet(ring(me + i, groups), z)

    @pl.loop(1, planes)
    def _(i):
        greet(me, ring(z + i, planes))

    for u in range(2):
        target = 2 * own_chunk + u

        @pl.when(jnp.logical_not(jnp.logical_and(target == me, column == z)))
        def _():
            greet(target, column)

        source = 2 * z + u

        @pl.when(jnp.logical_not(jnp.logical_and(source == me, source_plane == z)))
        def _():
            greet(source, source_plane)

    def lengths(mask):
        return jnp.sum(mask[...].astype(F32), axis=1, keepdims=True)

    query_lengths = lengths(query_mask)
    passage_lengths = lengths(passage_mask)
    found = [pooled(query_logits[s], query_lengths[s : s + 1, :]) for s in range(2)]
    found += [pooled(passage_logits[s], passage_lengths[s : s + 1, :]) for s in range(2)]
    block = jnp.concatenate([f[0] for f in found] + [f[1] for f in found], axis=0)

    def slot(group):
        return pools.at[group]

    pools[me] = block

    pl.semaphore_wait(barrier, groups + planes + 2 - 2 * self_last.astype(jnp.int32))

    def pool_copy(group, target, m):
        return pltpu.make_async_remote_copy(
            src_ref=slot(group),
            dst_ref=slot(group),
            send_sem=pool_send.at[m],
            recv_sem=pool_recv.at[m],
            device_id=(target, z),
            device_id_type=MESH,
        )

    def twin_copy(group, m):
        return pltpu.make_async_remote_copy(
            src_ref=slot(group),
            dst_ref=slot(group),
            send_sem=twin_send.at[m],
            recv_sem=twin_recv.at[m],
            device_id=(twin, z),
            device_id_type=MESH,
        )

    @pl.loop(1, chips)
    def _(m):
        pool_copy(me, 2 * ring(column + m, chips) + core, m).start()

    twin_copy(me, 0).start()

    @pl.loop(1, chips)
    def _(m):
        from_group = 2 * ring(column - m, chips) + core
        pool_copy(from_group, me, m).wait_recv()
        twin_copy(from_group, m).start()

    @pl.loop(0, chips)
    def _(m):
        twin_copy(2 * ring(column - m, chips) + 1 - core, m).wait_recv()

    def pool_rows(k):
        return pools[:, k, :]

    for k in range(4):
        rep[k * groups : (k + 1) * groups, :] = jnp.log1p(jnp.maximum(pool_rows(k), 0.0))
    part = lax.dot_general(
        rep[0:queries, :],
        rep[...],
        (((1,), (1,)), ((), ())),
        precision=HIGHEST,
        preferred_element_type=F32,
    )
    share = queries // planes
    part_out[...] = jnp.zeros_like(part_out)
    for b in range(planes):
        part_out[8 * b : 8 * b + share, :] = part[b * share : (b + 1) * share, :]

    def tile(ref, plane):
        return ref.at[pl.ds(pl.multiple_of(plane * 8, 8), 8)]

    def one_copy(plane, i):
        return pltpu.make_async_remote_copy(
            src_ref=tile(part_out, plane),
            dst_ref=tile(part_in, z),
            send_sem=one_send.at[i],
            recv_sem=one_recv.at[i],
            device_id=(me, plane),
            device_id_type=MESH,
        )

    def two_copy(plane, i):
        return pltpu.make_async_remote_copy(
            src_ref=tile(part_sum, z),
            dst_ref=tile(part_sum, z),
            send_sem=two_send.at[i],
            recv_sem=two_recv.at[i],
            device_id=(me, plane),
            device_id_type=MESH,
        )

    @pl.loop(1, planes)
    def _(i):
        one_copy(ring(z + i, planes), i).start()

    def owner_at(j):
        i = lax.div(j + 1, 2)
        sign = 2 * lax.rem(j, 2) - 1
        return ring(z + sign * (half - i), planes)

    def hidden_parts(j, cr, target):
        out = []
        columns = pl.ds(pl.multiple_of(target * width, width), width)
        for p, (source, start, count) in enumerate(
            ((query_hidden, 0, query_rows), (passage_hidden, query_rows, rows - query_rows))
        ):
            first = pl.multiple_of(me * rows + start, 64)
            out.append(
                (
                    source.at[:, columns],
                    hidden.at[pl.ds(first, count)],
                    hidden_send.at[(2 * j + cr) * 2 + p],
                    hidden_recv.at[me * 2 + p],
                )
            )
        return out

    def hidden_target(j, cr):
        return 2 * ring(column + TURN * owner_at(j), planes) + cr

    def send_hidden(j):
        for cr in range(2):
            target = hidden_target(j, cr)

            @pl.when(target != me)
            def _():
                for source, dest, send, recv in hidden_parts(j, cr, target):
                    pltpu.make_async_remote_copy(
                        src_ref=source,
                        dst_ref=dest,
                        send_sem=send,
                        recv_sem=recv,
                        device_id=(target, z),
                        device_id_type=MESH,
                    ).start()

            @pl.when(target == me)
            def _():
                for source, dest, _, recv in hidden_parts(j, cr, target):
                    pltpu.make_async_copy(source, dest, recv).start()

    @pl.loop(0, planes // 2)
    def _(j):
        send_hidden(j)

    part_in[pl.ds(pl.multiple_of(z * 8, 8), 8), :] = part_out[
        pl.ds(pl.multiple_of(z * 8, 8), 8), :
    ]

    @pl.loop(1, planes)
    def _(i):
        one_copy(ring(z - i, planes), i).wait_recv()

    summed = part_in[0:8, :]
    for b in range(1, planes):
        summed = summed + part_in[8 * b : 8 * b + 8, :]
    part_sum[pl.ds(pl.multiple_of(z * 8, 8), 8), :] = summed

    @pl.loop(1, planes)
    def _(i):
        two_copy(ring(z + i, planes), i).start()

    @pl.loop(planes // 2, planes)
    def _(j):
        send_hidden(j)

    @pl.loop(1, planes)
    def _(i):
        two_copy(ring(z - i, planes), i).wait_recv()

    factor = scale[0] / (vocab_local * planes)
    sums = jnp.concatenate([part_sum[8 * b : 8 * b + share, :] for b in range(planes)], axis=0)
    lane = lax.broadcasted_iota(jnp.int32, sums.shape, 1)
    row = lax.broadcasted_iota(jnp.int32, sums.shape, 0)
    passage_lane = lane >= queries
    scores = jnp.where(passage_lane, sums * factor, -jnp.inf)
    weights = jnp.exp(scores - jnp.max(scores, axis=1, keepdims=True))
    soft = weights / jnp.sum(weights, axis=1, keepdims=True)
    square = (queries, queries)
    square_row = lax.broadcasted_iota(jnp.int32, square, 0)
    square_lane = lax.broadcasted_iota(jnp.int32, square, 1)
    query_of_row = jnp.where(square_row < groups, 2 * square_row, 2 * (square_row - groups) + 1)
    wanted = jnp.sum(
        jnp.where(
            square_lane == query_of_row,
            jnp.broadcast_to(positive[...].astype(F32), square),
            0.0,
        ),
        axis=1,
        keepdims=True,
    )
    passage_of_lane = jnp.where(
        lane < queries + groups, 2 * (lane - queries), 2 * (lane - queries - groups) + 1
    ).astype(F32)
    target_mark = jnp.where(jnp.logical_and(passage_lane, passage_of_lane == wanted), 1.0, 0.0)
    excess = soft - target_mark
    corner = jnp.concatenate([excess, jnp.zeros_like(excess)], axis=0)
    full_row = lax.broadcasted_iota(jnp.int32, corner.shape, 0)
    full_lane = lax.broadcasted_iota(jnp.int32, corner.shape, 1)
    query_part = jnp.logical_and(full_row < queries, full_lane < queries)
    passage_part = jnp.logical_and(full_row >= queries, full_lane >= queries)
    means = jnp.where(
        query_part,
        2.0 * QUERY_WEIGHT / queries / queries,
        jnp.where(passage_part, 2.0 * PASSAGE_WEIGHT / queries / queries, 0.0),
    )
    mixing = LOSS_SCALE * (factor * (corner + corner.T) + means)
    gradient = jnp.dot(mixing, rep[...], precision=HIGHEST, preferred_element_type=F32)
    for k in range(4):
        pool = pool_rows(k)
        slope = jnp.where(pool > 0.0, 1.0 / (1.0 + jnp.maximum(pool, 0.0)), 0.0)
        pushed = gradient[k * groups : (k + 1) * groups, :] * slope
        push[k * groups : (k + 1) * groups, :] = pushed.astype(BF16).astype(F32)

    def spread(group):
        first = pl.multiple_of(group * rows, 64)
        start = 0
        for k in range(4):
            length = query_length if k < 2 else passage_length
            push_row = push[pl.ds(k * groups + group, 1), :]
            spot_row = pools[group, 4 + k : 5 + k, :]
            positions = lax.broadcasted_iota(jnp.int32, (length, vocab_local), 0).astype(F32)
            tables[pl.ds(first + start, length), :] = jnp.where(
                positions == spot_row, push_row, 0.0
            ).astype(BF16)
            start += length
        return jnp.dot(
            tables[pl.ds(first, rows), :], weight[...], preferred_element_type=F32
        )

    def place(way, step, u):
        return (way * half + step) * 2 + u

    def ring_copy(way, step, u):
        index = place(way, step, u)
        neighbour = ring(z + 1 - 2 * way, planes)
        return pltpu.make_async_remote_copy(
            src_ref=stage.at[index],
            dst_ref=inbox.at[index],
            send_sem=ring_send.at[index],
            recv_sem=ring_recv.at[index],
            device_id=(me, neighbour),
            device_id_type=MESH,
        )

    def owner_of(way, step):
        return ring(z + (1 - 2 * way) * (half - step), planes)

    def ring_step(step, chains):
        for n, (way, u, _) in enumerate(chains):
            partials[n] = spread(2 * chunk_of(owner_of(way, step)) + u)
        for n, (way, u, follows) in enumerate(chains):
            value = partials[n]
            if follows:
                ring_copy(way, step - 1, u).wait_recv()
                value = value + inbox[place(way, step - 1, u)].astype(F32)
            stage[place(way, step, u)] = value.astype(BF16)
            ring_copy(way, step, u).start()

    def add_weight(owner):
        chunk = chunk_of(owner)

        for u in range(2):
            group = 2 * chunk + u
            for p, (start, count) in enumerate(((0, query_rows), (query_rows, rows - query_rows))):
                landed = hidden.at[pl.ds(pl.multiple_of(group * rows + start, 64), count)]
                pltpu.make_async_copy(landed, landed, hidden_recv.at[group * 2 + p]).wait()
        first = pl.multiple_of(chunk * 2 * rows, 64)
        total[...] += lax.dot_general(
            hidden[pl.ds(first, 2 * rows), :],
            tables[pl.ds(first, 2 * rows), :],
            (((0,), (0,)), ((), ())),
            preferred_element_type=F32,
        )

    total[...] = jnp.zeros_like(total)
    ring_step(0, ((0, 0, False), (1, 1, False)))
    ring_step(1, ((0, 0, True), (1, 1, True), (0, 1, False), (1, 0, False)))

    @pl.loop(2, half)
    def _(step):
        ring_step(step, ((0, 0, True), (1, 1, True), (0, 1, True), (1, 0, True)))
        for way in range(2):
            add_weight(owner_of(way, step - 1))

    def last_parts(u):
        out = []
        columns = pl.ds(pl.multiple_of(core * width, width), width)
        for p, (dest, start, count) in enumerate(
            ((grad_query, 0, query_rows), (grad_passage, query_rows, rows - query_rows))
        ):
            out.append(
                (
                    last.at[u, pl.ds(start, count)],
                    dest.at[:, columns],
                    last_send.at[u * 2 + p],
                    last_recv.at[core * 2 + p],
                )
            )
        return out

    def last_remote(u):
        return [
            pltpu.make_async_remote_copy(
                src_ref=source,
                dst_ref=dest,
                send_sem=send,
                recv_sem=recv,
                device_id=(2 * own_chunk + u, column),
                device_id_type=MESH,
            )
            for source, dest, send, recv in last_parts(u)
        ]

    def to_self(u):
        return jnp.logical_and(2 * own_chunk + u == me, column == z)

    for u in range(2):
        partials[u] = spread(2 * own_chunk + u)
    for u in range(2):
        value = partials[u]
        for way in range(2):
            ring_copy(way, half - 1, u).wait_recv()
            value = value + inbox[place(way, half - 1, u)].astype(F32)
        last[u] = value.astype(BF16)

        @pl.when(jnp.logical_not(to_self(u)))
        def _():
            for copy in last_remote(u):
                copy.start()

        @pl.when(to_self(u))
        def _():
            for source, dest, _, recv in last_parts(u):
                pltpu.make_async_copy(source, dest, recv).start()

    for way in range(2):
        add_weight(owner_of(way, half - 1))
    add_weight(owner_of(0, 0))
    add_weight(z)
    grad_weight[...] = total[...].T

    for h in range(2):
        columns = pl.ds(h * width, width)
        for p, (dest, count) in enumerate(
            ((grad_query, query_rows), (grad_passage, rows - query_rows))
        ):
            landed = dest.at[:, columns]
            pltpu.make_async_copy(landed, landed, last_recv.at[h * 2 + p]).wait()
    for u in range(2):

        @pl.when(jnp.logical_not(to_self(u)))
        def _():
            for copy in last_remote(u):
                copy.wait_send()

    for way in range(2):
        for u in range(2):

            @pl.loop(0 if way == u else 1, half)
            def _(step):
                ring_copy(way, step, u).wait_send()

    @pl.loop(0, planes)
    def _(j):
        for cr in range(2):
            target = hidden_target(j, cr)

            @pl.when(target != me)
            def _():
                for source, dest, send, recv in hidden_parts(j, cr, target):
                    pltpu.make_async_remote_copy(
                        src_ref=source,
                        dst_ref=dest,
                        send_sem=send,
                        recv_sem=recv,
                        device_id=(target, z),
                        device_id_type=MESH,
                    ).wait_send()

    @pl.loop(1, planes)
    def _(i):
        one_copy(ring(z + i, planes), i).wait_send()
        two_copy(ring(z + i, planes), i).wait_send()

    @pl.loop(1, chips)
    def _(m):
        pool_copy(me, 2 * ring(column + m, chips) + core, m).wait_send()

    @pl.loop(0, chips)
    def _(m):
        twin_copy(me, m).wait_send()


def on_device(
    groups,
    planes,
    query_hidden,
    passage_hidden,
    query_logits,
    passage_logits,
    head_weight,
    query_mask,
    passage_mask,
    positive,
    score_scale,
):
    width = query_hidden.shape[2]
    query_rows = query_hidden.shape[0] * query_hidden.shape[1]
    passage_rows = passage_hidden.shape[0] * passage_hidden.shape[1]
    rows = query_rows + passage_rows
    vocab_local, block = head_weight.shape
    chips = groups // 2
    half = planes // 2
    sequences = 4 * groups
    inverse = pow(TURN, -1, planes)
    vmem = pl.BlockSpec(memory_space=pltpu.VMEM)
    anywhere = pl.BlockSpec(memory_space=pl.ANY)
    units = 4 * half
    dma = pltpu.SemaphoreType.DMA
    grad_query, grad_passage, grad_weight = pl.pallas_call(
        functools.partial(kernel, groups, planes, inverse),
        out_shape=(
            jax.ShapeDtypeStruct((query_rows, 2 * block), BF16),
            jax.ShapeDtypeStruct((passage_rows, 2 * block), BF16),
            jax.ShapeDtypeStruct((vocab_local, block), F32),
        ),
        in_specs=[anywhere] * 2 + [vmem] * 6 + [pl.BlockSpec(memory_space=pltpu.SMEM)],
        out_specs=(anywhere, anywhere, vmem),
        scratch_shapes=[
            pltpu.VMEM((groups, 8, vocab_local), F32),
            pltpu.VMEM((sequences, vocab_local), F32),
            pltpu.VMEM((sequences, vocab_local), F32),
            pltpu.VMEM((8 * planes, sequences), F32),
            pltpu.VMEM((8 * planes, sequences), F32),
            pltpu.VMEM((8 * planes, sequences), F32),
            pltpu.VMEM((groups * rows, block), BF16),
            pltpu.VMEM((groups * rows, vocab_local), BF16),
            pltpu.VMEM((4, rows, block), F32),
            pltpu.VMEM((units, rows, block), BF16),
            pltpu.VMEM((units, rows, block), BF16),
            pltpu.VMEM((2, rows, block), BF16),
            pltpu.VMEM((block, vocab_local), F32),
            dma((chips,)),
            dma((chips,)),
            dma((chips,)),
            dma((chips,)),
            dma((planes,)),
            dma((planes,)),
            dma((planes,)),
            dma((planes,)),
            dma((4 * planes,)),
            dma((2 * groups,)),
            dma((units,)),
            dma((units,)),
            dma((4,)),
            dma((4,)),
        ],
        compiler_params=pltpu.CompilerParams(
            collective_id=0, has_side_effects=True, vmem_limit_bytes=48 * 1024 * 1024
        ),
    )(
        query_hidden.reshape(query_rows, width),
        passage_hidden.reshape(passage_rows, width),
        query_logits,
        passage_logits,
        head_weight,
        query_mask,
        passage_mask,
        positive.reshape(1, -1),
        score_scale,
    )
    return (
        grad_query.reshape(query_hidden.shape[:2] + (2 * block,)),
        grad_passage.reshape(passage_hidden.shape[:2] + (2 * block,)),
        grad_weight,
    )


def solution(mesh):
    in_specs = (
        P("dp", None, None),
        P("dp", None, None),
        P("dp", None, "vocab"),
        P("dp", None, "vocab"),
        P("vocab", "dp"),
        P("dp", None),
        P("dp", None),
        P(),
        P(),
    )
    out_specs = (P("dp", None, "vocab"), P("dp", None, "vocab"), P("vocab", "dp"))
    return jax.shard_map(
        functools.partial(on_device, mesh.shape["dp"], mesh.shape["vocab"]),
        mesh=mesh,
        in_specs=in_specs,
        out_specs=out_specs,
        check_vma=False,
    )
```

```python
import functools

import jax
import jax.numpy as jnp
from jax import lax
from jax.experimental import pallas as pl
from jax.experimental.pallas import tpu as pltpu
from jax.sharding import PartitionSpec as P

MESH = pl.DeviceIdType.MESH
HIGHEST = lax.Precision.HIGHEST
LOSS_SCALE = 256.0
QUERY_WEIGHT = 3.0
PASSAGE_WEIGHT = 1.0
F32 = jnp.float32
BF16 = jnp.bfloat16


def pooled(logits, length):
    spots = lax.broadcasted_iota(jnp.int32, logits.shape, 0).astype(F32)
    masked = jnp.where(spots < length, logits, -jnp.inf)
    largest = jnp.max(masked, axis=0, keepdims=True)
    where = jnp.min(jnp.where(masked == largest, spots, 1e9), axis=0, keepdims=True)
    return largest, where


def kernel(
    groups,
    planes,
    query_hidden,
    passage_hidden,
    query_logits_in,
    passage_logits_in,
    weight_in,
    query_mask_in,
    passage_mask_in,
    positive_in,
    scale,
    grad_query,
    grad_passage,
    grad_weight,
    query_logits,
    passage_logits,
    weight,
    query_mask,
    passage_mask,
    positive,
    pools,
    spots,
    rep,
    push,
    part_out,
    part_in,
    part_sum,
    turned,
    mixed,
    hidden,
    tables,
    partial,
    stage,
    inbox,
    last,
    final,
    total,
    load,
    pool_send,
    pool_recv,
    twin_send,
    twin_recv,
    spot_send,
    spot_recv,
    spot_twin_send,
    spot_twin_recv,
    one_send,
    one_recv,
    two_send,
    two_recv,
    mixed_send,
    mixed_recv,
    hidden_send,
    hidden_recv,
    ring_send,
    ring_recv,
    last_send,
    last_recv,
):
    chips = groups // 2
    half = planes // 2
    query_length = query_logits.shape[1]
    passage_length = passage_logits.shape[1]
    vocab_local = query_logits.shape[2]
    query_rows = 2 * query_length
    rows = query_rows + 2 * passage_length
    width = weight.shape[1]
    queries = 2 * groups
    strip = 2 * width // chips
    span = rows * chips // 2
    me = lax.axis_index("dp")
    z = lax.axis_index("vocab")
    column = lax.div(me, 2)
    core = lax.rem(me, 2)
    twin = 2 * column + 1 - core

    def ring(value, size):
        return lax.rem(value + 2 * size, size)

    def remote(source, dest, send, recv, target, plane):
        return pltpu.make_async_remote_copy(
            src_ref=source,
            dst_ref=dest,
            send_sem=send,
            recv_sem=recv,
            device_id=(target, plane),
            device_id_type=MESH,
        )

    loads = [
        pltpu.make_async_copy(source, dest, load.at[n])
        for n, (source, dest) in enumerate(
            (
                (query_mask_in, query_mask),
                (passage_mask_in, passage_mask),
                (query_logits_in, query_logits),
                (passage_logits_in, passage_logits),
                (weight_in, weight),
                (positive_in, positive),
            )
        )
    ]
    for copy in loads:
        copy.start()

    barrier = pltpu.get_barrier_semaphore()

    def greet(dp_index, plane):
        pl.semaphore_signal(barrier, inc=1, device_id=(dp_index, plane), device_id_type=MESH)

    @pl.loop(1, groups)
    def _(i):
        greet(ring(me + i, groups), z)

    @pl.loop(1, planes)
    def _(i):
        greet(me, ring(z + i, planes))

    def lengths(mask):
        return jnp.sum(mask[...].astype(F32), axis=1, keepdims=True)

    for copy in loads[:4]:
        copy.wait()
    query_lengths = lengths(query_mask)
    passage_lengths = lengths(passage_mask)
    found = [pooled(query_logits[s], query_lengths[s : s + 1, :]) for s in range(2)]
    found += [pooled(passage_logits[s], passage_lengths[s : s + 1, :]) for s in range(2)]
    middle = vocab_local // 2

    def folded(lines):
        return jnp.concatenate(
            [line[:, :middle] for line in lines] + [line[:, middle:] for line in lines], axis=0
        )

    pools[me] = folded([f[0] for f in found])
    spots[me] = folded([f[1] for f in found])

    pl.semaphore_wait(barrier, groups + planes - 2)

    def plane_copy(ref, send, recv, group, target, m):
        return remote(ref.at[group], ref.at[group], send.at[m], recv.at[m], target, z)

    def pool_copy(group, target, m):
        return plane_copy(pools, pool_send, pool_recv, group, target, m)

    def pool_twin(group, m):
        return plane_copy(pools, twin_send, twin_recv, group, twin, m)

    def spot_copy(group, target, m):
        return plane_copy(spots, spot_send, spot_recv, group, target, m)

    def spot_twin(group, m):
        return plane_copy(spots, spot_twin_send, spot_twin_recv, group, twin, m)

    def spread_out(copy, twin_copy):
        @pl.loop(1, chips)
        def _(m):
            copy(me, 2 * ring(column + m, chips) + core, m).start()

        twin_copy(me, 0).start()

    def hand_on(copy, twin_copy):
        @pl.loop(1, chips)
        def _(m):
            group = 2 * ring(column - m, chips) + core
            copy(group, me, m).wait_recv()
            twin_copy(group, m).start()

    def take_from_twin(twin_copy):
        @pl.loop(0, chips)
        def _(m):
            twin_copy(2 * ring(column - m, chips) + 1 - core, m).wait_recv()

    spread_out(pool_copy, pool_twin)
    hand_on(pool_copy, pool_twin)
    spread_out(spot_copy, spot_twin)
    take_from_twin(pool_twin)

    def pool_rows(k):
        return jnp.concatenate([pools[:, k, :], pools[:, 4 + k, :]], axis=1)

    for k in range(4):
        rep[k * groups : (k + 1) * groups, :] = jnp.log1p(jnp.maximum(pool_rows(k), 0.0))
    part = lax.dot_general(
        rep[0:queries, :],
        rep[...],
        (((1,), (1,)), ((), ())),
        precision=HIGHEST,
        preferred_element_type=F32,
    )
    share = queries // chips
    part_out[...] = jnp.zeros_like(part_out)
    for b in range(chips):
        part_out[8 * b : 8 * b + share, :] = part[b * share : (b + 1) * share, :]

    def tile(ref, index):
        return ref.at[pl.ds(pl.multiple_of(index * 8, 8), 8)]

    def one_copy(plane, i):
        return remote(
            tile(part_out, column), tile(part_in, z), one_send.at[i], one_recv.at[i], me, plane
        )

    def two_copy(chip, i):
        return remote(
            tile(part_sum, column),
            tile(part_sum, column),
            two_send.at[i],
            two_recv.at[i],
            2 * chip + core,
            z,
        )

    @pl.loop(1, planes)
    def _(i):
        one_copy(ring(z + i, planes), i).start()

    part_in[pl.ds(pl.multiple_of(z * 8, 8), 8), :] = part_out[
        pl.ds(pl.multiple_of(column * 8, 8), 8), :
    ]

    for copy in loads[4:]:
        copy.wait()
    turned[...] = weight[...].astype(F32).T.astype(BF16)

    def strip_rows(ref, index):
        return ref.at[pl.ds(pl.multiple_of(index * strip, strip), strip)]

    def mixed_target(i):
        chip = core * half + lax.div(i, 2)
        return 2 * ring(chip + column, half) + 2 * core * half + lax.rem(i, 2)

    def mixed_copy(i):
        target = mixed_target(i)
        return remote(
            strip_rows(turned, lax.div(target, 2) - core * half),
            strip_rows(mixed, column),
            mixed_send.at[i],
            mixed_recv.at[column],
            target,
            z,
        )

    @pl.loop(0, 2 * half)
    def _(i):
        @pl.when(mixed_target(i) != me)
        def _():
            mixed_copy(i).start()

        @pl.when(mixed_target(i) == me)
        def _():
            pltpu.make_async_copy(
                strip_rows(turned, column - core * half),
                strip_rows(mixed, column),
                mixed_recv.at[column],
            ).start()

    def hidden_parts(j, cr, target):
        out = []
        columns = pl.ds(pl.multiple_of(target * width, width), width)
        for p, (source, start, count) in enumerate(
            ((query_hidden, 0, query_rows), (passage_hidden, query_rows, rows - query_rows))
        ):
            first = pl.multiple_of(me * rows + start, 64)
            out.append(
                (
                    source.at[:, columns],
                    hidden.at[pl.ds(first, count)],
                    hidden_send.at[(2 * j + cr) * 2 + p],
                    hidden_recv.at[me * 2 + p],
                )
            )
        return out

    def hidden_target(j, cr):
        return 2 * ring(column - j, chips) + cr

    def send_hidden(j):
        for cr in range(2):
            target = hidden_target(j, cr)

            @pl.when(target != me)
            def _():
                for source, dest, send, recv in hidden_parts(j, cr, target):
                    remote(source, dest, send, recv, target, z).start()

            @pl.when(target == me)
            def _():
                for source, dest, _, recv in hidden_parts(j, cr, target):
                    pltpu.make_async_copy(source, dest, recv).start()

    @pl.loop(0, chips // 2)
    def _(j):
        send_hidden(j)

    @pl.loop(1, planes)
    def _(i):
        one_copy(ring(z - i, planes), i).wait_recv()

    summed = part_in[0:8, :]
    for b in range(1, planes):
        summed = summed + part_in[8 * b : 8 * b + 8, :]
    part_sum[pl.ds(pl.multiple_of(column * 8, 8), 8), :] = summed

    @pl.loop(1, chips)
    def _(i):
        two_copy(ring(column + i, chips), i).start()

    hand_on(spot_copy, spot_twin)

    @pl.loop(chips // 2, chips)
    def _(j):
        send_hidden(j)

    @pl.loop(1, chips)
    def _(i):
        other = ring(column - i, chips)
        remote(
            tile(part_sum, other),
            tile(part_sum, other),
            two_send.at[i],
            two_recv.at[i],
            me,
            z,
        ).wait_recv()

    factor = scale[0] / (vocab_local * planes)
    sums = jnp.concatenate([part_sum[8 * b : 8 * b + share, :] for b in range(chips)], axis=0)
    lane = lax.broadcasted_iota(jnp.int32, sums.shape, 1)
    passage_lane = lane >= queries
    scores = jnp.where(passage_lane, sums * factor, -jnp.inf)
    weights = jnp.exp(scores - jnp.max(scores, axis=1, keepdims=True))
    soft = weights / jnp.sum(weights, axis=1, keepdims=True)
    square = (queries, queries)
    square_row = lax.broadcasted_iota(jnp.int32, square, 0)
    square_lane = lax.broadcasted_iota(jnp.int32, square, 1)
    query_of_row = jnp.where(square_row < groups, 2 * square_row, 2 * (square_row - groups) + 1)
    wanted = jnp.sum(
        jnp.where(
            square_lane == query_of_row,
            jnp.broadcast_to(positive[...].astype(F32), square),
            0.0,
        ),
        axis=1,
        keepdims=True,
    )
    passage_of_lane = jnp.where(
        lane < queries + groups, 2 * (lane - queries), 2 * (lane - queries - groups) + 1
    ).astype(F32)
    target_mark = jnp.where(jnp.logical_and(passage_lane, passage_of_lane == wanted), 1.0, 0.0)
    excess = soft - target_mark
    corner = jnp.concatenate([excess, jnp.zeros_like(excess)], axis=0)
    full_row = lax.broadcasted_iota(jnp.int32, corner.shape, 0)
    full_lane = lax.broadcasted_iota(jnp.int32, corner.shape, 1)
    query_part = jnp.logical_and(full_row < queries, full_lane < queries)
    passage_part = jnp.logical_and(full_row >= queries, full_lane >= queries)
    means = jnp.where(
        query_part,
        2.0 * QUERY_WEIGHT / queries / queries,
        jnp.where(passage_part, 2.0 * PASSAGE_WEIGHT / queries / queries, 0.0),
    )
    mixing = LOSS_SCALE * (factor * (corner + corner.T) + means)
    gradient = jnp.dot(mixing, rep[...], precision=HIGHEST, preferred_element_type=F32)
    for k in range(4):
        pool = pool_rows(k)
        slope = jnp.where(pool > 0.0, 1.0 / (1.0 + jnp.maximum(pool, 0.0)), 0.0)
        pushed = gradient[k * groups : (k + 1) * groups, :] * slope
        push[k * groups : (k + 1) * groups, :] = pushed.astype(BF16).astype(F32)

    take_from_twin(spot_twin)

    @pl.loop(0, chips)
    def _(chip):
        landed = strip_rows(mixed, chip)
        pltpu.make_async_copy(landed, landed, mixed_recv.at[chip]).wait()

    def table(group):
        return tables.at[pl.ds(pl.multiple_of(group * rows, rows), rows)]

    def build(group):
        first = group * rows
        start = 0
        for k in range(4):
            length = query_length if k < 2 else passage_length
            push_row = push[pl.ds(k * groups + group, 1), :]
            spot_row = jnp.concatenate(
                [spots[group, k : k + 1, :], spots[group, 4 + k : 5 + k, :]], axis=1
            )
            positions = lax.broadcasted_iota(jnp.int32, (length, vocab_local), 0).astype(F32)
            tables[pl.ds(pl.multiple_of(first + start, 32), length), :] = jnp.where(
                positions == spot_row, push_row, 0.0
            ).astype(BF16)
            start += length

    def sum_unit(u):
        @pl.loop(u * (chips // 2), (u + 1) * (chips // 2))
        def _(j):
            group = 2 * j + core
            build(group)
            partial[:, pl.ds(pl.multiple_of(j * rows, rows), rows)] = lax.dot_general(
                mixed[...],
                table(group)[...],
                (((1,), (1,)), ((), ())),
                preferred_element_type=F32,
            )

    def own_part(plane, u):
        return partial[
            pl.ds(pl.multiple_of(plane * strip, strip), strip), u * span : (u + 1) * span
        ]

    def place(way, step, u):
        return (way * half + step) * 2 + u

    def ring_copy(way, step, u):
        index = place(way, step, u)
        neighbour = ring(z + 1 - 2 * way, planes)
        return remote(
            stage.at[index], inbox.at[index], ring_send.at[index], ring_recv.at[index], me, neighbour
        )

    def owner_of(way, step):
        return ring(z + (1 - 2 * way) * (half - step), planes)

    def ring_step(step, chains):
        for way, u, follows in chains:
            value = own_part(owner_of(way, step), u)
            if follows:
                ring_copy(way, step - 1, u).wait_recv()
                value = value + inbox[place(way, step - 1, u)].astype(F32)
            stage[place(way, step, u)] = value.astype(BF16)
            ring_copy(way, step, u).start()

    def add_weight(m):
        chip = ring(column + m, chips)
        build(2 * chip + 1 - core)
        for u in range(2):
            group = 2 * chip + u
            for p, (start, count) in enumerate(((0, query_rows), (query_rows, rows - query_rows))):
                landed = hidden.at[pl.ds(pl.multiple_of(group * rows + start, 64), count)]
                pltpu.make_async_copy(landed, landed, hidden_recv.at[group * 2 + p]).wait()
        first = pl.multiple_of(chip * 2 * rows, 64)
        total[...] += lax.dot_general(
            hidden[pl.ds(first, 2 * rows), :],
            tables[pl.ds(first, 2 * rows), :],
            (((0,), (0,)), ((), ())),
            preferred_element_type=F32,
        )

    sum_unit(0)
    ring_step(0, ((0, 0, False),))
    sum_unit(1)
    ring_step(0, ((1, 1, False),))
    ring_step(1, ((0, 0, True), (1, 0, False), (0, 1, False), (1, 1, True)))
    total[...] = jnp.zeros_like(total)

    @pl.loop(2, half)
    def _(step):
        ring_step(step, ((0, 0, True), (1, 0, True), (0, 1, True), (1, 1, True)))
        for i in range(2):
            add_weight(2 * (step - 2) + i)

    def last_copy(j, target):
        return remote(
            last.at[:, pl.ds(pl.multiple_of(j * rows, rows), rows)],
            strip_rows(final, column),
            last_send.at[j],
            last_recv.at[column],
            target,
            z,
        )

    for u in range(2):
        value = own_part(z, u)
        for way in range(2):
            ring_copy(way, half - 1, u).wait_recv()
            value = value + inbox[place(way, half - 1, u)].astype(F32)
        last[:, u * span : (u + 1) * span] = value.astype(BF16)

        @pl.loop(u * (chips // 2), (u + 1) * (chips // 2))
        def _(j):
            @pl.when(j != column)
            def _():
                last_copy(j, 2 * j + core).start()

            @pl.when(j == column)
            def _():
                pltpu.make_async_copy(
                    last.at[:, pl.ds(pl.multiple_of(j * rows, rows), rows)],
                    strip_rows(final, column),
                    last_recv.at[column],
                ).start()

    @pl.loop(2 * (half - 2), chips)
    def _(m):
        add_weight(m)

    grad_weight[...] = total[...].T

    @pl.loop(0, chips)
    def _(chip):
        landed = strip_rows(final, chip)
        pltpu.make_async_copy(landed, landed, last_recv.at[chip]).wait()

    whole = final[...].astype(F32).T.astype(BF16)
    grad_query[...] = whole[:query_rows, :]
    grad_passage[...] = whole[query_rows:, :]

    @pl.loop(0, chips)
    def _(j):
        @pl.when(j != column)
        def _():
            last_copy(j, 2 * j + core).wait_send()

    for way in range(2):
        for u in range(2):

            @pl.loop(0 if way == u else 1, half)
            def _(step):
                ring_copy(way, step, u).wait_send()

    @pl.loop(0, chips)
    def _(j):
        for cr in range(2):
            target = hidden_target(j, cr)

            @pl.when(target != me)
            def _():
                for source, dest, send, recv in hidden_parts(j, cr, target):
                    remote(source, dest, send, recv, target, z).wait_send()

    @pl.loop(0, 2 * half)
    def _(i):
        @pl.when(mixed_target(i) != me)
        def _():
            mixed_copy(i).wait_send()

    @pl.loop(1, planes)
    def _(i):
        one_copy(ring(z + i, planes), i).wait_send()

    @pl.loop(1, chips)
    def _(m):
        two_copy(ring(column + m, chips), m).wait_send()
        pool_copy(me, 2 * ring(column + m, chips) + core, m).wait_send()
        spot_copy(me, 2 * ring(column + m, chips) + core, m).wait_send()

    @pl.loop(0, chips)
    def _(m):
        pool_twin(me, m).wait_send()
        spot_twin(me, m).wait_send()


def on_device(
    groups,
    planes,
    query_hidden,
    passage_hidden,
    query_logits,
    passage_logits,
    head_weight,
    query_mask,
    passage_mask,
    positive,
    score_scale,
):
    width = query_hidden.shape[2]
    query_rows = query_hidden.shape[0] * query_hidden.shape[1]
    passage_rows = passage_hidden.shape[0] * passage_hidden.shape[1]
    rows = query_rows + passage_rows
    vocab_local, block = head_weight.shape
    chips = groups // 2
    half = planes // 2
    strip = 2 * block // chips
    sequences = 4 * groups
    vmem = pl.BlockSpec(memory_space=pltpu.VMEM)
    main = pl.BlockSpec(memory_space=pltpu.HBM)
    units = 4 * half
    dma = pltpu.SemaphoreType.DMA
    grad_query, grad_passage, grad_weight = pl.pallas_call(
        functools.partial(kernel, groups, planes),
        out_shape=(
            jax.ShapeDtypeStruct((query_rows, 2 * block), BF16),
            jax.ShapeDtypeStruct((passage_rows, 2 * block), BF16),
            jax.ShapeDtypeStruct((vocab_local, block), F32),
        ),
        in_specs=[main] * 8 + [pl.BlockSpec(memory_space=pltpu.SMEM)],
        out_specs=(vmem, vmem, vmem),
        scratch_shapes=[
            pltpu.VMEM(query_logits.shape, F32),
            pltpu.VMEM(passage_logits.shape, F32),
            pltpu.VMEM(head_weight.shape, BF16),
            pltpu.VMEM(query_mask.shape, jnp.int32),
            pltpu.VMEM(passage_mask.shape, jnp.int32),
            pltpu.VMEM((1, positive.shape[0]), jnp.int32),
            pltpu.VMEM((groups, 8, vocab_local // 2), F32),
            pltpu.VMEM((groups, 8, vocab_local // 2), F32),
            pltpu.VMEM((sequences, vocab_local), F32),
            pltpu.VMEM((sequences, vocab_local), F32),
            pltpu.VMEM((8 * chips, sequences), F32),
            pltpu.VMEM((8 * planes, sequences), F32),
            pltpu.VMEM((8 * chips, sequences), F32),
            pltpu.VMEM((block, vocab_local), BF16),
            pltpu.VMEM((2 * block, vocab_local), BF16),
            pltpu.VMEM((groups * rows, block), BF16),
            pltpu.VMEM((groups * rows, vocab_local), BF16),
            pltpu.VMEM((2 * block, chips * rows), F32),
            pltpu.VMEM((units, strip, chips * rows // 2), BF16),
            pltpu.VMEM((units, strip, chips * rows // 2), BF16),
            pltpu.VMEM((strip, chips * rows), BF16),
            pltpu.VMEM((2 * block, rows), BF16),
            pltpu.VMEM((block, vocab_local), F32),
            dma((6,)),
            dma((chips,)),
            dma((chips,)),
            dma((chips,)),
            dma((chips,)),
            dma((chips,)),
            dma((chips,)),
            dma((chips,)),
            dma((chips,)),
            dma((planes,)),
            dma((planes,)),
            dma((chips,)),
            dma((chips,)),
            dma((2 * half,)),
            dma((chips,)),
            dma((4 * chips,)),
            dma((2 * groups,)),
            dma((units,)),
            dma((units,)),
            dma((chips,)),
            dma((chips,)),
        ],
        compiler_params=pltpu.CompilerParams(
            collective_id=0, has_side_effects=True, vmem_limit_bytes=60 * 1024 * 1024
        ),
    )(
        query_hidden.reshape(query_rows, width),
        passage_hidden.reshape(passage_rows, width),
        query_logits,
        passage_logits,
        head_weight,
        query_mask,
        passage_mask,
        positive.reshape(1, -1),
        score_scale,
    )
    return (
        grad_query.reshape(query_hidden.shape[:2] + (2 * block,)),
        grad_passage.reshape(passage_hidden.shape[:2] + (2 * block,)),
        grad_weight,
    )


def solution(mesh):
    in_specs = (
        P("dp", None, None),
        P("dp", None, None),
        P("dp", None, "vocab"),
        P("dp", None, "vocab"),
        P("vocab", "dp"),
        P("dp", None),
        P("dp", None),
        P(),
        P(),
    )
    out_specs = (P("dp", None, "vocab"), P("dp", None, "vocab"), P("vocab", "dp"))
    return jax.shard_map(
        functools.partial(on_device, mesh.shape["dp"], mesh.shape["vocab"]),
        mesh=mesh,
        in_specs=in_specs,
        out_specs=out_specs,
        check_vma=False,
    )
```

```python
import functools

import jax
import jax.numpy as jnp
from jax import lax
from jax.experimental import pallas as pl
from jax.experimental.pallas import tpu as pltpu
from jax.sharding import PartitionSpec as P

MESH = pl.DeviceIdType.MESH
HIGHEST = lax.Precision.HIGHEST
LOSS_SCALE = 256.0
QUERY_WEIGHT = 3.0
PASSAGE_WEIGHT = 1.0
F32 = jnp.float32
BF16 = jnp.bfloat16
UNITS = 4


def pooled(logits, length):
    spots = lax.broadcasted_iota(jnp.int32, logits.shape, 0).astype(F32)
    masked = jnp.where(spots < length, logits, -jnp.inf)
    largest = jnp.max(masked, axis=0, keepdims=True)
    where = jnp.min(jnp.where(masked == largest, spots, 1e9), axis=0, keepdims=True)
    return largest, where


def kernel(
    groups,
    planes,
    query_hidden,
    passage_hidden,
    query_logits_in,
    passage_logits_in,
    weight_in,
    query_mask_in,
    passage_mask_in,
    positive_in,
    scale,
    grad_query,
    grad_passage,
    grad_weight,
    query_logits,
    passage_logits,
    weight,
    query_mask,
    passage_mask,
    positive,
    pools,
    spots,
    rep,
    push,
    part_out,
    part_in,
    part_sum,
    turned,
    mixed,
    hidden,
    tables,
    partial,
    stage,
    inbox,
    last,
    final,
    total,
    load,
    sent,
    pool_recv,
    twin_recv,
    spot_recv,
    spot_twin_recv,
    one_recv,
    two_recv,
    mixed_recv,
    mixed_twin_recv,
    hidden_recv,
    ring_recv,
    last_recv,
):
    chips = groups // 2
    half = planes // 2
    query_length = query_logits.shape[1]
    passage_length = passage_logits.shape[1]
    vocab_local = query_logits.shape[2]
    query_rows = 2 * query_length
    rows = query_rows + 2 * passage_length
    width = weight.shape[1]
    queries = 2 * groups
    strip = 2 * width // chips
    span = rows * chips // UNITS
    me = lax.axis_index("dp")
    z = lax.axis_index("vocab")
    column = lax.div(me, 2)
    core = lax.rem(me, 2)
    twin = 2 * column + 1 - core
    pool_sent, twin_sent, spot_sent, spot_twin_sent, one_sent = (sent.at[i] for i in range(5))
    two_sent, mixed_sent, mixed_twin_sent, hidden_sent = (sent.at[i] for i in range(5, 9))
    ring_sent, last_sent = sent.at[9], sent.at[10]

    def ring(value, size):
        return lax.rem(value + 2 * size, size)

    def remote(source, dest, send, recv, target, plane):
        return pltpu.make_async_remote_copy(
            src_ref=source,
            dst_ref=dest,
            send_sem=send,
            recv_sem=recv,
            device_id=(target, plane),
            device_id_type=MESH,
        )

    def settle(ref, sem):
        pltpu.make_async_copy(ref, ref, sem).wait()

    loads = [
        pltpu.make_async_copy(source, dest, load.at[n])
        for n, (source, dest) in enumerate(
            (
                (query_mask_in, query_mask),
                (passage_mask_in, passage_mask),
                (query_logits_in, query_logits),
                (passage_logits_in, passage_logits),
                (weight_in, weight),
                (positive_in, positive),
            )
        )
    ]
    for copy in loads:
        copy.start()

    barrier = pltpu.get_barrier_semaphore()

    def greet(dp_index, plane):
        pl.semaphore_signal(barrier, inc=1, device_id=(dp_index, plane), device_id_type=MESH)

    @pl.loop(1, planes)
    def _(i):
        greet(me, ring(z + i, planes))

    @pl.loop(1, groups)
    def _(i):
        greet(ring(me + i, groups), z)

    def lengths(mask):
        return jnp.sum(mask[...].astype(F32), axis=1, keepdims=True)

    for copy in loads[:4]:
        copy.wait()
    query_lengths = lengths(query_mask)
    passage_lengths = lengths(passage_mask)
    found = [pooled(query_logits[s], query_lengths[s : s + 1, :]) for s in range(2)]
    found += [pooled(passage_logits[s], passage_lengths[s : s + 1, :]) for s in range(2)]
    middle = vocab_local // 2

    def folded(lines):
        return jnp.concatenate(
            [line[:, :middle] for line in lines] + [line[:, middle:] for line in lines], axis=0
        )

    pools[me] = folded([f[0] for f in found])
    spots[me] = folded([f[1] for f in found])
    for copy in loads[4:]:
        copy.wait()
    turned[...] = weight[...].astype(F32).T.astype(BF16)

    pl.semaphore_wait(barrier, groups + planes - 2)

    def pool_copy(group, target, m):
        return remote(pools.at[group], pools.at[group], pool_sent, pool_recv.at[m], target, z)

    def pool_twin(group):
        return remote(pools.at[group], pools.at[group], twin_sent, twin_recv, twin, z)

    def spot_copy(group, target, m):
        return remote(spots.at[group], spots.at[group], spot_sent, spot_recv.at[m], target, z)

    def spot_twin(group):
        return remote(spots.at[group], spots.at[group], spot_twin_sent, spot_twin_recv, twin, z)

    def spread_out(copy, twin_copy):
        @pl.loop(1, chips)
        def _(m):
            copy(me, 2 * ring(column + m, chips) + core, m).start()

        twin_copy(me).start()

    def hand_on(copy, twin_copy):
        @pl.loop(1, chips)
        def _(m):
            group = 2 * ring(column - m, chips) + core
            copy(group, me, m).wait_recv()
            twin_copy(group).start()

    spread_out(pool_copy, pool_twin)
    hand_on(pool_copy, pool_twin)

    def strip_rows(ref, index):
        return ref.at[pl.ds(pl.multiple_of(index * strip, strip), strip)]

    @pl.loop(0, half)
    def _(i):
        chip = core * half + ring(i + column, half)

        @pl.when(chip != column)
        def _():
            remote(
                strip_rows(turned, chip - core * half),
                strip_rows(mixed, column),
                mixed_sent,
                mixed_recv.at[column],
                2 * chip + core,
                z,
            ).start()

        @pl.when(chip == column)
        def _():
            pltpu.make_async_copy(
                strip_rows(turned, chip - core * half),
                strip_rows(mixed, column),
                mixed_recv.at[column],
            ).start()

    takes_strips = core == lax.div(column, half)

    def pool_rows(k):
        return jnp.concatenate([pools[:, k, :], pools[:, 4 + k, :]], axis=1)

    settle(pools.at[pl.ds(0, chips)], twin_recv)
    for k in range(4):
        rep[k * groups : (k + 1) * groups, :] = jnp.log1p(jnp.maximum(pool_rows(k), 0.0))
    part = lax.dot_general(
        rep[pl.ds(pl.multiple_of(core * groups, groups), groups), :],
        rep[queries:, :],
        (((1,), (1,)), ((), ())),
        precision=HIGHEST,
        preferred_element_type=F32,
    )
    fold = groups // 2
    part_out[...] = jnp.concatenate([part[:fold, :], part[fold:, :]], axis=1)

    @pl.loop(1, planes)
    def _(i):
        remote(part_out, part_in.at[z], one_sent, one_recv, me, ring(z + i, planes)).start()

    part_in[z] = part_out[...]
    spread_out(spot_copy, spot_twin)
    hand_on(spot_copy, spot_twin)

    @pl.when(takes_strips)
    def _():
        @pl.loop(0, chips)
        def _(chip):
            landed = strip_rows(mixed, chip)
            settle(landed, mixed_recv.at[chip])
            remote(landed, landed, mixed_twin_sent, mixed_twin_recv, twin, z).start()

    def send_hidden(j):
        for cr in range(2):
            target = 2 * ring(column - j, chips) + cr
            columns = pl.ds(pl.multiple_of(target * width, width), width)
            for source, start, count in (
                (query_hidden, 0, query_rows),
                (passage_hidden, query_rows, rows - query_rows),
            ):
                block = source.at[:, columns]
                dest = hidden.at[pl.ds(pl.multiple_of(me * rows + start, 64), count)]
                arrived = hidden_recv.at[column]

                @pl.when(target != me)
                def _():
                    remote(block, dest, hidden_sent, arrived, target, z).start()

                @pl.when(target == me)
                def _():
                    pltpu.make_async_copy(block, dest, arrived).start()

    @pl.loop(0, chips // 2)
    def _(j):
        send_hidden(j)

    settle(part_in.at[pl.ds(0, planes - 1)], one_recv)
    summed = part_in[0]
    for b in range(1, planes):
        summed = summed + part_in[b]
    part_sum[core] = summed
    swap = remote(part_sum.at[core], part_sum.at[core], two_sent, two_recv, twin, z)
    swap.start()
    swap.wait_recv()

    factor = scale[0] / (vocab_local * planes)
    sums = jnp.concatenate(
        [part_sum[k][:, h * queries : (h + 1) * queries] for k in range(2) for h in range(2)],
        axis=0,
    )
    scores = sums * factor
    weights = jnp.exp(scores - jnp.max(scores, axis=1, keepdims=True))
    soft = weights / jnp.sum(weights, axis=1, keepdims=True)
    row = lax.broadcasted_iota(jnp.int32, scores.shape, 0)
    lane = lax.broadcasted_iota(jnp.int32, scores.shape, 1)

    def natural(index):
        return jnp.where(index < groups, 2 * index, 2 * (index - groups) + 1)

    wanted = jnp.sum(
        jnp.where(
            lane == natural(row),
            jnp.broadcast_to(positive[...].astype(F32), scores.shape),
            0.0,
        ),
        axis=1,
        keepdims=True,
    )
    excess = soft - jnp.where(natural(lane).astype(F32) == wanted, 1.0, 0.0)
    nothing = jnp.zeros_like(excess)
    corner = jnp.concatenate(
        [
            jnp.concatenate([nothing, excess], axis=1),
            jnp.concatenate([nothing, nothing], axis=1),
        ],
        axis=0,
    )
    full_row = lax.broadcasted_iota(jnp.int32, corner.shape, 0)
    full_lane = lax.broadcasted_iota(jnp.int32, corner.shape, 1)
    query_part = jnp.logical_and(full_row < queries, full_lane < queries)
    passage_part = jnp.logical_and(full_row >= queries, full_lane >= queries)
    means = jnp.where(
        query_part,
        2.0 * QUERY_WEIGHT / queries / queries,
        jnp.where(passage_part, 2.0 * PASSAGE_WEIGHT / queries / queries, 0.0),
    )
    mixing = LOSS_SCALE * (factor * (corner + corner.T) + means)
    gradient = jnp.dot(mixing, rep[...], precision=HIGHEST, preferred_element_type=F32)
    for k in range(4):
        pool = pool_rows(k)
        slope = jnp.where(pool > 0.0, 1.0 / (1.0 + jnp.maximum(pool, 0.0)), 0.0)
        pushed = gradient[k * groups : (k + 1) * groups, :] * slope
        push[k * groups : (k + 1) * groups, :] = pushed.astype(BF16).astype(F32)

    settle(spots.at[pl.ds(0, chips)], spot_twin_recv)

    @pl.when(jnp.logical_not(takes_strips))
    def _():
        settle(mixed, mixed_twin_recv)

    def build(group):
        start = 0
        for k in range(4):
            length = query_length if k < 2 else passage_length
            push_row = push[pl.ds(k * groups + group, 1), :]
            spot_row = jnp.concatenate(
                [spots[group, k : k + 1, :], spots[group, 4 + k : 5 + k, :]], axis=1
            )
            positions = lax.broadcasted_iota(jnp.int32, (length, vocab_local), 0).astype(F32)
            tables[pl.ds(pl.multiple_of(group * rows + start, 32), length), :] = jnp.where(
                positions == spot_row, push_row, 0.0
            ).astype(BF16)
            start += length

    def sum_unit(u):
        @pl.loop(u * (chips // UNITS), (u + 1) * (chips // UNITS))
        def _(j):
            group = 2 * j + core
            build(group)
            partial[:, pl.ds(pl.multiple_of(j * rows, rows), rows)] = lax.dot_general(
                mixed[...],
                tables[pl.ds(pl.multiple_of(group * rows, rows), rows), :],
                (((1,), (1,)), ((), ())),
                preferred_element_type=F32,
            )

    def own_part(plane, u):
        return partial[
            pl.ds(pl.multiple_of(plane * strip, strip), strip), u * span : (u + 1) * span
        ]

    def place(way, step, u):
        return (way * half + step) * UNITS + u

    def ring_copy(way, step, u):
        index = place(way, step, u)
        neighbour = ring(z + 1 - 2 * way, planes)
        return remote(
            stage.at[index], inbox.at[index], ring_sent, ring_recv.at[index], me, neighbour
        )

    def owner_of(way, step):
        return ring(z + (1 - 2 * way) * (half - step), planes)

    def ring_step(step, way, u, follows):
        value = own_part(owner_of(way, step), u)
        if follows:
            ring_copy(way, step - 1, u).wait_recv()
            value = value + inbox[place(way, step - 1, u)].astype(F32)
        stage[place(way, step, u)] = value.astype(BF16)
        ring_copy(way, step, u).start()

    def add_weight(m):
        chip = ring(column + m, chips)
        build(2 * chip + 1 - core)
        first = pl.multiple_of(chip * 2 * rows, 64)
        settle(hidden.at[pl.ds(first, 2 * rows)], hidden_recv.at[chip])
        total[...] += lax.dot_general(
            hidden[pl.ds(first, 2 * rows), :],
            tables[pl.ds(first, 2 * rows), :],
            (((0,), (0,)), ((), ())),
            preferred_element_type=F32,
        )

    for u in range(UNITS):
        way = 0 if u < UNITS // 2 else 1
        sum_unit(u)
        ring_step(0, way, u, False)
        ring_step(1, 1 - way, u, False)
    for u in range(UNITS):
        ring_step(1, 0 if u < UNITS // 2 else 1, u, True)

    @pl.loop(chips // 2, chips)
    def _(j):
        send_hidden(j)

    total[...] = jnp.zeros_like(total)

    @pl.loop(2, half)
    def _(step):
        for u in range(UNITS):
            for way in range(2):
                ring_step(step, way, u, True)

        @pl.when(step >= 3)
        def _():
            for i in range(2):
                add_weight(2 * (step - 3) + i)

    for u in range(UNITS):
        value = own_part(z, u)
        for way in range(2):
            ring_copy(way, half - 1, u).wait_recv()
            value = value + inbox[place(way, half - 1, u)].astype(F32)
        last[:, u * span : (u + 1) * span] = value.astype(BF16)

        @pl.loop(u * (chips // UNITS), (u + 1) * (chips // UNITS))
        def _(j):
            block = last.at[:, pl.ds(pl.multiple_of(j * rows, rows), rows)]
            dest = strip_rows(final, column)

            @pl.when(j != column)
            def _():
                remote(block, dest, last_sent, last_recv, 2 * j + core, z).start()

            @pl.when(j == column)
            def _():
                pltpu.make_async_copy(block, dest, last_recv).start()

    @pl.loop(max(0, 2 * (half - 3)), chips)
    def _(m):
        add_weight(m)

    grad_weight[...] = total[...].T

    settle(final, last_recv)
    whole = final[...].astype(F32).T.astype(BF16)
    grad_query[...] = whole[:query_rows, :]
    grad_passage[...] = whole[query_rows:, :]

    settle(pools.at[pl.ds(0, chips - 1)], pool_sent)
    settle(pools.at[pl.ds(0, chips)], twin_sent)
    settle(spots.at[pl.ds(0, chips - 1)], spot_sent)
    settle(spots.at[pl.ds(0, chips)], spot_twin_sent)
    settle(part_in.at[pl.ds(0, planes - 1)], one_sent)
    swap.wait_send()

    @pl.when(takes_strips)
    def _():
        settle(mixed.at[pl.ds(0, (half - 1) * strip)], mixed_sent)
        settle(mixed, mixed_twin_sent)

    @pl.when(jnp.logical_not(takes_strips))
    def _():
        settle(mixed.at[pl.ds(0, half * strip)], mixed_sent)

    settle(hidden.at[pl.ds(0, (groups - 1) * rows)], hidden_sent)
    settle(stage.at[pl.ds(0, (2 * half - 1) * UNITS)], ring_sent)
    settle(last.at[:, pl.ds(0, (chips - 1) * rows)], last_sent)


def hand_over(*refs):
    count = (len(refs) - 1) // 2
    copies = [
        pltpu.make_async_copy(refs[n], refs[count + n], refs[-1].at[n]) for n in range(count)
    ]
    for copy in copies:
        copy.start()
    for copy in copies:
        copy.wait()


def on_device(
    groups,
    planes,
    query_hidden,
    passage_hidden,
    query_logits,
    passage_logits,
    head_weight,
    query_mask,
    passage_mask,
    positive,
    score_scale,
):
    width = query_hidden.shape[2]
    query_rows = query_hidden.shape[0] * query_hidden.shape[1]
    passage_rows = passage_hidden.shape[0] * passage_hidden.shape[1]
    rows = query_rows + passage_rows
    vocab_local, block = head_weight.shape
    chips = groups // 2
    half = planes // 2
    strip = 2 * block // chips
    sequences = 4 * groups
    vmem = pl.BlockSpec(memory_space=pltpu.VMEM)
    main = pl.BlockSpec(memory_space=pltpu.HBM)
    units = 2 * half * UNITS
    span = rows * chips // UNITS
    dma = pltpu.SemaphoreType.DMA
    grad_query, grad_passage, grad_weight = pl.pallas_call(
        functools.partial(kernel, groups, planes),
        out_shape=(
            jax.ShapeDtypeStruct((query_rows, 2 * block), BF16),
            jax.ShapeDtypeStruct((passage_rows, 2 * block), BF16),
            jax.ShapeDtypeStruct((vocab_local, block), F32),
        ),
        in_specs=[main] * 8 + [pl.BlockSpec(memory_space=pltpu.SMEM)],
        out_specs=(vmem, vmem, vmem),
        scratch_shapes=[
            pltpu.VMEM(query_logits.shape, F32),
            pltpu.VMEM(passage_logits.shape, F32),
            pltpu.VMEM(head_weight.shape, BF16),
            pltpu.VMEM(query_mask.shape, jnp.int32),
            pltpu.VMEM(passage_mask.shape, jnp.int32),
            pltpu.VMEM((1, positive.shape[0]), jnp.int32),
            pltpu.VMEM((groups, 8, vocab_local // 2), F32),
            pltpu.VMEM((groups, 8, vocab_local // 2), F32),
            pltpu.VMEM((sequences, vocab_local), F32),
            pltpu.VMEM((sequences, vocab_local), F32),
            pltpu.VMEM((chips, sequences), F32),
            pltpu.VMEM((planes, chips, sequences), F32),
            pltpu.VMEM((2, chips, sequences), F32),
            pltpu.VMEM((block, vocab_local), BF16),
            pltpu.VMEM((2 * block, vocab_local), BF16),
            pltpu.VMEM((groups * rows, block), BF16),
            pltpu.VMEM((groups * rows, vocab_local), BF16),
            pltpu.VMEM((2 * block, chips * rows), F32),
            pltpu.VMEM((units, strip, span), BF16),
            pltpu.VMEM((units, strip, span), BF16),
            pltpu.VMEM((strip, chips * rows), BF16),
            pltpu.VMEM((2 * block, rows), BF16),
            pltpu.VMEM((block, vocab_local), F32),
            dma((6,)),
            dma((11,)),
            dma((chips,)),
            dma,
            dma((chips,)),
            dma,
            dma,
            dma,
            dma((chips,)),
            dma,
            dma((chips,)),
            dma((units,)),
            dma,
        ],
        compiler_params=pltpu.CompilerParams(
            collective_id=0, has_side_effects=True, vmem_limit_bytes=60 * 1024 * 1024
        ),
    )(
        query_hidden.reshape(query_rows, width),
        passage_hidden.reshape(passage_rows, width),
        query_logits,
        passage_logits,
        head_weight,
        query_mask,
        passage_mask,
        positive.reshape(1, -1),
        score_scale,
    )
    results = (grad_query, grad_passage, grad_weight)
    grad_query, grad_passage, grad_weight = pl.pallas_call(
        hand_over,
        out_shape=tuple(jax.ShapeDtypeStruct(r.shape, r.dtype) for r in results),
        in_specs=[main] * 3,
        out_specs=(main,) * 3,
        scratch_shapes=[dma((3,))],
        compiler_params=pltpu.CompilerParams(vmem_limit_bytes=60 * 1024 * 1024),
    )(*results)
    return (
        grad_query.reshape(query_hidden.shape[:2] + (2 * block,)),
        grad_passage.reshape(passage_hidden.shape[:2] + (2 * block,)),
        grad_weight,
    )


def solution(mesh):
    in_specs = (
        P("dp", None, None),
        P("dp", None, None),
        P("dp", None, "vocab"),
        P("dp", None, "vocab"),
        P("vocab", "dp"),
        P("dp", None),
        P("dp", None),
        P(),
        P(),
    )
    out_specs = (P("dp", None, "vocab"), P("dp", None, "vocab"), P("vocab", "dp"))
    return jax.shard_map(
        functools.partial(on_device, mesh.shape["dp"], mesh.shape["vocab"]),
        mesh=mesh,
        in_specs=in_specs,
        out_specs=out_specs,
        check_vma=False,
    )
```

```python
import functools

import jax
import jax.numpy as jnp
from jax import lax
from jax.experimental import pallas as pl
from jax.experimental.pallas import tpu as pltpu
from jax.sharding import PartitionSpec as P

MESH = pl.DeviceIdType.MESH
HIGHEST = lax.Precision.HIGHEST
LOSS_SCALE = 256.0
QUERY_WEIGHT = 3.0
PASSAGE_WEIGHT = 1.0
F32 = jnp.float32
BF16 = jnp.bfloat16
UNITS = 4


def pooled(logits, length):
    spots = lax.broadcasted_iota(jnp.int32, logits.shape, 0).astype(F32)
    masked = jnp.where(spots < length, logits, -jnp.inf)
    largest = jnp.max(masked, axis=0, keepdims=True)
    where = jnp.min(jnp.where(masked == largest, spots, 1e9), axis=0, keepdims=True)
    return largest, where


def kernel(
    groups,
    planes,
    query_hidden,
    passage_hidden,
    query_logits_in,
    passage_logits_in,
    weight_in,
    query_mask_in,
    passage_mask_in,
    positive_in,
    scale,
    grad_query,
    grad_passage,
    grad_weight,
    query_logits,
    passage_logits,
    weight,
    query_mask,
    passage_mask,
    positive,
    pools,
    spots,
    rep,
    push,
    part_out,
    part_in,
    part_sum,
    turned,
    mixed,
    hidden,
    tables,
    partial,
    stage,
    inbox,
    last,
    final,
    total,
    load,
    sent,
    pool_recv,
    twin_recv,
    spot_recv,
    spot_twin_recv,
    one_recv,
    two_recv,
    mixed_recv,
    mixed_twin_recv,
    hidden_recv,
    ring_recv,
    last_recv,
):
    chips = groups // 2
    half = planes // 2
    query_length = query_logits.shape[1]
    passage_length = passage_logits.shape[1]
    vocab_local = query_logits.shape[2]
    query_rows = 2 * query_length
    rows = query_rows + 2 * passage_length
    width = weight.shape[1]
    queries = 2 * groups
    strip = 2 * width // chips
    span = rows * chips // UNITS
    me = lax.axis_index("dp")
    z = lax.axis_index("vocab")
    column = lax.div(me, 2)
    core = lax.rem(me, 2)
    twin = 2 * column + 1 - core
    pool_sent, twin_sent, spot_sent, spot_twin_sent, one_sent = (sent.at[i] for i in range(5))
    two_sent, mixed_sent, mixed_twin_sent, hidden_sent = (sent.at[i] for i in range(5, 9))
    ring_sent, last_sent = sent.at[9], sent.at[10]

    def ring(value, size):
        return lax.rem(value + 2 * size, size)

    def remote(source, dest, send, recv, target, plane):
        return pltpu.make_async_remote_copy(
            src_ref=source,
            dst_ref=dest,
            send_sem=send,
            recv_sem=recv,
            device_id=(target, plane),
            device_id_type=MESH,
        )

    def settle(ref, sem):
        pltpu.make_async_copy(ref, ref, sem).wait()

    loads = [
        pltpu.make_async_copy(source, dest, load.at[n])
        for n, (source, dest) in enumerate(
            (
                (query_mask_in, query_mask),
                (passage_mask_in, passage_mask),
                (query_logits_in, query_logits),
                (passage_logits_in, passage_logits),
                (weight_in, weight),
                (positive_in, positive),
            )
        )
    ]
    for copy in loads:
        copy.start()

    barrier = pltpu.get_barrier_semaphore()

    def greet(dp_index, plane):
        pl.semaphore_signal(barrier, inc=1, device_id=(dp_index, plane), device_id_type=MESH)

    @pl.loop(1, planes)
    def _(i):
        greet(me, ring(z + i, planes))

    @pl.loop(1, groups)
    def _(i):
        greet(ring(me + i, groups), z)

    def lengths(mask):
        return jnp.sum(mask[...].astype(F32), axis=1, keepdims=True)

    for copy in loads[:4]:
        copy.wait()
    query_lengths = lengths(query_mask)
    passage_lengths = lengths(passage_mask)
    found = [pooled(query_logits[s], query_lengths[s : s + 1, :]) for s in range(2)]
    found += [pooled(passage_logits[s], passage_lengths[s : s + 1, :]) for s in range(2)]
    middle = vocab_local // 2

    def folded(lines):
        return jnp.concatenate(
            [line[:, :middle] for line in lines] + [line[:, middle:] for line in lines], axis=0
        )

    pools[me] = folded([f[0] for f in found])
    spots[me] = folded([f[1] for f in found])
    for copy in loads[4:]:
        copy.wait()
    turned[...] = weight[...].astype(F32).T.astype(BF16)

    pl.semaphore_wait(barrier, groups + planes - 2)

    def pool_copy(group, target, m):
        return remote(pools.at[group], pools.at[group], pool_sent, pool_recv.at[m], target, z)

    def pool_twin(group):
        return remote(pools.at[group], pools.at[group], twin_sent, twin_recv, twin, z)

    def spot_copy(group, target, m):
        return remote(spots.at[group], spots.at[group], spot_sent, spot_recv.at[m], target, z)

    def spot_twin(group):
        return remote(spots.at[group], spots.at[group], spot_twin_sent, spot_twin_recv, twin, z)

    def spread_out(copy, twin_copy):
        @pl.loop(1, chips)
        def _(m):
            copy(me, 2 * ring(column + m, chips) + core, m).start()

        twin_copy(me).start()

    def hand_on(copy, twin_copy):
        @pl.loop(1, chips)
        def _(m):
            group = 2 * ring(column - m, chips) + core
            copy(group, me, m).wait_recv()
            twin_copy(group).start()

    spread_out(pool_copy, pool_twin)
    hand_on(pool_copy, pool_twin)

    def strip_rows(ref, index):
        return ref.at[pl.ds(pl.multiple_of(index * strip, strip), strip)]

    @pl.loop(0, half)
    def _(i):
        chip = core * half + ring(i + column, half)

        @pl.when(chip != column)
        def _():
            remote(
                strip_rows(turned, chip - core * half),
                strip_rows(mixed, column),
                mixed_sent,
                mixed_recv.at[column],
                2 * chip + core,
                z,
            ).start()

        @pl.when(chip == column)
        def _():
            pltpu.make_async_copy(
                strip_rows(turned, chip - core * half),
                strip_rows(mixed, column),
                mixed_recv.at[column],
            ).start()

    takes_strips = core == lax.div(column, half)

    def pool_rows(k):
        return jnp.concatenate([pools[:, k, :], pools[:, 4 + k, :]], axis=1)

    settle(pools.at[pl.ds(0, chips)], twin_recv)
    for k in range(4):
        rep[k * groups : (k + 1) * groups, :] = jnp.log1p(jnp.maximum(pool_rows(k), 0.0))
    part = lax.dot_general(
        rep[pl.ds(pl.multiple_of(core * groups, groups), groups), :],
        rep[queries:, :],
        (((1,), (1,)), ((), ())),
        precision=HIGHEST,
        preferred_element_type=F32,
    )
    fold = groups // 2
    part_out[...] = jnp.concatenate([part[:fold, :], part[fold:, :]], axis=1)

    @pl.loop(1, planes)
    def _(i):
        remote(part_out, part_in.at[z], one_sent, one_recv, me, ring(z + i, planes)).start()

    part_in[z] = part_out[...]
    spread_out(spot_copy, spot_twin)
    hand_on(spot_copy, spot_twin)

    @pl.when(takes_strips)
    def _():
        @pl.loop(0, chips)
        def _(chip):
            landed = strip_rows(mixed, chip)
            settle(landed, mixed_recv.at[chip])
            remote(landed, landed, mixed_twin_sent, mixed_twin_recv, twin, z).start()

    def send_hidden(j):
        for cr in range(2):
            target = 2 * ring(column - j, chips) + cr
            columns = pl.ds(pl.multiple_of(target * width, width), width)
            for source, start, count in (
                (query_hidden, 0, query_rows),
                (passage_hidden, query_rows, rows - query_rows),
            ):
                block = source.at[:, columns]
                dest = hidden.at[pl.ds(pl.multiple_of(me * rows + start, 64), count)]
                arrived = hidden_recv.at[column]

                @pl.when(target != me)
                def _():
                    remote(block, dest, hidden_sent, arrived, target, z).start()

                @pl.when(target == me)
                def _():
                    pltpu.make_async_copy(block, dest, arrived).start()

    @pl.loop(0, chips // 2)
    def _(j):
        send_hidden(j)

    settle(part_in.at[pl.ds(0, planes - 1)], one_recv)
    summed = part_in[0]
    for b in range(1, planes):
        summed = summed + part_in[b]
    part_sum[core] = summed
    swap = remote(part_sum.at[core], part_sum.at[core], two_sent, two_recv, twin, z)
    swap.start()
    swap.wait_recv()

    factor = scale[0] / (vocab_local * planes)
    sums = jnp.concatenate(
        [part_sum[k][:, h * queries : (h + 1) * queries] for k in range(2) for h in range(2)],
        axis=0,
    )
    scores = sums * factor
    weights = jnp.exp(scores - jnp.max(scores, axis=1, keepdims=True))
    soft = weights / jnp.sum(weights, axis=1, keepdims=True)
    row = lax.broadcasted_iota(jnp.int32, scores.shape, 0)
    lane = lax.broadcasted_iota(jnp.int32, scores.shape, 1)

    def natural(index):
        return jnp.where(index < groups, 2 * index, 2 * (index - groups) + 1)

    wanted = jnp.sum(
        jnp.where(
            lane == natural(row),
            jnp.broadcast_to(positive[...].astype(F32), scores.shape),
            0.0,
        ),
        axis=1,
        keepdims=True,
    )
    excess = soft - jnp.where(natural(lane).astype(F32) == wanted, 1.0, 0.0)
    nothing = jnp.zeros_like(excess)
    corner = jnp.concatenate(
        [
            jnp.concatenate([nothing, excess], axis=1),
            jnp.concatenate([nothing, nothing], axis=1),
        ],
        axis=0,
    )
    full_row = lax.broadcasted_iota(jnp.int32, corner.shape, 0)
    full_lane = lax.broadcasted_iota(jnp.int32, corner.shape, 1)
    query_part = jnp.logical_and(full_row < queries, full_lane < queries)
    passage_part = jnp.logical_and(full_row >= queries, full_lane >= queries)
    means = jnp.where(
        query_part,
        2.0 * QUERY_WEIGHT / queries / queries,
        jnp.where(passage_part, 2.0 * PASSAGE_WEIGHT / queries / queries, 0.0),
    )
    mixing = LOSS_SCALE * (factor * (corner + corner.T) + means)
    gradient = jnp.dot(mixing, rep[...], precision=HIGHEST, preferred_element_type=F32)
    for k in range(4):
        pool = pool_rows(k)
        slope = jnp.where(pool > 0.0, 1.0 / (1.0 + jnp.maximum(pool, 0.0)), 0.0)
        pushed = gradient[k * groups : (k + 1) * groups, :] * slope
        push[k * groups : (k + 1) * groups, :] = pushed.astype(BF16).astype(F32)

    settle(spots.at[pl.ds(0, chips)], spot_twin_recv)

    @pl.when(jnp.logical_not(takes_strips))
    def _():
        settle(mixed, mixed_twin_recv)

    def build(group):
        start = 0
        for k in range(4):
            length = query_length if k < 2 else passage_length
            push_row = push[pl.ds(k * groups + group, 1), :]
            spot_row = jnp.concatenate(
                [spots[group, k : k + 1, :], spots[group, 4 + k : 5 + k, :]], axis=1
            )
            positions = lax.broadcasted_iota(jnp.int32, (length, vocab_local), 0).astype(F32)
            tables[pl.ds(pl.multiple_of(group * rows + start, 32), length), :] = jnp.where(
                positions == spot_row, push_row, 0.0
            ).astype(BF16)
            start += length

    def sum_unit(u):
        @pl.loop(u * (chips // UNITS), (u + 1) * (chips // UNITS))
        def _(j):
            group = 2 * j + core
            build(group)
            partial[:, pl.ds(pl.multiple_of(j * rows, rows), rows)] = lax.dot_general(
                mixed[...],
                tables[pl.ds(pl.multiple_of(group * rows, rows), rows), :],
                (((1,), (1,)), ((), ())),
                preferred_element_type=F32,
            )

    def own_part(plane, u):
        return partial[
            pl.ds(pl.multiple_of(plane * strip, strip), strip), u * span : (u + 1) * span
        ]

    def place(way, step, u):
        return (way * half + step) * UNITS + u

    def ring_copy(way, step, u):
        index = place(way, step, u)
        neighbour = ring(z + 1 - 2 * way, planes)
        return remote(
            stage.at[index], inbox.at[index], ring_sent, ring_recv.at[index], me, neighbour
        )

    def owner_of(way, step):
        return ring(z + (1 - 2 * way) * (half - step), planes)

    def ring_step(step, way, u, follows):
        value = own_part(owner_of(way, step), u)
        if follows:
            ring_copy(way, step - 1, u).wait_recv()
            value = value + inbox[place(way, step - 1, u)].astype(F32)
        stage[place(way, step, u)] = value.astype(BF16)
        ring_copy(way, step, u).start()

    def add_weight(m):
        chip = ring(column + m, chips)
        build(2 * chip + 1 - core)
        first = pl.multiple_of(chip * 2 * rows, 64)
        settle(hidden.at[pl.ds(first, 2 * rows)], hidden_recv.at[chip])
        total[...] += lax.dot_general(
            hidden[pl.ds(first, 2 * rows), :],
            tables[pl.ds(first, 2 * rows), :],
            (((0,), (0,)), ((), ())),
            preferred_element_type=F32,
        )

    for u in range(UNITS):
        way = 0 if u < UNITS // 2 else 1
        sum_unit(u)
        ring_step(0, way, u, False)
        ring_step(1, 1 - way, u, False)
    for u in range(UNITS):
        ring_step(1, 0 if u < UNITS // 2 else 1, u, True)

    @pl.loop(chips // 2, chips)
    def _(j):
        send_hidden(j)

    total[...] = jnp.zeros_like(total)

    @pl.loop(2, half)
    def _(step):
        for u in range(UNITS):
            for way in range(2):
                ring_step(step, way, u, True)

        @pl.when(step >= 3)
        def _():
            for i in range(2):
                add_weight(2 * (step - 3) + i)

    for u in range(UNITS):
        value = own_part(z, u)
        for way in range(2):
            ring_copy(way, half - 1, u).wait_recv()
            value = value + inbox[place(way, half - 1, u)].astype(F32)
        last[:, u * span : (u + 1) * span] = value.astype(BF16)

        @pl.loop(u * (chips // UNITS), (u + 1) * (chips // UNITS))
        def _(j):
            block = last.at[:, pl.ds(pl.multiple_of(j * rows, rows), rows)]
            dest = strip_rows(final, column)

            @pl.when(j != column)
            def _():
                remote(block, dest, last_sent, last_recv, 2 * j + core, z).start()

            @pl.when(j == column)
            def _():
                pltpu.make_async_copy(block, dest, last_recv).start()

    @pl.loop(max(0, 2 * (half - 3)), chips)
    def _(m):
        add_weight(m)

    grad_weight[...] = total[...].T

    settle(final, last_recv)
    whole = final[...].astype(F32).T.astype(BF16)
    grad_query[...] = whole[:query_rows, :]
    grad_passage[...] = whole[query_rows:, :]

    settle(pools.at[pl.ds(0, chips - 1)], pool_sent)
    settle(pools.at[pl.ds(0, chips)], twin_sent)
    settle(spots.at[pl.ds(0, chips - 1)], spot_sent)
    settle(spots.at[pl.ds(0, chips)], spot_twin_sent)
    settle(part_in.at[pl.ds(0, planes - 1)], one_sent)
    swap.wait_send()

    @pl.when(takes_strips)
    def _():
        settle(mixed.at[pl.ds(0, (half - 1) * strip)], mixed_sent)
        settle(mixed, mixed_twin_sent)

    @pl.when(jnp.logical_not(takes_strips))
    def _():
        settle(mixed.at[pl.ds(0, half * strip)], mixed_sent)

    settle(hidden.at[pl.ds(0, (groups - 1) * rows)], hidden_sent)
    settle(stage.at[pl.ds(0, (2 * half - 1) * UNITS)], ring_sent)
    settle(last.at[:, pl.ds(0, (chips - 1) * rows)], last_sent)


def hand_over(*refs):
    count = (len(refs) - 1) // 3
    sources, dests, holds = refs[:count], refs[count : 2 * count], refs[2 * count : -1]
    arrive = [pltpu.make_async_copy(sources[n], holds[n], refs[-1].at[n]) for n in range(count)]
    leave = [pltpu.make_async_copy(holds[n], dests[n], refs[-1].at[n]) for n in range(count)]
    for copy in arrive:
        copy.start()
    for n in range(count):
        arrive[n].wait()
        leave[n].start()
    for copy in leave:
        copy.wait()


def on_device(
    groups,
    planes,
    query_hidden,
    passage_hidden,
    query_logits,
    passage_logits,
    head_weight,
    query_mask,
    passage_mask,
    positive,
    score_scale,
):
    width = query_hidden.shape[2]
    query_rows = query_hidden.shape[0] * query_hidden.shape[1]
    passage_rows = passage_hidden.shape[0] * passage_hidden.shape[1]
    rows = query_rows + passage_rows
    vocab_local, block = head_weight.shape
    chips = groups // 2
    half = planes // 2
    strip = 2 * block // chips
    sequences = 4 * groups
    vmem = pl.BlockSpec(memory_space=pltpu.VMEM)
    main = pl.BlockSpec(memory_space=pltpu.HBM)
    units = 2 * half * UNITS
    span = rows * chips // UNITS
    dma = pltpu.SemaphoreType.DMA
    grad_query, grad_passage, grad_weight = pl.pallas_call(
        functools.partial(kernel, groups, planes),
        out_shape=(
            jax.ShapeDtypeStruct((query_rows, 2 * block), BF16),
            jax.ShapeDtypeStruct((passage_rows, 2 * block), BF16),
            jax.ShapeDtypeStruct((vocab_local, block), F32),
        ),
        in_specs=[main] * 8 + [pl.BlockSpec(memory_space=pltpu.SMEM)],
        out_specs=(vmem, vmem, vmem),
        scratch_shapes=[
            pltpu.VMEM(query_logits.shape, F32),
            pltpu.VMEM(passage_logits.shape, F32),
            pltpu.VMEM(head_weight.shape, BF16),
            pltpu.VMEM(query_mask.shape, jnp.int32),
            pltpu.VMEM(passage_mask.shape, jnp.int32),
            pltpu.VMEM((1, positive.shape[0]), jnp.int32),
            pltpu.VMEM((groups, 8, vocab_local // 2), F32),
            pltpu.VMEM((groups, 8, vocab_local // 2), F32),
            pltpu.VMEM((sequences, vocab_local), F32),
            pltpu.VMEM((sequences, vocab_local), F32),
            pltpu.VMEM((chips, sequences), F32),
            pltpu.VMEM((planes, chips, sequences), F32),
            pltpu.VMEM((2, chips, sequences), F32),
            pltpu.VMEM((block, vocab_local), BF16),
            pltpu.VMEM((2 * block, vocab_local), BF16),
            pltpu.VMEM((groups * rows, block), BF16),
            pltpu.VMEM((groups * rows, vocab_local), BF16),
            pltpu.VMEM((2 * block, chips * rows), F32),
            pltpu.VMEM((units, strip, span), BF16),
            pltpu.VMEM((units, strip, span), BF16),
            pltpu.VMEM((strip, chips * rows), BF16),
            pltpu.VMEM((2 * block, rows), BF16),
            pltpu.VMEM((block, vocab_local), F32),
            dma((6,)),
            dma((11,)),
            dma((chips,)),
            dma,
            dma((chips,)),
            dma,
            dma,
            dma,
            dma((chips,)),
            dma,
            dma((chips,)),
            dma((units,)),
            dma,
        ],
        compiler_params=pltpu.CompilerParams(
            collective_id=0, has_side_effects=True, vmem_limit_bytes=60 * 1024 * 1024
        ),
    )(
        query_hidden.reshape(query_rows, width),
        passage_hidden.reshape(passage_rows, width),
        query_logits,
        passage_logits,
        head_weight,
        query_mask,
        passage_mask,
        positive.reshape(1, -1),
        score_scale,
    )
    results = (grad_query, grad_passage, grad_weight)
    grad_query, grad_passage, grad_weight = pl.pallas_call(
        hand_over,
        out_shape=tuple(jax.ShapeDtypeStruct(r.shape, r.dtype) for r in results),
        in_specs=[main] * 3,
        out_specs=(main,) * 3,
        scratch_shapes=[pltpu.VMEM(r.shape, r.dtype) for r in results] + [dma((3,))],
        compiler_params=pltpu.CompilerParams(vmem_limit_bytes=60 * 1024 * 1024),
    )(*results)
    return (
        grad_query.reshape(query_hidden.shape[:2] + (2 * block,)),
        grad_passage.reshape(passage_hidden.shape[:2] + (2 * block,)),
        grad_weight,
    )


def solution(mesh):
    in_specs = (
        P("dp", None, None),
        P("dp", None, None),
        P("dp", None, "vocab"),
        P("dp", None, "vocab"),
        P("vocab", "dp"),
        P("dp", None),
        P("dp", None),
        P(),
        P(),
    )
    out_specs = (P("dp", None, "vocab"), P("dp", None, "vocab"), P("vocab", "dp"))
    return jax.shard_map(
        functools.partial(on_device, mesh.shape["dp"], mesh.shape["vocab"]),
        mesh=mesh,
        in_specs=in_specs,
        out_specs=out_specs,
        check_vma=False,
    )
```

```python
import functools

import jax
import jax.numpy as jnp
from jax import lax
from jax.experimental import pallas as pl
from jax.experimental.pallas import tpu as pltpu
from jax.sharding import PartitionSpec as P

MESH = pl.DeviceIdType.MESH
HIGHEST = lax.Precision.HIGHEST
LOSS_SCALE = 256.0
QUERY_WEIGHT = 3.0
PASSAGE_WEIGHT = 1.0
F32 = jnp.float32
BF16 = jnp.bfloat16
UNITS = 4
SLOTS = 8


def pooled(logits, length):
    spots = lax.broadcasted_iota(jnp.int32, logits.shape, 0).astype(F32)
    masked = jnp.where(spots < length, logits, -jnp.inf)
    largest = jnp.max(masked, axis=0, keepdims=True)
    where = jnp.min(jnp.where(masked == largest, spots, 1e9), axis=0, keepdims=True)
    return largest, where


def kernel(
    groups,
    planes,
    query_hidden,
    passage_hidden,
    query_logits_in,
    passage_logits_in,
    weight_in,
    query_mask_in,
    passage_mask_in,
    positive_in,
    scale,
    grad_query,
    grad_passage,
    grad_weight,
    query_logits,
    passage_logits,
    weight,
    query_mask,
    passage_mask,
    positive,
    pools,
    spots,
    rep,
    push,
    part_out,
    part_in,
    part_sum,
    turned,
    mixed,
    hidden,
    tables,
    partial,
    stage,
    inbox,
    last,
    final,
    total,
    load,
    sent,
    pool_recv,
    twin_recv,
    spot_recv,
    spot_twin_recv,
    one_recv,
    two_recv,
    mixed_recv,
    mixed_twin_recv,
    hidden_recv,
    ring_recv,
    last_recv,
):
    chips = groups // 2
    half = planes // 2
    query_length = query_logits.shape[1]
    passage_length = passage_logits.shape[1]
    vocab_local = query_logits.shape[2]
    query_rows = 2 * query_length
    rows = query_rows + 2 * passage_length
    width = weight.shape[1]
    queries = 2 * groups
    strip = 2 * width // chips
    span = rows * chips // UNITS
    me = lax.axis_index("dp")
    z = lax.axis_index("vocab")
    column = lax.div(me, 2)
    core = lax.rem(me, 2)
    twin = 2 * column + 1 - core
    pool_sent, twin_sent, spot_sent, spot_twin_sent, one_sent = (sent.at[i] for i in range(5))
    two_sent, mixed_sent, mixed_twin_sent, hidden_sent = (sent.at[i] for i in range(5, 9))
    ring_sent, last_sent = sent.at[9], sent.at[10]

    def ring(value, size):
        return lax.rem(value + 2 * size, size)

    def remote(source, dest, send, recv, target, plane):
        return pltpu.make_async_remote_copy(
            src_ref=source,
            dst_ref=dest,
            send_sem=send,
            recv_sem=recv,
            device_id=(target, plane),
            device_id_type=MESH,
        )

    def settle(ref, sem):
        pltpu.make_async_copy(ref, ref, sem).wait()

    def far_first(n, middle):
        return middle + (1 - 2 * lax.rem(n, 2)) * lax.div(n + 1, 2)

    loads = [
        pltpu.make_async_copy(source, dest, load.at[n])
        for n, (source, dest) in enumerate(
            (
                (query_mask_in, query_mask),
                (passage_mask_in, passage_mask),
                (query_logits_in, query_logits),
                (passage_logits_in, passage_logits),
                (weight_in, weight),
                (positive_in, positive),
            )
        )
    ]
    for copy in loads:
        copy.start()

    barrier = pltpu.get_barrier_semaphore()

    def greet(dp_index, plane):
        pl.semaphore_signal(barrier, inc=1, device_id=(dp_index, plane), device_id_type=MESH)

    @pl.loop(0, planes - 1)
    def _(n):
        greet(me, ring(z + far_first(n, half), planes))

    @pl.loop(1, groups)
    def _(i):
        greet(ring(me + i, groups), z)

    def lengths(mask):
        return jnp.sum(mask[...].astype(F32), axis=1, keepdims=True)

    for copy in loads[:4]:
        copy.wait()
    query_lengths = lengths(query_mask)
    passage_lengths = lengths(passage_mask)
    found = [pooled(query_logits[s], query_lengths[s : s + 1, :]) for s in range(2)]
    found += [pooled(passage_logits[s], passage_lengths[s : s + 1, :]) for s in range(2)]
    middle = vocab_local // 2

    def folded(lines):
        return jnp.concatenate(
            [line[:, :middle] for line in lines] + [line[:, middle:] for line in lines], axis=0
        )

    pools[me] = folded([f[0] for f in found])
    spots[me] = folded([f[1] for f in found])
    for copy in loads[4:]:
        copy.wait()
    turned[...] = weight[...].astype(F32).T.astype(BF16)

    pl.semaphore_wait(barrier, groups + planes - 2)

    def pool_copy(group, target, m):
        return remote(pools.at[group], pools.at[group], pool_sent, pool_recv.at[m], target, z)

    def pool_twin(group):
        return remote(pools.at[group], pools.at[group], twin_sent, twin_recv, twin, z)

    def spot_copy(group, target, m):
        return remote(spots.at[group], spots.at[group], spot_sent, spot_recv.at[m], target, z)

    def spot_twin(group):
        return remote(spots.at[group], spots.at[group], spot_twin_sent, spot_twin_recv, twin, z)

    def spread_out(copy, twin_copy):
        @pl.loop(0, chips - 1)
        def _(n):
            m = far_first(n, chips // 2)
            copy(me, 2 * ring(column + m, chips) + core, m).start()

        twin_copy(me).start()

    def hand_on(copy, twin_copy):
        @pl.loop(1, chips)
        def _(m):
            group = 2 * ring(column - m, chips) + core
            copy(group, me, m).wait_recv()
            twin_copy(group).start()

    spread_out(pool_copy, pool_twin)
    hand_on(pool_copy, pool_twin)

    def strip_rows(ref, index):
        return ref.at[pl.ds(pl.multiple_of(index * strip, strip), strip)]

    @pl.loop(0, half)
    def _(i):
        chip = core * half + ring(i + column, half)

        @pl.when(chip != column)
        def _():
            remote(
                strip_rows(turned, chip - core * half),
                strip_rows(mixed, column),
                mixed_sent,
                mixed_recv.at[column],
                2 * chip + core,
                z,
            ).start()

        @pl.when(chip == column)
        def _():
            pltpu.make_async_copy(
                strip_rows(turned, chip - core * half),
                strip_rows(mixed, column),
                mixed_recv.at[column],
            ).start()

    takes_strips = core == lax.div(column, half)

    def pool_rows(k):
        return jnp.concatenate([pools[:, k, :], pools[:, 4 + k, :]], axis=1)

    settle(pools.at[pl.ds(0, chips)], twin_recv)
    for k in range(4):
        rep[k * groups : (k + 1) * groups, :] = jnp.log1p(jnp.maximum(pool_rows(k), 0.0))
    part = lax.dot_general(
        rep[pl.ds(pl.multiple_of(core * groups, groups), groups), :],
        rep[queries:, :],
        (((1,), (1,)), ((), ())),
        precision=HIGHEST,
        preferred_element_type=F32,
    )
    fold = groups // 2
    part_out[...] = jnp.concatenate([part[:fold, :], part[fold:, :]], axis=1)

    @pl.loop(0, planes - 1)
    def _(n):
        plane = ring(z + far_first(n, half), planes)
        remote(part_out, part_in.at[z], one_sent, one_recv, me, plane).start()

    part_in[z] = part_out[...]
    spread_out(spot_copy, spot_twin)

    def send_hidden(j):
        for cr in range(2):
            target = 2 * ring(column - j, chips) + cr
            columns = pl.ds(pl.multiple_of(target * width, width), width)
            for source, start, count in (
                (query_hidden, 0, query_rows),
                (passage_hidden, query_rows, rows - query_rows),
            ):
                block = source.at[:, columns]
                dest = hidden.at[pl.ds(pl.multiple_of(me * rows + start, 64), count)]
                arrived = hidden_recv.at[column]

                @pl.when(target != me)
                def _():
                    remote(block, dest, hidden_sent, arrived, target, z).start()

                @pl.when(target == me)
                def _():
                    pltpu.make_async_copy(block, dest, arrived).start()

    @pl.loop(0, chips // 2)
    def _(j):
        send_hidden(j)

    @pl.when(takes_strips)
    def _():
        @pl.loop(0, chips)
        def _(chip):
            landed = strip_rows(mixed, chip)
            settle(landed, mixed_recv.at[chip])
            remote(landed, landed, mixed_twin_sent, mixed_twin_recv, twin, z).start()

    settle(part_in.at[pl.ds(0, planes - 1)], one_recv)
    summed = part_in[0]
    for b in range(1, planes):
        summed = summed + part_in[b]
    part_sum[core] = summed
    swap = remote(part_sum.at[core], part_sum.at[core], two_sent, two_recv, twin, z)
    swap.start()
    hand_on(spot_copy, spot_twin)
    swap.wait_recv()

    factor = scale[0] / (vocab_local * planes)
    sums = jnp.concatenate(
        [part_sum[k][:, h * queries : (h + 1) * queries] for k in range(2) for h in range(2)],
        axis=0,
    )
    scores = sums * factor
    weights = jnp.exp(scores - jnp.max(scores, axis=1, keepdims=True))
    soft = weights / jnp.sum(weights, axis=1, keepdims=True)
    row = lax.broadcasted_iota(jnp.int32, scores.shape, 0)
    lane = lax.broadcasted_iota(jnp.int32, scores.shape, 1)

    def natural(index):
        return jnp.where(index < groups, 2 * index, 2 * (index - groups) + 1)

    wanted = jnp.sum(
        jnp.where(
            lane == natural(row),
            jnp.broadcast_to(positive[...].astype(F32), scores.shape),
            0.0,
        ),
        axis=1,
        keepdims=True,
    )
    excess = soft - jnp.where(natural(lane).astype(F32) == wanted, 1.0, 0.0)
    nothing = jnp.zeros_like(excess)
    corner = jnp.concatenate(
        [
            jnp.concatenate([nothing, excess], axis=1),
            jnp.concatenate([nothing, nothing], axis=1),
        ],
        axis=0,
    )
    full_row = lax.broadcasted_iota(jnp.int32, corner.shape, 0)
    full_lane = lax.broadcasted_iota(jnp.int32, corner.shape, 1)
    query_part = jnp.logical_and(full_row < queries, full_lane < queries)
    passage_part = jnp.logical_and(full_row >= queries, full_lane >= queries)
    means = jnp.where(
        query_part,
        2.0 * QUERY_WEIGHT / queries / queries,
        jnp.where(passage_part, 2.0 * PASSAGE_WEIGHT / queries / queries, 0.0),
    )
    mixing = LOSS_SCALE * (factor * (corner + corner.T) + means)
    gradient = jnp.dot(mixing, rep[...], precision=HIGHEST, preferred_element_type=F32)
    for k in range(4):
        pool = pool_rows(k)
        slope = jnp.where(pool > 0.0, 1.0 / (1.0 + jnp.maximum(pool, 0.0)), 0.0)
        pushed = gradient[k * groups : (k + 1) * groups, :] * slope
        push[k * groups : (k + 1) * groups, :] = pushed.astype(BF16).astype(F32)

    settle(spots.at[pl.ds(0, chips)], spot_twin_recv)

    @pl.when(jnp.logical_not(takes_strips))
    def _():
        settle(mixed, mixed_twin_recv)

    def build(group):
        start = 0
        for k in range(4):
            length = query_length if k < 2 else passage_length
            push_row = push[pl.ds(k * groups + group, 1), :]
            spot_row = jnp.concatenate(
                [spots[group, k : k + 1, :], spots[group, 4 + k : 5 + k, :]], axis=1
            )
            positions = lax.broadcasted_iota(jnp.int32, (length, vocab_local), 0).astype(F32)
            tables[pl.ds(pl.multiple_of(group * rows + start, 32), length), :] = jnp.where(
                positions == spot_row, push_row, 0.0
            ).astype(BF16)
            start += length

    def sum_unit(u):
        @pl.loop(u * (chips // UNITS), (u + 1) * (chips // UNITS))
        def _(j):
            group = 2 * j + core
            build(group)
            partial[:, pl.ds(pl.multiple_of(j * rows, rows), rows)] = lax.dot_general(
                mixed[...],
                tables[pl.ds(pl.multiple_of(group * rows, rows), rows), :],
                (((1,), (1,)), ((), ())),
                preferred_element_type=F32,
            )

    def own_part(plane, u):
        return partial[
            pl.ds(pl.multiple_of(plane * strip, strip), strip), u * span : (u + 1) * span
        ]

    def place(way, u, slot):
        return (way * UNITS + u) * SLOTS + slot

    def own(way, distance, u):
        return own_part(ring(z + (1 - 2 * way) * distance, planes), u)

    def send(way, u, slot, hops, value):
        index = place(way, u, slot)
        stage[index] = value.astype(BF16)
        target = ring(z + (1 - 2 * way) * hops, planes)
        remote(
            stage.at[index], inbox.at[index], ring_sent, ring_recv.at[index], me, target
        ).start()

    def take(way, u, slot):
        index = place(way, u, slot)
        settle(inbox.at[index], ring_recv.at[index])
        return inbox[index].astype(F32)

    def add_weight(m):
        chip = ring(column + m, chips)
        build(2 * chip + 1 - core)
        first = pl.multiple_of(chip * 2 * rows, 64)
        settle(hidden.at[pl.ds(first, 2 * rows)], hidden_recv.at[chip])
        total[...] += lax.dot_general(
            hidden[pl.ds(first, 2 * rows), :],
            tables[pl.ds(first, 2 * rows), :],
            (((0,), (0,)), ((), ())),
            preferred_element_type=F32,
        )

    def begins(way, u):
        return half if (u < UNITS // 2) == (way == 0) else half - 1

    for u in range(UNITS):
        sum_unit(u)
        for way in (0, 1) if u < UNITS // 2 else (1, 0):
            far = begins(way, u)
            send(way, u, 0, 2, own(way, far, u))
            send(way, u, 1, 1, own(way, far - 1, u))
            if far == half:
                send(way, u, 2, 1, own(way, far - 3, u))
    for u in range(UNITS):
        for way in (0, 1) if u < UNITS // 2 else (1, 0):
            far = begins(way, u) - 2
            value = own(way, far, u) + take(way, u, 0) + take(way, u, 1)
            send(way, u, 3, far - half + 4, value)

    @pl.loop(chips // 2, chips)
    def _(j):
        send_hidden(j)

    total[...] = jnp.zeros_like(total)
    weighed = 0
    for slot in range(4, SLOTS):
        distance = half - slot
        for u in range(UNITS):
            for way in (0, 1) if u < UNITS // 2 else (1, 0):
                value = own(way, distance, u) + take(way, u, slot - 1)
                if slot == 4 and begins(way, u) == half:
                    value = value + take(way, u, 2)
                send(way, u, slot, 1, value)
        if slot > 4:

            @pl.loop(weighed, weighed + 3)
            def _(m):
                add_weight(m)

            weighed += 3

    for u in range(UNITS):
        value = own_part(z, u)
        for way in range(2):
            value = value + take(way, u, SLOTS - 1)
        last[:, u * span : (u + 1) * span] = value.astype(BF16)

        @pl.loop(u * (chips // UNITS), (u + 1) * (chips // UNITS))
        def _(j):
            block = last.at[:, pl.ds(pl.multiple_of(j * rows, rows), rows)]
            dest = strip_rows(final, column)

            @pl.when(j != column)
            def _():
                remote(block, dest, last_sent, last_recv, 2 * j + core, z).start()

            @pl.when(j == column)
            def _():
                pltpu.make_async_copy(block, dest, last_recv).start()

    @pl.loop(weighed, chips)
    def _(m):
        add_weight(m)

    grad_weight[...] = total[...].T

    settle(final, last_recv)
    whole = final[...].astype(F32).T.astype(BF16)
    grad_query[...] = whole[:query_rows, :]
    grad_passage[...] = whole[query_rows:, :]

    settle(pools.at[pl.ds(0, chips - 1)], pool_sent)
    settle(pools.at[pl.ds(0, chips)], twin_sent)
    settle(spots.at[pl.ds(0, chips - 1)], spot_sent)
    settle(spots.at[pl.ds(0, chips)], spot_twin_sent)
    settle(part_in.at[pl.ds(0, planes - 1)], one_sent)
    swap.wait_send()

    @pl.when(takes_strips)
    def _():
        settle(mixed.at[pl.ds(0, (half - 1) * strip)], mixed_sent)
        settle(mixed, mixed_twin_sent)

    @pl.when(jnp.logical_not(takes_strips))
    def _():
        settle(mixed.at[pl.ds(0, half * strip)], mixed_sent)

    settle(hidden.at[pl.ds(0, (groups - 1) * rows)], hidden_sent)
    settle(stage.at[pl.ds(0, (2 * half - 1) * UNITS)], ring_sent)
    settle(last.at[:, pl.ds(0, (chips - 1) * rows)], last_sent)


def hand_over(*refs):
    count = (len(refs) - 1) // 3
    sources, dests, holds = refs[:count], refs[count : 2 * count], refs[2 * count : -1]
    arrive = [pltpu.make_async_copy(sources[n], holds[n], refs[-1].at[n]) for n in range(count)]
    leave = [pltpu.make_async_copy(holds[n], dests[n], refs[-1].at[n]) for n in range(count)]
    for copy in arrive:
        copy.start()
    for n in range(count):
        arrive[n].wait()
        leave[n].start()
    for copy in leave:
        copy.wait()


def on_device(
    groups,
    planes,
    query_hidden,
    passage_hidden,
    query_logits,
    passage_logits,
    head_weight,
    query_mask,
    passage_mask,
    positive,
    score_scale,
):
    width = query_hidden.shape[2]
    query_rows = query_hidden.shape[0] * query_hidden.shape[1]
    passage_rows = passage_hidden.shape[0] * passage_hidden.shape[1]
    rows = query_rows + passage_rows
    vocab_local, block = head_weight.shape
    chips = groups // 2
    half = planes // 2
    strip = 2 * block // chips
    sequences = 4 * groups
    vmem = pl.BlockSpec(memory_space=pltpu.VMEM)
    main = pl.BlockSpec(memory_space=pltpu.HBM)
    units = 2 * UNITS * SLOTS
    span = rows * chips // UNITS
    dma = pltpu.SemaphoreType.DMA
    grad_query, grad_passage, grad_weight = pl.pallas_call(
        functools.partial(kernel, groups, planes),
        out_shape=(
            jax.ShapeDtypeStruct((query_rows, 2 * block), BF16),
            jax.ShapeDtypeStruct((passage_rows, 2 * block), BF16),
            jax.ShapeDtypeStruct((vocab_local, block), F32),
        ),
        in_specs=[main] * 8 + [pl.BlockSpec(memory_space=pltpu.SMEM)],
        out_specs=(vmem, vmem, vmem),
        scratch_shapes=[
            pltpu.VMEM(query_logits.shape, F32),
            pltpu.VMEM(passage_logits.shape, F32),
            pltpu.VMEM(head_weight.shape, BF16),
            pltpu.VMEM(query_mask.shape, jnp.int32),
            pltpu.VMEM(passage_mask.shape, jnp.int32),
            pltpu.VMEM((1, positive.shape[0]), jnp.int32),
            pltpu.VMEM((groups, 8, vocab_local // 2), F32),
            pltpu.VMEM((groups, 8, vocab_local // 2), F32),
            pltpu.VMEM((sequences, vocab_local), F32),
            pltpu.VMEM((sequences, vocab_local), F32),
            pltpu.VMEM((chips, sequences), F32),
            pltpu.VMEM((planes, chips, sequences), F32),
            pltpu.VMEM((2, chips, sequences), F32),
            pltpu.VMEM((block, vocab_local), BF16),
            pltpu.VMEM((2 * block, vocab_local), BF16),
            pltpu.VMEM((groups * rows, block), BF16),
            pltpu.VMEM((groups * rows, vocab_local), BF16),
            pltpu.VMEM((2 * block, chips * rows), F32),
            pltpu.VMEM((units, strip, span), BF16),
            pltpu.VMEM((units, strip, span), BF16),
            pltpu.VMEM((strip, chips * rows), BF16),
            pltpu.VMEM((2 * block, rows), BF16),
            pltpu.VMEM((block, vocab_local), F32),
            dma((6,)),
            dma((11,)),
            dma((chips,)),
            dma,
            dma((chips,)),
            dma,
            dma,
            dma,
            dma((chips,)),
            dma,
            dma((chips,)),
            dma((units,)),
            dma,
        ],
        compiler_params=pltpu.CompilerParams(
            collective_id=0, has_side_effects=True, vmem_limit_bytes=60 * 1024 * 1024
        ),
    )(
        query_hidden.reshape(query_rows, width),
        passage_hidden.reshape(passage_rows, width),
        query_logits,
        passage_logits,
        head_weight,
        query_mask,
        passage_mask,
        positive.reshape(1, -1),
        score_scale,
    )
    results = (grad_query, grad_passage, grad_weight)
    grad_query, grad_passage, grad_weight = pl.pallas_call(
        hand_over,
        out_shape=tuple(jax.ShapeDtypeStruct(r.shape, r.dtype) for r in results),
        in_specs=[main] * 3,
        out_specs=(main,) * 3,
        scratch_shapes=[pltpu.VMEM(r.shape, r.dtype) for r in results] + [dma((3,))],
        compiler_params=pltpu.CompilerParams(vmem_limit_bytes=60 * 1024 * 1024),
    )(*results)
    return (
        grad_query.reshape(query_hidden.shape[:2] + (2 * block,)),
        grad_passage.reshape(passage_hidden.shape[:2] + (2 * block,)),
        grad_weight,
    )


def solution(mesh):
    in_specs = (
        P("dp", None, None),
        P("dp", None, None),
        P("dp", None, "vocab"),
        P("dp", None, "vocab"),
        P("vocab", "dp"),
        P("dp", None),
        P("dp", None),
        P(),
        P(),
    )
    out_specs = (P("dp", None, "vocab"), P("dp", None, "vocab"), P("vocab", "dp"))
    return jax.shard_map(
        functools.partial(on_device, mesh.shape["dp"], mesh.shape["vocab"]),
        mesh=mesh,
        in_specs=in_specs,
        out_specs=out_specs,
        check_vma=False,
    )
```

```python
import functools

import jax
import jax.numpy as jnp
from jax import lax
from jax.experimental import pallas as pl
from jax.experimental.pallas import tpu as pltpu
from jax.sharding import PartitionSpec as P

MESH = pl.DeviceIdType.MESH
HIGHEST = lax.Precision.HIGHEST
LOSS_SCALE = 256.0
QUERY_WEIGHT = 3.0
PASSAGE_WEIGHT = 1.0
F32 = jnp.float32
BF16 = jnp.bfloat16
UNITS = 4


def pooled(logits, length):
    spots = lax.broadcasted_iota(jnp.int32, logits.shape, 0).astype(F32)
    masked = jnp.where(spots < length, logits, -jnp.inf)
    largest = jnp.max(masked, axis=0, keepdims=True)
    where = jnp.min(jnp.where(masked == largest, spots, 1e9), axis=0, keepdims=True)
    return largest, where


def kernel(
    groups,
    planes,
    query_hidden,
    passage_hidden,
    query_logits_in,
    passage_logits_in,
    weight_in,
    query_mask_in,
    passage_mask_in,
    positive_in,
    scale,
    grad_query,
    grad_passage,
    grad_weight,
    query_logits,
    passage_logits,
    weight,
    query_mask,
    passage_mask,
    positive,
    pools,
    spots,
    rep,
    push,
    part_out,
    part_in,
    part_sum,
    turned,
    mixed,
    hidden,
    tables,
    partial,
    stage,
    inbox,
    last,
    final,
    total,
    query_out,
    passage_out,
    weight_out,
    load,
    sent,
    pool_recv,
    twin_recv,
    spot_recv,
    spot_twin_recv,
    one_recv,
    two_recv,
    mixed_recv,
    mixed_twin_recv,
    hidden_recv,
    ring_recv,
    last_recv,
    leave,
):
    chips = groups // 2
    half = planes // 2
    query_length = query_logits.shape[1]
    passage_length = passage_logits.shape[1]
    vocab_local = query_logits.shape[2]
    query_rows = 2 * query_length
    rows = query_rows + 2 * passage_length
    width = weight.shape[1]
    queries = 2 * groups
    strip = 2 * width // chips
    span = rows * chips // UNITS
    me = lax.axis_index("dp")
    z = lax.axis_index("vocab")
    column = lax.div(me, 2)
    core = lax.rem(me, 2)
    twin = 2 * column + 1 - core
    pool_sent, twin_sent, spot_sent, spot_twin_sent, one_sent = (sent.at[i] for i in range(5))
    two_sent, mixed_sent, mixed_twin_sent, hidden_sent = (sent.at[i] for i in range(5, 9))
    ring_sent, last_sent = sent.at[9], sent.at[10]

    def ring(value, size):
        return lax.rem(value + 2 * size, size)

    def remote(source, dest, send, recv, target, plane):
        return pltpu.make_async_remote_copy(
            src_ref=source,
            dst_ref=dest,
            send_sem=send,
            recv_sem=recv,
            device_id=(target, plane),
            device_id_type=MESH,
        )

    def settle(ref, sem):
        pltpu.make_async_copy(ref, ref, sem).wait()

    loads = [
        pltpu.make_async_copy(source, dest, load.at[n])
        for n, (source, dest) in enumerate(
            (
                (query_mask_in, query_mask),
                (passage_mask_in, passage_mask),
                (query_logits_in, query_logits),
                (passage_logits_in, passage_logits),
                (weight_in, weight),
                (positive_in, positive),
            )
        )
    ]
    for copy in loads:
        copy.start()

    barrier = pltpu.get_barrier_semaphore()

    def greet(dp_index, plane):
        pl.semaphore_signal(barrier, inc=1, device_id=(dp_index, plane), device_id_type=MESH)

    @pl.loop(1, planes)
    def _(i):
        greet(me, ring(z + i, planes))

    @pl.loop(1, groups)
    def _(i):
        greet(ring(me + i, groups), z)

    def lengths(mask):
        return jnp.sum(mask[...].astype(F32), axis=1, keepdims=True)

    for copy in loads[:4]:
        copy.wait()
    query_lengths = lengths(query_mask)
    passage_lengths = lengths(passage_mask)
    found = [pooled(query_logits[s], query_lengths[s : s + 1, :]) for s in range(2)]
    found += [pooled(passage_logits[s], passage_lengths[s : s + 1, :]) for s in range(2)]
    middle = vocab_local // 2

    def folded(lines):
        return jnp.concatenate(
            [line[:, :middle] for line in lines] + [line[:, middle:] for line in lines], axis=0
        )

    pools[me] = folded([f[0] for f in found])
    spots[me] = folded([f[1] for f in found])
    for copy in loads[4:]:
        copy.wait()
    turned[...] = weight[...].astype(F32).T.astype(BF16)

    pl.semaphore_wait(barrier, groups + planes - 2)

    def pool_copy(group, target, m):
        return remote(pools.at[group], pools.at[group], pool_sent, pool_recv.at[m], target, z)

    def pool_twin(group):
        return remote(pools.at[group], pools.at[group], twin_sent, twin_recv, twin, z)

    def spot_copy(group, target, m):
        return remote(spots.at[group], spots.at[group], spot_sent, spot_recv.at[m], target, z)

    def spot_twin(group):
        return remote(spots.at[group], spots.at[group], spot_twin_sent, spot_twin_recv, twin, z)

    def spread_out(copy, twin_copy):
        @pl.loop(1, chips)
        def _(m):
            copy(me, 2 * ring(column + m, chips) + core, m).start()

        twin_copy(me).start()

    def hand_on(copy, twin_copy):
        @pl.loop(1, chips)
        def _(m):
            group = 2 * ring(column - m, chips) + core
            copy(group, me, m).wait_recv()
            twin_copy(group).start()

    spread_out(pool_copy, pool_twin)
    hand_on(pool_copy, pool_twin)

    def strip_rows(ref, index):
        return ref.at[pl.ds(pl.multiple_of(index * strip, strip), strip)]

    @pl.loop(0, half)
    def _(i):
        chip = core * half + ring(i + column, half)

        @pl.when(chip != column)
        def _():
            remote(
                strip_rows(turned, chip - core * half),
                strip_rows(mixed, column),
                mixed_sent,
                mixed_recv.at[column],
                2 * chip + core,
                z,
            ).start()

        @pl.when(chip == column)
        def _():
            pltpu.make_async_copy(
                strip_rows(turned, chip - core * half),
                strip_rows(mixed, column),
                mixed_recv.at[column],
            ).start()

    takes_strips = core == lax.div(column, half)

    def pool_rows(k):
        return jnp.concatenate([pools[:, k, :], pools[:, 4 + k, :]], axis=1)

    settle(pools.at[pl.ds(0, chips)], twin_recv)
    for k in range(4):
        rep[k * groups : (k + 1) * groups, :] = jnp.log1p(jnp.maximum(pool_rows(k), 0.0))
    part = lax.dot_general(
        rep[pl.ds(pl.multiple_of(core * groups, groups), groups), :],
        rep[queries:, :],
        (((1,), (1,)), ((), ())),
        precision=HIGHEST,
        preferred_element_type=F32,
    )
    fold = groups // 2
    part_out[...] = jnp.concatenate([part[:fold, :], part[fold:, :]], axis=1)

    @pl.loop(1, planes)
    def _(i):
        remote(part_out, part_in.at[z], one_sent, one_recv, me, ring(z + i, planes)).start()

    part_in[z] = part_out[...]
    spread_out(spot_copy, spot_twin)
    hand_on(spot_copy, spot_twin)

    @pl.when(takes_strips)
    def _():
        @pl.loop(0, chips)
        def _(chip):
            landed = strip_rows(mixed, chip)
            settle(landed, mixed_recv.at[chip])
            remote(landed, landed, mixed_twin_sent, mixed_twin_recv, twin, z).start()

    def send_hidden(j):
        for cr in range(2):
            target = 2 * ring(column - j, chips) + cr
            columns = pl.ds(pl.multiple_of(target * width, width), width)
            for source, start, count in (
                (query_hidden, 0, query_rows),
                (passage_hidden, query_rows, rows - query_rows),
            ):
                block = source.at[:, columns]
                dest = hidden.at[pl.ds(pl.multiple_of(me * rows + start, 64), count)]
                arrived = hidden_recv.at[column]

                @pl.when(target != me)
                def _():
                    remote(block, dest, hidden_sent, arrived, target, z).start()

                @pl.when(target == me)
                def _():
                    pltpu.make_async_copy(block, dest, arrived).start()

    @pl.loop(0, chips // 2)
    def _(j):
        send_hidden(j)

    settle(part_in.at[pl.ds(0, planes - 1)], one_recv)
    summed = part_in[0]
    for b in range(1, planes):
        summed = summed + part_in[b]
    part_sum[core] = summed
    swap = remote(part_sum.at[core], part_sum.at[core], two_sent, two_recv, twin, z)
    swap.start()
    swap.wait_recv()

    factor = scale[0] / (vocab_local * planes)
    sums = jnp.concatenate(
        [part_sum[k][:, h * queries : (h + 1) * queries] for k in range(2) for h in range(2)],
        axis=0,
    )
    scores = sums * factor
    weights = jnp.exp(scores - jnp.max(scores, axis=1, keepdims=True))
    soft = weights / jnp.sum(weights, axis=1, keepdims=True)
    row = lax.broadcasted_iota(jnp.int32, scores.shape, 0)
    lane = lax.broadcasted_iota(jnp.int32, scores.shape, 1)

    def natural(index):
        return jnp.where(index < groups, 2 * index, 2 * (index - groups) + 1)

    wanted = jnp.sum(
        jnp.where(
            lane == natural(row),
            jnp.broadcast_to(positive[...].astype(F32), scores.shape),
            0.0,
        ),
        axis=1,
        keepdims=True,
    )
    excess = soft - jnp.where(natural(lane).astype(F32) == wanted, 1.0, 0.0)
    nothing = jnp.zeros_like(excess)
    corner = jnp.concatenate(
        [
            jnp.concatenate([nothing, excess], axis=1),
            jnp.concatenate([nothing, nothing], axis=1),
        ],
        axis=0,
    )
    full_row = lax.broadcasted_iota(jnp.int32, corner.shape, 0)
    full_lane = lax.broadcasted_iota(jnp.int32, corner.shape, 1)
    query_part = jnp.logical_and(full_row < queries, full_lane < queries)
    passage_part = jnp.logical_and(full_row >= queries, full_lane >= queries)
    means = jnp.where(
        query_part,
        2.0 * QUERY_WEIGHT / queries / queries,
        jnp.where(passage_part, 2.0 * PASSAGE_WEIGHT / queries / queries, 0.0),
    )
    mixing = LOSS_SCALE * (factor * (corner + corner.T) + means)
    gradient = jnp.dot(mixing, rep[...], precision=HIGHEST, preferred_element_type=F32)
    for k in range(4):
        pool = pool_rows(k)
        slope = jnp.where(pool > 0.0, 1.0 / (1.0 + jnp.maximum(pool, 0.0)), 0.0)
        pushed = gradient[k * groups : (k + 1) * groups, :] * slope
        push[k * groups : (k + 1) * groups, :] = pushed.astype(BF16).astype(F32)

    settle(spots.at[pl.ds(0, chips)], spot_twin_recv)

    @pl.when(jnp.logical_not(takes_strips))
    def _():
        settle(mixed, mixed_twin_recv)

    def table_of(group):
        parts = []
        for k in range(4):
            length = query_length if k < 2 else passage_length
            push_row = push[pl.ds(k * groups + group, 1), :]
            spot_row = jnp.concatenate(
                [spots[group, k : k + 1, :], spots[group, 4 + k : 5 + k, :]], axis=1
            )
            positions = lax.broadcasted_iota(jnp.int32, (length, vocab_local), 0).astype(F32)
            parts.append(jnp.where(positions == spot_row, push_row, 0.0).astype(BF16))
        return jnp.concatenate(parts, axis=0)

    def keep(group, value):
        tables[pl.ds(pl.multiple_of(group * rows, rows), rows), :] = value

    def sum_unit(u):
        members = [2 * j + core for j in range(u * (chips // UNITS), (u + 1) * (chips // UNITS))]
        parts = [table_of(group) for group in members]
        partial[:, u * span : (u + 1) * span] = lax.dot_general(
            mixed[...],
            jnp.concatenate(parts, axis=0),
            (((1,), (1,)), ((), ())),
            preferred_element_type=F32,
        )
        for group, value in zip(members, parts):
            keep(group, value)

    def own_part(plane, u):
        return partial[
            pl.ds(pl.multiple_of(plane * strip, strip), strip), u * span : (u + 1) * span
        ]

    def place(way, step, u):
        return (way * half + step) * UNITS + u

    def ring_copy(way, step, u):
        index = place(way, step, u)
        neighbour = ring(z + 1 - 2 * way, planes)
        return remote(
            stage.at[index], inbox.at[index], ring_sent, ring_recv.at[index], me, neighbour
        )

    def owner_of(way, step):
        return ring(z + (1 - 2 * way) * (half - step), planes)

    def ring_step(step, way, u, follows):
        value = own_part(owner_of(way, step), u)
        if follows:
            ring_copy(way, step - 1, u).wait_recv()
            value = value + inbox[place(way, step - 1, u)].astype(F32)
        stage[place(way, step, u)] = value.astype(BF16)
        ring_copy(way, step, u).start()

    def add_weight(m):
        chip = ring(column + m, chips)
        other = 2 * chip + 1 - core
        keep(other, table_of(other))
        first = pl.multiple_of(chip * 2 * rows, 64)
        settle(hidden.at[pl.ds(first, 2 * rows)], hidden_recv.at[chip])
        total[...] += lax.dot_general(
            hidden[pl.ds(first, 2 * rows), :],
            tables[pl.ds(first, 2 * rows), :],
            (((0,), (0,)), ((), ())),
            preferred_element_type=F32,
        )

    for u in range(UNITS):
        way = 0 if u < UNITS // 2 else 1
        sum_unit(u)
        ring_step(0, way, u, False)
        ring_step(1, 1 - way, u, False)
    for u in range(UNITS):
        ring_step(1, 0 if u < UNITS // 2 else 1, u, True)

    @pl.loop(chips // 2, chips)
    def _(j):
        send_hidden(j)

    total[...] = jnp.zeros_like(total)

    @pl.loop(2, half)
    def _(step):
        for u in range(UNITS):
            for way in range(2):
                ring_step(step, way, u, True)

        @pl.when(step >= 3)
        def _():
            for i in range(2):
                add_weight(2 * (step - 3) + i)

    for u in range(UNITS):
        value = own_part(z, u)
        for way in range(2):
            ring_copy(way, half - 1, u).wait_recv()
            value = value + inbox[place(way, half - 1, u)].astype(F32)
        last[:, u * span : (u + 1) * span] = value.astype(BF16)

        @pl.loop(u * (chips // UNITS), (u + 1) * (chips // UNITS))
        def _(j):
            block = last.at[:, pl.ds(pl.multiple_of(j * rows, rows), rows)]
            dest = strip_rows(final, column)

            @pl.when(j != column)
            def _():
                remote(block, dest, last_sent, last_recv, 2 * j + core, z).start()

            @pl.when(j == column)
            def _():
                pltpu.make_async_copy(block, dest, last_recv).start()

    @pl.loop(max(0, 2 * (half - 3)), chips)
    def _(m):
        add_weight(m)

    results = [
        pltpu.make_async_copy(source, dest, leave.at[n])
        for n, (source, dest) in enumerate(
            ((weight_out, grad_weight), (query_out, grad_query), (passage_out, grad_passage))
        )
    ]
    weight_out[...] = total[...].T
    results[0].start()

    settle(final, last_recv)
    whole = final[...].astype(F32).T.astype(BF16)
    query_out[...] = whole[:query_rows, :]
    passage_out[...] = whole[query_rows:, :]
    for copy in results[1:]:
        copy.start()

    settle(pools.at[pl.ds(0, chips - 1)], pool_sent)
    settle(pools.at[pl.ds(0, chips)], twin_sent)
    settle(spots.at[pl.ds(0, chips - 1)], spot_sent)
    settle(spots.at[pl.ds(0, chips)], spot_twin_sent)
    settle(part_in.at[pl.ds(0, planes - 1)], one_sent)
    swap.wait_send()

    @pl.when(takes_strips)
    def _():
        settle(mixed.at[pl.ds(0, (half - 1) * strip)], mixed_sent)
        settle(mixed, mixed_twin_sent)

    @pl.when(jnp.logical_not(takes_strips))
    def _():
        settle(mixed.at[pl.ds(0, half * strip)], mixed_sent)

    settle(hidden.at[pl.ds(0, (groups - 1) * rows)], hidden_sent)
    settle(stage.at[pl.ds(0, (2 * half - 1) * UNITS)], ring_sent)
    settle(last.at[:, pl.ds(0, (chips - 1) * rows)], last_sent)
    for copy in results:
        copy.wait()


def hand_over(*refs):
    count = (len(refs) - 1) // 3
    sources, dests, holds = refs[:count], refs[count : 2 * count], refs[2 * count : -1]
    arrive = [pltpu.make_async_copy(sources[n], holds[n], refs[-1].at[n]) for n in range(count)]
    leave = [pltpu.make_async_copy(holds[n], dests[n], refs[-1].at[n]) for n in range(count)]
    for copy in arrive:
        copy.start()
    for n in range(count):
        arrive[n].wait()
        leave[n].start()
    for copy in leave:
        copy.wait()


def on_device(
    groups,
    planes,
    query_hidden,
    passage_hidden,
    query_logits,
    passage_logits,
    head_weight,
    query_mask,
    passage_mask,
    positive,
    score_scale,
):
    width = query_hidden.shape[2]
    query_rows = query_hidden.shape[0] * query_hidden.shape[1]
    passage_rows = passage_hidden.shape[0] * passage_hidden.shape[1]
    rows = query_rows + passage_rows
    vocab_local, block = head_weight.shape
    chips = groups // 2
    half = planes // 2
    strip = 2 * block // chips
    sequences = 4 * groups
    main = pl.BlockSpec(memory_space=pltpu.HBM)
    units = 2 * half * UNITS
    span = rows * chips // UNITS
    dma = pltpu.SemaphoreType.DMA
    grad_query, grad_passage, grad_weight = pl.pallas_call(
        functools.partial(kernel, groups, planes),
        out_shape=(
            jax.ShapeDtypeStruct((query_rows, 2 * block), BF16),
            jax.ShapeDtypeStruct((passage_rows, 2 * block), BF16),
            jax.ShapeDtypeStruct((vocab_local, block), F32),
        ),
        in_specs=[main] * 8 + [pl.BlockSpec(memory_space=pltpu.SMEM)],
        out_specs=(main,) * 3,
        scratch_shapes=[
            pltpu.VMEM(query_logits.shape, F32),
            pltpu.VMEM(passage_logits.shape, F32),
            pltpu.VMEM(head_weight.shape, BF16),
            pltpu.VMEM(query_mask.shape, jnp.int32),
            pltpu.VMEM(passage_mask.shape, jnp.int32),
            pltpu.VMEM((1, positive.shape[0]), jnp.int32),
            pltpu.VMEM((groups, 8, vocab_local // 2), F32),
            pltpu.VMEM((groups, 8, vocab_local // 2), F32),
            pltpu.VMEM((sequences, vocab_local), F32),
            pltpu.VMEM((sequences, vocab_local), F32),
            pltpu.VMEM((chips, sequences), F32),
            pltpu.VMEM((planes, chips, sequences), F32),
            pltpu.VMEM((2, chips, sequences), F32),
            pltpu.VMEM((block, vocab_local), BF16),
            pltpu.VMEM((2 * block, vocab_local), BF16),
            pltpu.VMEM((groups * rows, block), BF16),
            pltpu.VMEM((groups * rows, vocab_local), BF16),
            pltpu.VMEM((2 * block, chips * rows), F32),
            pltpu.VMEM((units, strip, span), BF16),
            pltpu.VMEM((units, strip, span), BF16),
            pltpu.VMEM((strip, chips * rows), BF16),
            pltpu.VMEM((2 * block, rows), BF16),
            pltpu.VMEM((block, vocab_local), F32),
            pltpu.VMEM((query_rows, 2 * block), BF16),
            pltpu.VMEM((passage_rows, 2 * block), BF16),
            pltpu.VMEM((vocab_local, block), F32),
            dma((6,)),
            dma((11,)),
            dma((chips,)),
            dma,
            dma((chips,)),
            dma,
            dma,
            dma,
            dma((chips,)),
            dma,
            dma((chips,)),
            dma((units,)),
            dma,
            dma((3,)),
        ],
        compiler_params=pltpu.CompilerParams(
            collective_id=0, has_side_effects=True, vmem_limit_bytes=60 * 1024 * 1024
        ),
    )(
        query_hidden.reshape(query_rows, width),
        passage_hidden.reshape(passage_rows, width),
        query_logits,
        passage_logits,
        head_weight,
        query_mask,
        passage_mask,
        positive.reshape(1, -1),
        score_scale,
    )
    results = (grad_query, grad_passage, grad_weight)
    grad_query, grad_passage, grad_weight = pl.pallas_call(
        hand_over,
        out_shape=tuple(jax.ShapeDtypeStruct(r.shape, r.dtype) for r in results),
        in_specs=[main] * 3,
        out_specs=(main,) * 3,
        scratch_shapes=[pltpu.VMEM(r.shape, r.dtype) for r in results] + [dma((3,))],
        compiler_params=pltpu.CompilerParams(vmem_limit_bytes=60 * 1024 * 1024),
    )(*results)
    return (
        grad_query.reshape(query_hidden.shape[:2] + (2 * block,)),
        grad_passage.reshape(passage_hidden.shape[:2] + (2 * block,)),
        grad_weight,
    )


def solution(mesh):
    in_specs = (
        P("dp", None, None),
        P("dp", None, None),
        P("dp", None, "vocab"),
        P("dp", None, "vocab"),
        P("vocab", "dp"),
        P("dp", None),
        P("dp", None),
        P(),
        P(),
    )
    out_specs = (P("dp", None, "vocab"), P("dp", None, "vocab"), P("vocab", "dp"))
    return jax.shard_map(
        functools.partial(on_device, mesh.shape["dp"], mesh.shape["vocab"]),
        mesh=mesh,
        in_specs=in_specs,
        out_specs=out_specs,
        check_vma=False,
    )
```

```python
import functools

import jax
import jax.numpy as jnp
from jax import lax
from jax.experimental import pallas as pl
from jax.experimental.pallas import tpu as pltpu
from jax.sharding import PartitionSpec as P

MESH = pl.DeviceIdType.MESH
HIGHEST = lax.Precision.HIGHEST
LOSS_SCALE = 256.0
QUERY_WEIGHT = 3.0
PASSAGE_WEIGHT = 1.0
F32 = jnp.float32
BF16 = jnp.bfloat16
UNITS = 4


def pooled(logits, length):
    spots = lax.broadcasted_iota(jnp.int32, logits.shape, 0).astype(F32)
    masked = jnp.where(spots < length, logits, -jnp.inf)
    largest = jnp.max(masked, axis=0, keepdims=True)
    where = jnp.min(jnp.where(masked == largest, spots, 1e9), axis=0, keepdims=True)
    return largest, where


def kernel(
    groups,
    planes,
    query_hidden,
    passage_hidden,
    query_logits_in,
    passage_logits_in,
    weight_in,
    query_mask_in,
    passage_mask_in,
    positive_in,
    scale,
    grad_query,
    grad_passage,
    grad_weight,
    query_logits,
    passage_logits,
    weight,
    query_mask,
    passage_mask,
    positive,
    pools,
    spots,
    rep,
    push,
    part_out,
    part_in,
    part_sum,
    turned,
    mixed,
    held,
    hidden,
    tables,
    partial,
    stage,
    inbox,
    last,
    final,
    total,
    query_out,
    passage_out,
    weight_out,
    load,
    sent,
    pool_recv,
    twin_recv,
    spot_recv,
    spot_twin_recv,
    one_recv,
    two_recv,
    mixed_recv,
    mixed_twin_recv,
    hidden_recv,
    ring_recv,
    last_recv,
    leave,
):
    chips = groups // 2
    half = planes // 2
    query_length = query_logits.shape[1]
    passage_length = passage_logits.shape[1]
    vocab_local = query_logits.shape[2]
    query_rows = 2 * query_length
    rows = query_rows + 2 * passage_length
    width = weight.shape[1]
    queries = 2 * groups
    strip = 2 * width // chips
    span = rows * chips // UNITS
    me = lax.axis_index("dp")
    z = lax.axis_index("vocab")
    column = lax.div(me, 2)
    core = lax.rem(me, 2)
    twin = 2 * column + 1 - core
    pool_sent, twin_sent, spot_sent, spot_twin_sent, one_sent = (sent.at[i] for i in range(5))
    two_sent, mixed_sent, mixed_twin_sent, hidden_sent = (sent.at[i] for i in range(5, 9))
    ring_sent, last_sent = sent.at[9], sent.at[10]

    def ring(value, size):
        return lax.rem(value + 2 * size, size)

    def remote(source, dest, send, recv, target, plane):
        return pltpu.make_async_remote_copy(
            src_ref=source,
            dst_ref=dest,
            send_sem=send,
            recv_sem=recv,
            device_id=(target, plane),
            device_id_type=MESH,
        )

    def settle(ref, sem):
        pltpu.make_async_copy(ref, ref, sem).wait()

    loads = [
        pltpu.make_async_copy(source, dest, load.at[n])
        for n, (source, dest) in enumerate(
            (
                (query_mask_in, query_mask),
                (passage_mask_in, passage_mask),
                (query_logits_in, query_logits),
                (passage_logits_in, passage_logits),
                (weight_in, weight),
                (positive_in, positive),
                (query_hidden, held.at[pl.ds(0, query_rows)]),
                (passage_hidden, held.at[pl.ds(query_rows, rows - query_rows)]),
            )
        )
    ]
    for copy in loads:
        copy.start()

    barrier = pltpu.get_barrier_semaphore()

    def greet(dp_index, plane):
        pl.semaphore_signal(barrier, inc=1, device_id=(dp_index, plane), device_id_type=MESH)

    @pl.loop(1, planes)
    def _(i):
        greet(me, ring(z + i, planes))

    @pl.loop(1, groups)
    def _(i):
        greet(ring(me + i, groups), z)

    def lengths(mask):
        return jnp.sum(mask[...].astype(F32), axis=1, keepdims=True)

    for copy in loads[:4]:
        copy.wait()
    query_lengths = lengths(query_mask)
    passage_lengths = lengths(passage_mask)
    found = [pooled(query_logits[s], query_lengths[s : s + 1, :]) for s in range(2)]
    found += [pooled(passage_logits[s], passage_lengths[s : s + 1, :]) for s in range(2)]
    middle = vocab_local // 2

    def folded(lines):
        return jnp.concatenate(
            [line[:, :middle] for line in lines] + [line[:, middle:] for line in lines], axis=0
        )

    pools[me] = folded([f[0] for f in found])
    spots[me] = folded([f[1] for f in found])
    for copy in loads[4:]:
        copy.wait()
    turned[...] = weight[...].astype(F32).T.astype(BF16)

    pl.semaphore_wait(barrier, groups + planes - 2)

    def pool_copy(group, target, m):
        return remote(pools.at[group], pools.at[group], pool_sent, pool_recv.at[m], target, z)

    def pool_twin(group):
        return remote(pools.at[group], pools.at[group], twin_sent, twin_recv, twin, z)

    def spot_copy(group, target, m):
        return remote(spots.at[group], spots.at[group], spot_sent, spot_recv.at[m], target, z)

    def spot_twin(group):
        return remote(spots.at[group], spots.at[group], spot_twin_sent, spot_twin_recv, twin, z)

    def spread_out(copy, twin_copy):
        @pl.loop(1, chips)
        def _(m):
            copy(me, 2 * ring(column + m, chips) + core, m).start()

        twin_copy(me).start()

    def hand_on(copy, twin_copy):
        @pl.loop(1, chips)
        def _(m):
            group = 2 * ring(column - m, chips) + core
            copy(group, me, m).wait_recv()
            twin_copy(group).start()

    spread_out(pool_copy, pool_twin)
    hand_on(pool_copy, pool_twin)

    def strip_rows(ref, index):
        return ref.at[pl.ds(pl.multiple_of(index * strip, strip), strip)]

    @pl.loop(0, half)
    def _(i):
        chip = core * half + ring(i + column, half)

        @pl.when(chip != column)
        def _():
            remote(
                strip_rows(turned, chip - core * half),
                strip_rows(mixed, column),
                mixed_sent,
                mixed_recv.at[column],
                2 * chip + core,
                z,
            ).start()

        @pl.when(chip == column)
        def _():
            pltpu.make_async_copy(
                strip_rows(turned, chip - core * half),
                strip_rows(mixed, column),
                mixed_recv.at[column],
            ).start()

    takes_strips = core == lax.div(column, half)

    def pool_rows(k):
        return jnp.concatenate([pools[:, k, :], pools[:, 4 + k, :]], axis=1)

    settle(pools.at[pl.ds(0, chips)], twin_recv)
    for k in range(4):
        rep[k * groups : (k + 1) * groups, :] = jnp.log1p(jnp.maximum(pool_rows(k), 0.0))
    part = lax.dot_general(
        rep[pl.ds(pl.multiple_of(core * groups, groups), groups), :],
        rep[queries:, :],
        (((1,), (1,)), ((), ())),
        precision=HIGHEST,
        preferred_element_type=F32,
    )
    fold = groups // 2
    part_out[...] = jnp.concatenate([part[:fold, :], part[fold:, :]], axis=1)

    @pl.loop(1, planes)
    def _(i):
        remote(part_out, part_in.at[z], one_sent, one_recv, me, ring(z + i, planes)).start()

    part_in[z] = part_out[...]
    spread_out(spot_copy, spot_twin)
    hand_on(spot_copy, spot_twin)

    @pl.when(takes_strips)
    def _():
        @pl.loop(0, chips)
        def _(chip):
            landed = strip_rows(mixed, chip)
            settle(landed, mixed_recv.at[chip])
            remote(landed, landed, mixed_twin_sent, mixed_twin_recv, twin, z).start()

    pairs = chips // 2
    pair = lax.div(column, 2)

    def send_hidden(i):
        dest = hidden.at[pl.ds(pl.multiple_of(me * rows, rows), rows)]
        arrived = hidden_recv.at[pair]
        for n in range(4):
            target = 4 * ring(pair - i, pairs) + n
            block = held.at[:, pl.ds(pl.multiple_of(target * width, width), width)]

            @pl.when(target != me)
            def _():
                remote(block, dest, hidden_sent, arrived, target, z).start()

            @pl.when(target == me)
            def _():
                pltpu.make_async_copy(block, dest, arrived).start()

    @pl.loop(0, pairs // 2)
    def _(i):
        send_hidden(i)

    settle(part_in.at[pl.ds(0, planes - 1)], one_recv)
    summed = part_in[0]
    for b in range(1, planes):
        summed = summed + part_in[b]
    part_sum[core] = summed
    swap = remote(part_sum.at[core], part_sum.at[core], two_sent, two_recv, twin, z)
    swap.start()
    swap.wait_recv()

    factor = scale[0] / (vocab_local * planes)
    sums = jnp.concatenate(
        [part_sum[k][:, h * queries : (h + 1) * queries] for k in range(2) for h in range(2)],
        axis=0,
    )
    scores = sums * factor
    weights = jnp.exp(scores - jnp.max(scores, axis=1, keepdims=True))
    soft = weights / jnp.sum(weights, axis=1, keepdims=True)
    row = lax.broadcasted_iota(jnp.int32, scores.shape, 0)
    lane = lax.broadcasted_iota(jnp.int32, scores.shape, 1)

    def natural(index):
        return jnp.where(index < groups, 2 * index, 2 * (index - groups) + 1)

    wanted = jnp.sum(
        jnp.where(
            lane == natural(row),
            jnp.broadcast_to(positive[...].astype(F32), scores.shape),
            0.0,
        ),
        axis=1,
        keepdims=True,
    )
    excess = soft - jnp.where(natural(lane).astype(F32) == wanted, 1.0, 0.0)
    nothing = jnp.zeros_like(excess)
    corner = jnp.concatenate(
        [
            jnp.concatenate([nothing, excess], axis=1),
            jnp.concatenate([nothing, nothing], axis=1),
        ],
        axis=0,
    )
    full_row = lax.broadcasted_iota(jnp.int32, corner.shape, 0)
    full_lane = lax.broadcasted_iota(jnp.int32, corner.shape, 1)
    query_part = jnp.logical_and(full_row < queries, full_lane < queries)
    passage_part = jnp.logical_and(full_row >= queries, full_lane >= queries)
    means = jnp.where(
        query_part,
        2.0 * QUERY_WEIGHT / queries / queries,
        jnp.where(passage_part, 2.0 * PASSAGE_WEIGHT / queries / queries, 0.0),
    )
    mixing = LOSS_SCALE * (factor * (corner + corner.T) + means)
    gradient = jnp.dot(mixing, rep[...], precision=HIGHEST, preferred_element_type=F32)
    for k in range(4):
        pool = pool_rows(k)
        slope = jnp.where(pool > 0.0, 1.0 / (1.0 + jnp.maximum(pool, 0.0)), 0.0)
        pushed = gradient[k * groups : (k + 1) * groups, :] * slope
        push[k * groups : (k + 1) * groups, :] = pushed.astype(BF16).astype(F32)

    settle(spots.at[pl.ds(0, chips)], spot_twin_recv)

    @pl.when(jnp.logical_not(takes_strips))
    def _():
        settle(mixed, mixed_twin_recv)

    def table_of(group):
        parts = []
        for k in range(4):
            length = query_length if k < 2 else passage_length
            push_row = push[pl.ds(k * groups + group, 1), :]
            spot_row = jnp.concatenate(
                [spots[group, k : k + 1, :], spots[group, 4 + k : 5 + k, :]], axis=1
            )
            positions = lax.broadcasted_iota(jnp.int32, (length, vocab_local), 0).astype(F32)
            parts.append(jnp.where(positions == spot_row, push_row, 0.0).astype(BF16))
        return jnp.concatenate(parts, axis=0)

    def keep(group, value):
        tables[pl.ds(pl.multiple_of(group * rows, rows), rows), :] = value

    def sum_unit(u):
        members = [2 * j + core for j in range(u * (chips // UNITS), (u + 1) * (chips // UNITS))]
        parts = [table_of(group) for group in members]
        partial[:, u * span : (u + 1) * span] = lax.dot_general(
            mixed[...],
            jnp.concatenate(parts, axis=0),
            (((1,), (1,)), ((), ())),
            preferred_element_type=F32,
        )
        for group, value in zip(members, parts):
            keep(group, value)

    def own_part(plane, u):
        return partial[
            pl.ds(pl.multiple_of(plane * strip, strip), strip), u * span : (u + 1) * span
        ]

    def place(way, step, u):
        return (way * half + step) * UNITS + u

    def ring_copy(way, step, u):
        index = place(way, step, u)
        neighbour = ring(z + 1 - 2 * way, planes)
        return remote(
            stage.at[index], inbox.at[index], ring_sent, ring_recv.at[index], me, neighbour
        )

    def owner_of(way, step):
        return ring(z + (1 - 2 * way) * (half - step), planes)

    def ring_step(step, way, u, follows):
        value = own_part(owner_of(way, step), u)
        if follows:
            ring_copy(way, step - 1, u).wait_recv()
            value = value + inbox[place(way, step - 1, u)].astype(F32)
        stage[place(way, step, u)] = value.astype(BF16)
        ring_copy(way, step, u).start()

    def add_weight(i):
        taken = ring(pair + i, pairs)
        for n in range(2):
            other = 2 * (2 * taken + n) + 1 - core
            keep(other, table_of(other))
        batch = pl.ds(pl.multiple_of(taken * 4 * rows, rows), 4 * rows)
        settle(hidden.at[batch], hidden_recv.at[taken])
        total[...] += lax.dot_general(
            hidden[batch, :],
            tables[batch, :],
            (((0,), (0,)), ((), ())),
            preferred_element_type=F32,
        )

    for u in range(UNITS):
        way = 0 if u < UNITS // 2 else 1
        sum_unit(u)
        ring_step(0, way, u, False)
        ring_step(1, 1 - way, u, False)
    for u in range(UNITS):
        ring_step(1, 0 if u < UNITS // 2 else 1, u, True)

    @pl.loop(pairs // 2, pairs)
    def _(i):
        send_hidden(i)

    total[...] = jnp.zeros_like(total)

    @pl.loop(2, half)
    def _(step):
        for u in range(UNITS):
            for way in range(2):
                ring_step(step, way, u, True)
            if u == UNITS // 2 - 1:

                @pl.when(step >= 3)
                def _():
                    add_weight(step - 3)

    for u in range(UNITS):
        value = own_part(z, u)
        for way in range(2):
            ring_copy(way, half - 1, u).wait_recv()
            value = value + inbox[place(way, half - 1, u)].astype(F32)
        last[:, u * span : (u + 1) * span] = value.astype(BF16)

        @pl.loop(u * (chips // UNITS), (u + 1) * (chips // UNITS))
        def _(j):
            block = last.at[:, pl.ds(pl.multiple_of(j * rows, rows), rows)]
            dest = strip_rows(final, column)

            @pl.when(j != column)
            def _():
                remote(block, dest, last_sent, last_recv, 2 * j + core, z).start()

            @pl.when(j == column)
            def _():
                pltpu.make_async_copy(block, dest, last_recv).start()

    @pl.loop(max(0, half - 3), pairs)
    def _(i):
        add_weight(i)

    results = [
        pltpu.make_async_copy(source, dest, leave.at[n])
        for n, (source, dest) in enumerate(
            ((weight_out, grad_weight), (query_out, grad_query), (passage_out, grad_passage))
        )
    ]
    weight_out[...] = total[...].T
    results[0].start()

    settle(final, last_recv)
    whole = final[...].astype(F32).T.astype(BF16)
    query_out[...] = whole[:query_rows, :]
    passage_out[...] = whole[query_rows:, :]
    for copy in results[1:]:
        copy.start()

    settle(pools.at[pl.ds(0, chips - 1)], pool_sent)
    settle(pools.at[pl.ds(0, chips)], twin_sent)
    settle(spots.at[pl.ds(0, chips - 1)], spot_sent)
    settle(spots.at[pl.ds(0, chips)], spot_twin_sent)
    settle(part_in.at[pl.ds(0, planes - 1)], one_sent)
    swap.wait_send()

    @pl.when(takes_strips)
    def _():
        settle(mixed.at[pl.ds(0, (half - 1) * strip)], mixed_sent)
        settle(mixed, mixed_twin_sent)

    @pl.when(jnp.logical_not(takes_strips))
    def _():
        settle(mixed.at[pl.ds(0, half * strip)], mixed_sent)

    settle(hidden.at[pl.ds(0, (groups - 1) * rows)], hidden_sent)
    settle(stage.at[pl.ds(0, (2 * half - 1) * UNITS)], ring_sent)
    settle(last.at[:, pl.ds(0, (chips - 1) * rows)], last_sent)
    for copy in results:
        copy.wait()


def hand_over(*refs):
    count = (len(refs) - 1) // 3
    sources, dests, holds = refs[:count], refs[count : 2 * count], refs[2 * count : -1]
    arrive = [pltpu.make_async_copy(sources[n], holds[n], refs[-1].at[n]) for n in range(count)]
    leave = [pltpu.make_async_copy(holds[n], dests[n], refs[-1].at[n]) for n in range(count)]
    for copy in arrive:
        copy.start()
    for n in range(count):
        arrive[n].wait()
        leave[n].start()
    for copy in leave:
        copy.wait()


def on_device(
    groups,
    planes,
    query_hidden,
    passage_hidden,
    query_logits,
    passage_logits,
    head_weight,
    query_mask,
    passage_mask,
    positive,
    score_scale,
):
    width = query_hidden.shape[2]
    query_rows = query_hidden.shape[0] * query_hidden.shape[1]
    passage_rows = passage_hidden.shape[0] * passage_hidden.shape[1]
    rows = query_rows + passage_rows
    vocab_local, block = head_weight.shape
    chips = groups // 2
    half = planes // 2
    strip = 2 * block // chips
    sequences = 4 * groups
    main = pl.BlockSpec(memory_space=pltpu.HBM)
    units = 2 * half * UNITS
    span = rows * chips // UNITS
    dma = pltpu.SemaphoreType.DMA
    grad_query, grad_passage, grad_weight = pl.pallas_call(
        functools.partial(kernel, groups, planes),
        out_shape=(
            jax.ShapeDtypeStruct((query_rows, 2 * block), BF16),
            jax.ShapeDtypeStruct((passage_rows, 2 * block), BF16),
            jax.ShapeDtypeStruct((vocab_local, block), F32),
        ),
        in_specs=[main] * 8 + [pl.BlockSpec(memory_space=pltpu.SMEM)],
        out_specs=(main,) * 3,
        scratch_shapes=[
            pltpu.VMEM(query_logits.shape, F32),
            pltpu.VMEM(passage_logits.shape, F32),
            pltpu.VMEM(head_weight.shape, BF16),
            pltpu.VMEM(query_mask.shape, jnp.int32),
            pltpu.VMEM(passage_mask.shape, jnp.int32),
            pltpu.VMEM((1, positive.shape[0]), jnp.int32),
            pltpu.VMEM((groups, 8, vocab_local // 2), F32),
            pltpu.VMEM((groups, 8, vocab_local // 2), F32),
            pltpu.VMEM((sequences, vocab_local), F32),
            pltpu.VMEM((sequences, vocab_local), F32),
            pltpu.VMEM((chips, sequences), F32),
            pltpu.VMEM((planes, chips, sequences), F32),
            pltpu.VMEM((2, chips, sequences), F32),
            pltpu.VMEM((block, vocab_local), BF16),
            pltpu.VMEM((2 * block, vocab_local), BF16),
            pltpu.VMEM((rows, width), BF16),
            pltpu.VMEM((groups * rows, block), BF16),
            pltpu.VMEM((groups * rows, vocab_local), BF16),
            pltpu.VMEM((2 * block, chips * rows), F32),
            pltpu.VMEM((units, strip, span), BF16),
            pltpu.VMEM((units, strip, span), BF16),
            pltpu.VMEM((strip, chips * rows), BF16),
            pltpu.VMEM((2 * block, rows), BF16),
            pltpu.VMEM((block, vocab_local), F32),
            pltpu.VMEM((query_rows, 2 * block), BF16),
            pltpu.VMEM((passage_rows, 2 * block), BF16),
            pltpu.VMEM((vocab_local, block), F32),
            dma((8,)),
            dma((11,)),
            dma((chips,)),
            dma,
            dma((chips,)),
            dma,
            dma,
            dma,
            dma((chips,)),
            dma,
            dma((chips // 2,)),
            dma((units,)),
            dma,
            dma((3,)),
        ],
        compiler_params=pltpu.CompilerParams(
            collective_id=0, has_side_effects=True, vmem_limit_bytes=60 * 1024 * 1024
        ),
    )(
        query_hidden.reshape(query_rows, width),
        passage_hidden.reshape(passage_rows, width),
        query_logits,
        passage_logits,
        head_weight,
        query_mask,
        passage_mask,
        positive.reshape(1, -1),
        score_scale,
    )
    results = (grad_query, grad_passage, grad_weight)
    grad_query, grad_passage, grad_weight = pl.pallas_call(
        hand_over,
        out_shape=tuple(jax.ShapeDtypeStruct(r.shape, r.dtype) for r in results),
        in_specs=[main] * 3,
        out_specs=(main,) * 3,
        scratch_shapes=[pltpu.VMEM(r.shape, r.dtype) for r in results] + [dma((3,))],
        compiler_params=pltpu.CompilerParams(vmem_limit_bytes=60 * 1024 * 1024),
    )(*results)
    return (
        grad_query.reshape(query_hidden.shape[:2] + (2 * block,)),
        grad_passage.reshape(passage_hidden.shape[:2] + (2 * block,)),
        grad_weight,
    )


def solution(mesh):
    in_specs = (
        P("dp", None, None),
        P("dp", None, None),
        P("dp", None, "vocab"),
        P("dp", None, "vocab"),
        P("vocab", "dp"),
        P("dp", None),
        P("dp", None),
        P(),
        P(),
    )
    out_specs = (P("dp", None, "vocab"), P("dp", None, "vocab"), P("vocab", "dp"))
    return jax.shard_map(
        functools.partial(on_device, mesh.shape["dp"], mesh.shape["vocab"]),
        mesh=mesh,
        in_specs=in_specs,
        out_specs=out_specs,
        check_vma=False,
    )
```

```python
import functools

import jax
import jax.numpy as jnp
from jax import lax
from jax.experimental import pallas as pl
from jax.experimental.pallas import tpu as pltpu
from jax.sharding import PartitionSpec as P

MESH = pl.DeviceIdType.MESH
HIGHEST = lax.Precision.HIGHEST
LOSS_SCALE = 256.0
QUERY_WEIGHT = 3.0
PASSAGE_WEIGHT = 1.0
F32 = jnp.float32
BF16 = jnp.bfloat16
UNITS = 4


def pooled(logits, length):
    spots = lax.broadcasted_iota(jnp.int32, logits.shape, 0).astype(F32)
    masked = jnp.where(spots < length, logits, -jnp.inf)
    largest = jnp.max(masked, axis=0, keepdims=True)
    where = jnp.min(jnp.where(masked == largest, spots, 1e9), axis=0, keepdims=True)
    return largest, where


def kernel(
    groups,
    planes,
    query_hidden,
    passage_hidden,
    query_logits_in,
    passage_logits_in,
    weight_in,
    query_mask_in,
    passage_mask_in,
    positive_in,
    scale,
    grad_query,
    grad_passage,
    grad_weight,
    query_logits,
    passage_logits,
    weight,
    query_mask,
    passage_mask,
    positive,
    pools,
    spots,
    rep,
    push,
    part_out,
    part_in,
    part_sum,
    turned,
    mixed,
    held,
    hidden,
    tables,
    partial,
    stage,
    inbox,
    last,
    final,
    total,
    query_out,
    passage_out,
    weight_out,
    load,
    sent,
    pool_recv,
    twin_recv,
    spot_recv,
    spot_twin_recv,
    one_recv,
    two_recv,
    mixed_recv,
    mixed_twin_recv,
    hidden_recv,
    ring_recv,
    last_recv,
    leave,
):
    chips = groups // 2
    half = planes // 2
    query_length = query_logits.shape[1]
    passage_length = passage_logits.shape[1]
    vocab_local = query_logits.shape[2]
    query_rows = 2 * query_length
    rows = query_rows + 2 * passage_length
    width = weight.shape[1]
    queries = 2 * groups
    strip = 2 * width // chips
    span = rows * chips // UNITS
    me = lax.axis_index("dp")
    z = lax.axis_index("vocab")
    column = lax.div(me, 2)
    core = lax.rem(me, 2)
    twin = 2 * column + 1 - core
    pool_sent, twin_sent, spot_sent, spot_twin_sent, one_sent = (sent.at[i] for i in range(5))
    two_sent, mixed_sent, mixed_twin_sent, hidden_sent = (sent.at[i] for i in range(5, 9))
    ring_sent, last_sent = sent.at[9], sent.at[10]

    def ring(value, size):
        return lax.rem(value + 2 * size, size)

    def remote(source, dest, send, recv, target, plane):
        return pltpu.make_async_remote_copy(
            src_ref=source,
            dst_ref=dest,
            send_sem=send,
            recv_sem=recv,
            device_id=(target, plane),
            device_id_type=MESH,
        )

    def settle(ref, sem):
        pltpu.make_async_copy(ref, ref, sem).wait()

    loads = [
        pltpu.make_async_copy(source, dest, load.at[n])
        for n, (source, dest) in enumerate(
            (
                (query_mask_in, query_mask),
                (passage_mask_in, passage_mask),
                (query_logits_in, query_logits),
                (passage_logits_in, passage_logits),
                (weight_in, weight),
                (positive_in, positive),
                (query_hidden, held.at[pl.ds(0, query_rows)]),
                (passage_hidden, held.at[pl.ds(query_rows, rows - query_rows)]),
            )
        )
    ]
    for copy in loads:
        copy.start()

    barrier = pltpu.get_barrier_semaphore()

    def greet(dp_index, plane):
        pl.semaphore_signal(barrier, inc=1, device_id=(dp_index, plane), device_id_type=MESH)

    @pl.loop(1, planes)
    def _(i):
        greet(me, ring(z + i, planes))

    @pl.loop(1, groups)
    def _(i):
        greet(ring(me + i, groups), z)

    def lengths(mask):
        return jnp.sum(mask[...].astype(F32), axis=1, keepdims=True)

    for copy in loads[:4]:
        copy.wait()
    query_lengths = lengths(query_mask)
    passage_lengths = lengths(passage_mask)
    found = [pooled(query_logits[s], query_lengths[s : s + 1, :]) for s in range(2)]
    found += [pooled(passage_logits[s], passage_lengths[s : s + 1, :]) for s in range(2)]
    middle = vocab_local // 2

    def folded(lines):
        return jnp.concatenate(
            [line[:, :middle] for line in lines] + [line[:, middle:] for line in lines], axis=0
        )

    def slot_of(group):
        return lax.rem(group, 2) * chips + lax.div(group, 2)

    mine = slot_of(me)
    pools[mine] = folded([f[0] for f in found])
    spots[mine] = folded([f[1] for f in found])
    for copy in loads[4:]:
        copy.wait()
    turned[...] = weight[...].astype(F32).T.astype(BF16)

    pl.semaphore_wait(barrier, groups + planes - 2)

    def spread_out(ref, send, recv):
        @pl.loop(1, chips)
        def _(m):
            target = 2 * ring(column + m, chips) + core
            remote(ref.at[mine], ref.at[mine], send, recv, target, z).start()

    def pass_on(ref, recv, twin_send, twin_arrived):
        settle(ref.at[pl.ds(0, chips - 1)], recv)
        blocks = ref.at[pl.ds(core * chips, chips)]
        remote(blocks, blocks, twin_send, twin_arrived, twin, z).start()

    spread_out(pools, pool_sent, pool_recv)
    pass_on(pools, pool_recv, twin_sent, twin_recv)

    def strip_rows(ref, index):
        return ref.at[pl.ds(pl.multiple_of(index * strip, strip), strip)]

    @pl.loop(0, half)
    def _(i):
        chip = core * half + ring(i + column, half)

        @pl.when(chip != column)
        def _():
            remote(
                strip_rows(turned, chip - core * half),
                strip_rows(mixed, column),
                mixed_sent,
                mixed_recv,
                2 * chip + core,
                z,
            ).start()

        @pl.when(chip == column)
        def _():
            pltpu.make_async_copy(
                strip_rows(turned, chip - core * half),
                strip_rows(mixed, column),
                mixed_recv,
            ).start()

    takes_strips = core == lax.div(column, half)

    def pool_rows(k):
        return jnp.concatenate([pools[:, k, :], pools[:, 4 + k, :]], axis=1)

    settle(pools.at[pl.ds(0, chips)], twin_recv)
    for k in range(4):
        rep[k * groups : (k + 1) * groups, :] = jnp.log1p(jnp.maximum(pool_rows(k), 0.0))
    part = lax.dot_general(
        rep[pl.ds(pl.multiple_of(core * groups, groups), groups), :],
        rep[queries:, :],
        (((1,), (1,)), ((), ())),
        precision=HIGHEST,
        preferred_element_type=F32,
    )
    fold = groups // 2
    part_out[...] = jnp.concatenate([part[:fold, :], part[fold:, :]], axis=1)

    @pl.loop(1, planes)
    def _(i):
        remote(part_out, part_in.at[z], one_sent, one_recv, me, ring(z + i, planes)).start()

    part_in[z] = part_out[...]
    spread_out(spots, spot_sent, spot_recv)
    pass_on(spots, spot_recv, spot_twin_sent, spot_twin_recv)

    @pl.when(takes_strips)
    def _():
        settle(mixed, mixed_recv)
        remote(mixed, mixed, mixed_twin_sent, mixed_twin_recv, twin, z).start()

    pairs = chips // 2
    pair = lax.div(column, 2)

    def send_hidden(i):
        dest = hidden.at[pl.ds(pl.multiple_of(me * rows, rows), rows)]
        arrived = hidden_recv.at[pair]
        for n in range(4):
            target = 4 * ring(pair - i, pairs) + n
            block = held.at[:, pl.ds(pl.multiple_of(target * width, width), width)]

            @pl.when(target != me)
            def _():
                remote(block, dest, hidden_sent, arrived, target, z).start()

            @pl.when(target == me)
            def _():
                pltpu.make_async_copy(block, dest, arrived).start()

    @pl.loop(0, pairs // 2)
    def _(i):
        send_hidden(i)

    settle(part_in.at[pl.ds(0, planes - 1)], one_recv)
    summed = part_in[0]
    for b in range(1, planes):
        summed = summed + part_in[b]
    part_sum[core] = summed
    swap = remote(part_sum.at[core], part_sum.at[core], two_sent, two_recv, twin, z)
    swap.start()
    swap.wait_recv()

    factor = scale[0] / (vocab_local * planes)
    sums = jnp.concatenate(
        [part_sum[k][:, h * queries : (h + 1) * queries] for k in range(2) for h in range(2)],
        axis=0,
    )
    scores = sums * factor
    weights = jnp.exp(scores - jnp.max(scores, axis=1, keepdims=True))
    soft = weights / jnp.sum(weights, axis=1, keepdims=True)
    row = lax.broadcasted_iota(jnp.int32, scores.shape, 0)
    lane = lax.broadcasted_iota(jnp.int32, scores.shape, 1)

    def natural(index):
        k = jnp.where(index < groups, 0, 1)
        held_at = index - groups * k
        return 2 * jnp.where(held_at < chips, 2 * held_at, 2 * (held_at - chips) + 1) + k

    wanted = jnp.sum(
        jnp.where(
            lane == natural(row),
            jnp.broadcast_to(positive[...].astype(F32), scores.shape),
            0.0,
        ),
        axis=1,
        keepdims=True,
    )
    excess = soft - jnp.where(natural(lane).astype(F32) == wanted, 1.0, 0.0)
    nothing = jnp.zeros_like(excess)
    corner = jnp.concatenate(
        [
            jnp.concatenate([nothing, excess], axis=1),
            jnp.concatenate([nothing, nothing], axis=1),
        ],
        axis=0,
    )
    full_row = lax.broadcasted_iota(jnp.int32, corner.shape, 0)
    full_lane = lax.broadcasted_iota(jnp.int32, corner.shape, 1)
    query_part = jnp.logical_and(full_row < queries, full_lane < queries)
    passage_part = jnp.logical_and(full_row >= queries, full_lane >= queries)
    means = jnp.where(
        query_part,
        2.0 * QUERY_WEIGHT / queries / queries,
        jnp.where(passage_part, 2.0 * PASSAGE_WEIGHT / queries / queries, 0.0),
    )
    mixing = LOSS_SCALE * (factor * (corner + corner.T) + means)
    gradient = jnp.dot(mixing, rep[...], precision=HIGHEST, preferred_element_type=F32)
    for k in range(4):
        pool = pool_rows(k)
        slope = jnp.where(pool > 0.0, 1.0 / (1.0 + jnp.maximum(pool, 0.0)), 0.0)
        pushed = gradient[k * groups : (k + 1) * groups, :] * slope
        push[k * groups : (k + 1) * groups, :] = pushed.astype(BF16).astype(F32)

    settle(spots.at[pl.ds(0, chips)], spot_twin_recv)

    @pl.when(jnp.logical_not(takes_strips))
    def _():
        settle(mixed, mixed_twin_recv)

    def table_of(group):
        parts = []
        slot = slot_of(group)
        for k in range(4):
            length = query_length if k < 2 else passage_length
            push_row = push[pl.ds(k * groups + slot, 1), :]
            spot_row = jnp.concatenate(
                [spots[slot, k : k + 1, :], spots[slot, 4 + k : 5 + k, :]], axis=1
            )
            positions = lax.broadcasted_iota(jnp.int32, (length, vocab_local), 0).astype(F32)
            parts.append(jnp.where(positions == spot_row, push_row, 0.0).astype(BF16))
        return jnp.concatenate(parts, axis=0)

    def keep(group, value):
        tables[pl.ds(pl.multiple_of(group * rows, rows), rows), :] = value

    def sum_unit(u):
        members = [2 * j + core for j in range(u * (chips // UNITS), (u + 1) * (chips // UNITS))]
        parts = [table_of(group) for group in members]
        partial[:, u * span : (u + 1) * span] = lax.dot_general(
            mixed[...],
            jnp.concatenate(parts, axis=0),
            (((1,), (1,)), ((), ())),
            preferred_element_type=F32,
        )
        for group, value in zip(members, parts):
            keep(group, value)

    def own_part(plane, u):
        return partial[
            pl.ds(pl.multiple_of(plane * strip, strip), strip), u * span : (u + 1) * span
        ]

    def place(way, step, u):
        return (way * half + step) * UNITS + u

    def ring_copy(way, step, u):
        index = place(way, step, u)
        neighbour = ring(z + 1 - 2 * way, planes)
        return remote(
            stage.at[index], inbox.at[index], ring_sent, ring_recv.at[index], me, neighbour
        )

    def owner_of(way, step):
        return ring(z + (1 - 2 * way) * (half - step), planes)

    def ring_step(step, way, u, follows):
        value = own_part(owner_of(way, step), u)
        if follows:
            ring_copy(way, step - 1, u).wait_recv()
            value = value + inbox[place(way, step - 1, u)].astype(F32)
        stage[place(way, step, u)] = value.astype(BF16)
        ring_copy(way, step, u).start()

    def add_weight(i):
        taken = ring(pair + i, pairs)
        for n in range(2):
            other = 2 * (2 * taken + n) + 1 - core
            keep(other, table_of(other))
        batch = pl.ds(pl.multiple_of(taken * 4 * rows, rows), 4 * rows)
        settle(hidden.at[batch], hidden_recv.at[taken])
        total[...] += lax.dot_general(
            hidden[batch, :],
            tables[batch, :],
            (((0,), (0,)), ((), ())),
            preferred_element_type=F32,
        )

    for u in range(UNITS):
        way = 0 if u < UNITS // 2 else 1
        sum_unit(u)
        ring_step(0, way, u, False)
        ring_step(1, 1 - way, u, False)
    for u in range(UNITS):
        ring_step(1, 0 if u < UNITS // 2 else 1, u, True)

    @pl.loop(pairs // 2, pairs)
    def _(i):
        send_hidden(i)

    total[...] = jnp.zeros_like(total)

    @pl.loop(2, half)
    def _(step):
        for u in range(UNITS):
            for way in range(2):
                ring_step(step, way, u, True)
            if u == UNITS // 2 - 1:

                @pl.when(step >= 3)
                def _():
                    add_weight(step - 3)

    for u in range(UNITS):
        value = own_part(z, u)
        for way in range(2):
            ring_copy(way, half - 1, u).wait_recv()
            value = value + inbox[place(way, half - 1, u)].astype(F32)
        last[:, u * span : (u + 1) * span] = value.astype(BF16)

        @pl.loop(u * (chips // UNITS), (u + 1) * (chips // UNITS))
        def _(j):
            block = last.at[:, pl.ds(pl.multiple_of(j * rows, rows), rows)]
            dest = strip_rows(final, column)

            @pl.when(j != column)
            def _():
                remote(block, dest, last_sent, last_recv, 2 * j + core, z).start()

            @pl.when(j == column)
            def _():
                pltpu.make_async_copy(block, dest, last_recv).start()

    @pl.loop(max(0, half - 3), pairs)
    def _(i):
        add_weight(i)

    results = [
        pltpu.make_async_copy(source, dest, leave.at[n])
        for n, (source, dest) in enumerate(
            ((weight_out, grad_weight), (query_out, grad_query), (passage_out, grad_passage))
        )
    ]
    weight_out[...] = total[...].T
    results[0].start()

    settle(final, last_recv)
    whole = final[...].astype(F32).T.astype(BF16)
    query_out[...] = whole[:query_rows, :]
    passage_out[...] = whole[query_rows:, :]
    for copy in results[1:]:
        copy.start()

    settle(pools.at[pl.ds(0, chips - 1)], pool_sent)
    settle(pools.at[pl.ds(0, chips)], twin_sent)
    settle(spots.at[pl.ds(0, chips - 1)], spot_sent)
    settle(spots.at[pl.ds(0, chips)], spot_twin_sent)
    settle(part_in.at[pl.ds(0, planes - 1)], one_sent)
    swap.wait_send()

    @pl.when(takes_strips)
    def _():
        settle(mixed.at[pl.ds(0, (half - 1) * strip)], mixed_sent)
        settle(mixed, mixed_twin_sent)

    @pl.when(jnp.logical_not(takes_strips))
    def _():
        settle(mixed.at[pl.ds(0, half * strip)], mixed_sent)

    settle(hidden.at[pl.ds(0, (groups - 1) * rows)], hidden_sent)
    settle(stage.at[pl.ds(0, (2 * half - 1) * UNITS)], ring_sent)
    settle(last.at[:, pl.ds(0, (chips - 1) * rows)], last_sent)
    for copy in results:
        copy.wait()


def hand_over(*refs):
    count = (len(refs) - 1) // 3
    sources, dests, holds = refs[:count], refs[count : 2 * count], refs[2 * count : -1]
    arrive = [pltpu.make_async_copy(sources[n], holds[n], refs[-1].at[n]) for n in range(count)]
    leave = [pltpu.make_async_copy(holds[n], dests[n], refs[-1].at[n]) for n in range(count)]
    for copy in arrive:
        copy.start()
    for n in range(count):
        arrive[n].wait()
        leave[n].start()
    for copy in leave:
        copy.wait()


def on_device(
    groups,
    planes,
    query_hidden,
    passage_hidden,
    query_logits,
    passage_logits,
    head_weight,
    query_mask,
    passage_mask,
    positive,
    score_scale,
):
    width = query_hidden.shape[2]
    query_rows = query_hidden.shape[0] * query_hidden.shape[1]
    passage_rows = passage_hidden.shape[0] * passage_hidden.shape[1]
    rows = query_rows + passage_rows
    vocab_local, block = head_weight.shape
    chips = groups // 2
    half = planes // 2
    strip = 2 * block // chips
    sequences = 4 * groups
    main = pl.BlockSpec(memory_space=pltpu.HBM)
    units = 2 * half * UNITS
    span = rows * chips // UNITS
    dma = pltpu.SemaphoreType.DMA
    grad_query, grad_passage, grad_weight = pl.pallas_call(
        functools.partial(kernel, groups, planes),
        out_shape=(
            jax.ShapeDtypeStruct((query_rows, 2 * block), BF16),
            jax.ShapeDtypeStruct((passage_rows, 2 * block), BF16),
            jax.ShapeDtypeStruct((vocab_local, block), F32),
        ),
        in_specs=[main] * 8 + [pl.BlockSpec(memory_space=pltpu.SMEM)],
        out_specs=(main,) * 3,
        scratch_shapes=[
            pltpu.VMEM(query_logits.shape, F32),
            pltpu.VMEM(passage_logits.shape, F32),
            pltpu.VMEM(head_weight.shape, BF16),
            pltpu.VMEM(query_mask.shape, jnp.int32),
            pltpu.VMEM(passage_mask.shape, jnp.int32),
            pltpu.VMEM((1, positive.shape[0]), jnp.int32),
            pltpu.VMEM((groups, 8, vocab_local // 2), F32),
            pltpu.VMEM((groups, 8, vocab_local // 2), F32),
            pltpu.VMEM((sequences, vocab_local), F32),
            pltpu.VMEM((sequences, vocab_local), F32),
            pltpu.VMEM((chips, sequences), F32),
            pltpu.VMEM((planes, chips, sequences), F32),
            pltpu.VMEM((2, chips, sequences), F32),
            pltpu.VMEM((block, vocab_local), BF16),
            pltpu.VMEM((2 * block, vocab_local), BF16),
            pltpu.VMEM((rows, width), BF16),
            pltpu.VMEM((groups * rows, block), BF16),
            pltpu.VMEM((groups * rows, vocab_local), BF16),
            pltpu.VMEM((2 * block, chips * rows), F32),
            pltpu.VMEM((units, strip, span), BF16),
            pltpu.VMEM((units, strip, span), BF16),
            pltpu.VMEM((strip, chips * rows), BF16),
            pltpu.VMEM((2 * block, rows), BF16),
            pltpu.VMEM((block, vocab_local), F32),
            pltpu.VMEM((query_rows, 2 * block), BF16),
            pltpu.VMEM((passage_rows, 2 * block), BF16),
            pltpu.VMEM((vocab_local, block), F32),
            dma((8,)),
            dma((11,)),
            dma,
            dma,
            dma,
            dma,
            dma,
            dma,
            dma,
            dma,
            dma((chips // 2,)),
            dma((units,)),
            dma,
            dma((3,)),
        ],
        compiler_params=pltpu.CompilerParams(
            collective_id=0, has_side_effects=True, vmem_limit_bytes=60 * 1024 * 1024
        ),
    )(
        query_hidden.reshape(query_rows, width),
        passage_hidden.reshape(passage_rows, width),
        query_logits,
        passage_logits,
        head_weight,
        query_mask,
        passage_mask,
        positive.reshape(1, -1),
        score_scale,
    )
    results = (grad_query, grad_passage, grad_weight)
    grad_query, grad_passage, grad_weight = pl.pallas_call(
        hand_over,
        out_shape=tuple(jax.ShapeDtypeStruct(r.shape, r.dtype) for r in results),
        in_specs=[main] * 3,
        out_specs=(main,) * 3,
        scratch_shapes=[pltpu.VMEM(r.shape, r.dtype) for r in results] + [dma((3,))],
        compiler_params=pltpu.CompilerParams(vmem_limit_bytes=60 * 1024 * 1024),
    )(*results)
    return (
        grad_query.reshape(query_hidden.shape[:2] + (2 * block,)),
        grad_passage.reshape(passage_hidden.shape[:2] + (2 * block,)),
        grad_weight,
    )


def solution(mesh):
    in_specs = (
        P("dp", None, None),
        P("dp", None, None),
        P("dp", None, "vocab"),
        P("dp", None, "vocab"),
        P("vocab", "dp"),
        P("dp", None),
        P("dp", None),
        P(),
        P(),
    )
    out_specs = (P("dp", None, "vocab"), P("dp", None, "vocab"), P("vocab", "dp"))
    return jax.shard_map(
        functools.partial(on_device, mesh.shape["dp"], mesh.shape["vocab"]),
        mesh=mesh,
        in_specs=in_specs,
        out_specs=out_specs,
        check_vma=False,
    )
```

```python
import functools

import jax
import jax.numpy as jnp
from jax import lax
from jax.experimental import pallas as pl
from jax.experimental.pallas import tpu as pltpu
from jax.sharding import PartitionSpec as P

MESH = pl.DeviceIdType.MESH
HIGHEST = lax.Precision.HIGHEST
LOSS_SCALE = 256.0
QUERY_WEIGHT = 3.0
PASSAGE_WEIGHT = 1.0
F32 = jnp.float32
BF16 = jnp.bfloat16
UNITS = 4


def pooled(logits, length):
    spots = lax.broadcasted_iota(jnp.int32, logits.shape, 0).astype(F32)
    masked = jnp.where(spots < length, logits, -jnp.inf)
    largest = jnp.max(masked, axis=0, keepdims=True)
    where = jnp.min(jnp.where(masked == largest, spots, 1e9), axis=0, keepdims=True)
    return largest, where


def kernel(
    groups,
    planes,
    query_hidden,
    passage_hidden,
    query_logits_in,
    passage_logits_in,
    weight_in,
    query_mask_in,
    passage_mask_in,
    positive_in,
    scale,
    grad_query,
    grad_passage,
    grad_weight,
    query_logits,
    passage_logits,
    weight,
    query_mask,
    passage_mask,
    positive,
    pools,
    spots,
    rep,
    push,
    part_out,
    part_in,
    part_sum,
    turned,
    mixed,
    hidden,
    tables,
    partial,
    stage,
    inbox,
    last,
    final,
    total,
    query_out,
    passage_out,
    weight_out,
    load,
    sent,
    pool_recv,
    twin_recv,
    spot_recv,
    spot_twin_recv,
    one_recv,
    two_recv,
    mixed_recv,
    mixed_twin_recv,
    hidden_recv,
    ring_recv,
    last_recv,
    leave,
):
    chips = groups // 2
    half = planes // 2
    query_length = query_logits.shape[1]
    passage_length = passage_logits.shape[1]
    vocab_local = query_logits.shape[2]
    query_rows = 2 * query_length
    rows = query_rows + 2 * passage_length
    width = weight.shape[1]
    queries = 2 * groups
    strip = 2 * width // chips
    span = rows * chips // UNITS
    me = lax.axis_index("dp")
    z = lax.axis_index("vocab")
    column = lax.div(me, 2)
    core = lax.rem(me, 2)
    twin = 2 * column + 1 - core
    pool_sent, twin_sent, spot_sent, spot_twin_sent, one_sent = (sent.at[i] for i in range(5))
    two_sent, mixed_sent, mixed_twin_sent, hidden_sent = (sent.at[i] for i in range(5, 9))
    ring_sent, last_sent = sent.at[9], sent.at[10]

    def ring(value, size):
        return lax.rem(value + 2 * size, size)

    def remote(source, dest, send, recv, target, plane):
        return pltpu.make_async_remote_copy(
            src_ref=source,
            dst_ref=dest,
            send_sem=send,
            recv_sem=recv,
            device_id=(target, plane),
            device_id_type=MESH,
        )

    def settle(ref, sem):
        pltpu.make_async_copy(ref, ref, sem).wait()

    loads = [
        pltpu.make_async_copy(source, dest, load.at[n])
        for n, (source, dest) in enumerate(
            (
                (query_mask_in, query_mask),
                (passage_mask_in, passage_mask),
                (query_logits_in, query_logits),
                (passage_logits_in, passage_logits),
                (weight_in, weight),
                (positive_in, positive),
            )
        )
    ]
    for copy in loads:
        copy.start()

    barrier = pltpu.get_barrier_semaphore()

    def greet(dp_index, plane):
        pl.semaphore_signal(barrier, inc=1, device_id=(dp_index, plane), device_id_type=MESH)

    @pl.loop(1, planes)
    def _(i):
        greet(me, ring(z + i, planes))

    @pl.loop(1, groups)
    def _(i):
        greet(ring(me + i, groups), z)

    def lengths(mask):
        return jnp.sum(mask[...].astype(F32), axis=1, keepdims=True)

    for copy in loads[:4]:
        copy.wait()
    query_lengths = lengths(query_mask)
    passage_lengths = lengths(passage_mask)
    found = [pooled(query_logits[s], query_lengths[s : s + 1, :]) for s in range(2)]
    found += [pooled(passage_logits[s], passage_lengths[s : s + 1, :]) for s in range(2)]
    middle = vocab_local // 2

    def folded(lines):
        return jnp.concatenate(
            [line[:, :middle] for line in lines] + [line[:, middle:] for line in lines], axis=0
        )

    def slot_of(group):
        return lax.rem(group, 2) * chips + lax.div(group, 2)

    mine = slot_of(me)
    pools[mine] = folded([f[0] for f in found])
    spots[mine] = folded([f[1] for f in found])
    for copy in loads[4:]:
        copy.wait()
    turned[...] = weight[...].astype(F32).T.astype(BF16)

    pl.semaphore_wait(barrier, groups + planes - 2)

    def spread_out(ref, send, recv):
        @pl.loop(1, chips)
        def _(m):
            target = 2 * ring(column + m, chips) + core
            remote(ref.at[mine], ref.at[mine], send, recv, target, z).start()

    def pass_on(ref, recv, twin_send, twin_arrived):
        settle(ref.at[pl.ds(0, chips - 1)], recv)
        blocks = ref.at[pl.ds(core * chips, chips)]
        remote(blocks, blocks, twin_send, twin_arrived, twin, z).start()

    spread_out(pools, pool_sent, pool_recv)
    pass_on(pools, pool_recv, twin_sent, twin_recv)

    def strip_rows(ref, index):
        return ref.at[pl.ds(pl.multiple_of(index * strip, strip), strip)]

    @pl.loop(0, half)
    def _(i):
        chip = core * half + ring(i + column, half)

        @pl.when(chip != column)
        def _():
            remote(
                strip_rows(turned, chip - core * half),
                strip_rows(mixed, column),
                mixed_sent,
                mixed_recv,
                2 * chip + core,
                z,
            ).start()

        @pl.when(chip == column)
        def _():
            pltpu.make_async_copy(
                strip_rows(turned, chip - core * half),
                strip_rows(mixed, column),
                mixed_recv,
            ).start()

    takes_strips = core == lax.div(column, half)

    def pool_rows(k):
        return jnp.concatenate([pools[:, k, :], pools[:, 4 + k, :]], axis=1)

    settle(pools.at[pl.ds(0, chips)], twin_recv)
    for k in range(4):
        rep[k * groups : (k + 1) * groups, :] = jnp.log1p(jnp.maximum(pool_rows(k), 0.0))
    part = lax.dot_general(
        rep[pl.ds(pl.multiple_of(core * groups, groups), groups), :],
        rep[queries:, :],
        (((1,), (1,)), ((), ())),
        precision=HIGHEST,
        preferred_element_type=F32,
    )
    fold = groups // 2
    part_out[...] = jnp.concatenate([part[:fold, :], part[fold:, :]], axis=1)

    @pl.loop(1, planes)
    def _(i):
        remote(part_out, part_in.at[z], one_sent, one_recv, me, ring(z + i, planes)).start()

    part_in[z] = part_out[...]
    spread_out(spots, spot_sent, spot_recv)
    pass_on(spots, spot_recv, spot_twin_sent, spot_twin_recv)

    @pl.when(takes_strips)
    def _():
        settle(mixed, mixed_recv)
        remote(mixed, mixed, mixed_twin_sent, mixed_twin_recv, twin, z).start()

    pairs = chips // 2
    pair = lax.div(column, 2)

    def send_hidden(i):
        arrived = hidden_recv.at[pair]
        for n in range(4):
            target = 4 * ring(pair - i, pairs) + n
            columns = pl.ds(pl.multiple_of(target * width, width), width)
            for source, start, count in (
                (query_hidden, 0, query_rows),
                (passage_hidden, query_rows, rows - query_rows),
            ):
                block = source.at[:, columns]
                dest = hidden.at[pl.ds(pl.multiple_of(me * rows + start, 64), count)]

                @pl.when(target != me)
                def _():
                    remote(block, dest, hidden_sent, arrived, target, z).start()

                @pl.when(target == me)
                def _():
                    pltpu.make_async_copy(block, dest, arrived).start()

    @pl.loop(0, pairs // 2)
    def _(i):
        send_hidden(i)

    settle(part_in.at[pl.ds(0, planes - 1)], one_recv)
    summed = part_in[0]
    for b in range(1, planes):
        summed = summed + part_in[b]
    part_sum[core] = summed
    swap = remote(part_sum.at[core], part_sum.at[core], two_sent, two_recv, twin, z)
    swap.start()
    swap.wait_recv()

    factor = scale[0] / (vocab_local * planes)
    sums = jnp.concatenate(
        [part_sum[k][:, h * queries : (h + 1) * queries] for k in range(2) for h in range(2)],
        axis=0,
    )
    scores = sums * factor
    weights = jnp.exp(scores - jnp.max(scores, axis=1, keepdims=True))
    soft = weights / jnp.sum(weights, axis=1, keepdims=True)
    row = lax.broadcasted_iota(jnp.int32, scores.shape, 0)
    lane = lax.broadcasted_iota(jnp.int32, scores.shape, 1)

    def natural(index):
        k = jnp.where(index < groups, 0, 1)
        held_at = index - groups * k
        return 2 * jnp.where(held_at < chips, 2 * held_at, 2 * (held_at - chips) + 1) + k

    wanted = jnp.sum(
        jnp.where(
            lane == natural(row),
            jnp.broadcast_to(positive[...].astype(F32), scores.shape),
            0.0,
        ),
        axis=1,
        keepdims=True,
    )
    excess = soft - jnp.where(natural(lane).astype(F32) == wanted, 1.0, 0.0)
    nothing = jnp.zeros_like(excess)
    corner = jnp.concatenate(
        [
            jnp.concatenate([nothing, excess], axis=1),
            jnp.concatenate([nothing, nothing], axis=1),
        ],
        axis=0,
    )
    full_row = lax.broadcasted_iota(jnp.int32, corner.shape, 0)
    full_lane = lax.broadcasted_iota(jnp.int32, corner.shape, 1)
    query_part = jnp.logical_and(full_row < queries, full_lane < queries)
    passage_part = jnp.logical_and(full_row >= queries, full_lane >= queries)
    means = jnp.where(
        query_part,
        2.0 * QUERY_WEIGHT / queries / queries,
        jnp.where(passage_part, 2.0 * PASSAGE_WEIGHT / queries / queries, 0.0),
    )
    mixing = LOSS_SCALE * (factor * (corner + corner.T) + means)
    gradient = jnp.dot(mixing, rep[...], precision=HIGHEST, preferred_element_type=F32)
    for k in range(4):
        pool = pool_rows(k)
        slope = jnp.where(pool > 0.0, 1.0 / (1.0 + jnp.maximum(pool, 0.0)), 0.0)
        pushed = gradient[k * groups : (k + 1) * groups, :] * slope
        push[k * groups : (k + 1) * groups, :] = pushed.astype(BF16).astype(F32)

    settle(spots.at[pl.ds(0, chips)], spot_twin_recv)

    @pl.when(jnp.logical_not(takes_strips))
    def _():
        settle(mixed, mixed_twin_recv)

    def table_of(group):
        parts = []
        slot = slot_of(group)
        for k in range(4):
            length = query_length if k < 2 else passage_length
            push_row = push[pl.ds(k * groups + slot, 1), :]
            spot_row = jnp.concatenate(
                [spots[slot, k : k + 1, :], spots[slot, 4 + k : 5 + k, :]], axis=1
            )
            positions = lax.broadcasted_iota(jnp.int32, (length, vocab_local), 0).astype(F32)
            parts.append(jnp.where(positions == spot_row, push_row, 0.0).astype(BF16))
        return jnp.concatenate(parts, axis=0)

    def keep(group, value):
        tables[pl.ds(pl.multiple_of(group * rows, rows), rows), :] = value

    def sum_unit(u):
        members = [2 * j + core for j in range(u * (chips // UNITS), (u + 1) * (chips // UNITS))]
        parts = [table_of(group) for group in members]
        partial[:, u * span : (u + 1) * span] = lax.dot_general(
            mixed[...],
            jnp.concatenate(parts, axis=0),
            (((1,), (1,)), ((), ())),
            preferred_element_type=F32,
        )
        for group, value in zip(members, parts):
            keep(group, value)

    def own_part(plane, u):
        return partial[
            pl.ds(pl.multiple_of(plane * strip, strip), strip), u * span : (u + 1) * span
        ]

    def place(way, step, u):
        return (way * half + step) * UNITS + u

    def ring_copy(way, step, u):
        index = place(way, step, u)
        neighbour = ring(z + 1 - 2 * way, planes)
        return remote(
            stage.at[index], inbox.at[index], ring_sent, ring_recv.at[index], me, neighbour
        )

    def owner_of(way, step):
        return ring(z + (1 - 2 * way) * (half - step), planes)

    def ring_step(step, way, u, follows):
        value = own_part(owner_of(way, step), u)
        if follows:
            ring_copy(way, step - 1, u).wait_recv()
            value = value + inbox[place(way, step - 1, u)].astype(F32)
        stage[place(way, step, u)] = value.astype(BF16)
        ring_copy(way, step, u).start()

    def add_weight(i):
        taken = ring(pair + i, pairs)
        for n in range(2):
            other = 2 * (2 * taken + n) + 1 - core
            keep(other, table_of(other))
        batch = pl.ds(pl.multiple_of(taken * 4 * rows, rows), 4 * rows)
        settle(hidden.at[batch], hidden_recv.at[taken])
        total[...] += lax.dot_general(
            hidden[batch, :],
            tables[batch, :],
            (((0,), (0,)), ((), ())),
            preferred_element_type=F32,
        )

    for u in range(UNITS):
        way = 0 if u < UNITS // 2 else 1
        sum_unit(u)
        ring_step(0, way, u, False)
        ring_step(1, 1 - way, u, False)
    for u in range(UNITS):
        ring_step(1, 0 if u < UNITS // 2 else 1, u, True)

    @pl.loop(pairs // 2, pairs)
    def _(i):
        send_hidden(i)

    total[...] = jnp.zeros_like(total)

    @pl.loop(2, half)
    def _(step):
        for u in range(UNITS):
            for way in range(2):
                ring_step(step, way, u, True)
            if u == UNITS // 2 - 1:

                @pl.when(step >= 3)
                def _():
                    add_weight(step - 3)

    for u in range(UNITS):
        value = own_part(z, u)
        for way in range(2):
            ring_copy(way, half - 1, u).wait_recv()
            value = value + inbox[place(way, half - 1, u)].astype(F32)
        last[:, u * span : (u + 1) * span] = value.astype(BF16)

        @pl.loop(u * (chips // UNITS), (u + 1) * (chips // UNITS))
        def _(j):
            block = last.at[:, pl.ds(pl.multiple_of(j * rows, rows), rows)]
            dest = strip_rows(final, column)

            @pl.when(j != column)
            def _():
                remote(block, dest, last_sent, last_recv, 2 * j + core, z).start()

            @pl.when(j == column)
            def _():
                pltpu.make_async_copy(block, dest, last_recv).start()

    @pl.loop(max(0, half - 3), pairs)
    def _(i):
        add_weight(i)

    results = [
        pltpu.make_async_copy(source, dest, leave.at[n])
        for n, (source, dest) in enumerate(
            ((weight_out, grad_weight), (query_out, grad_query), (passage_out, grad_passage))
        )
    ]
    weight_out[...] = total[...].T
    results[0].start()

    settle(final, last_recv)
    whole = final[...].astype(F32).T.astype(BF16)
    query_out[...] = whole[:query_rows, :]
    passage_out[...] = whole[query_rows:, :]
    for copy in results[1:]:
        copy.start()

    settle(pools.at[pl.ds(0, chips - 1)], pool_sent)
    settle(pools.at[pl.ds(0, chips)], twin_sent)
    settle(spots.at[pl.ds(0, chips - 1)], spot_sent)
    settle(spots.at[pl.ds(0, chips)], spot_twin_sent)
    settle(part_in.at[pl.ds(0, planes - 1)], one_sent)
    swap.wait_send()

    @pl.when(takes_strips)
    def _():
        settle(mixed.at[pl.ds(0, (half - 1) * strip)], mixed_sent)
        settle(mixed, mixed_twin_sent)

    @pl.when(jnp.logical_not(takes_strips))
    def _():
        settle(mixed.at[pl.ds(0, half * strip)], mixed_sent)

    settle(hidden.at[pl.ds(0, (groups - 1) * rows)], hidden_sent)
    settle(stage.at[pl.ds(0, (2 * half - 1) * UNITS)], ring_sent)
    settle(last.at[:, pl.ds(0, (chips - 1) * rows)], last_sent)
    for copy in results:
        copy.wait()


def hand_over(*refs):
    count = (len(refs) - 1) // 3
    sources, dests, holds = refs[:count], refs[count : 2 * count], refs[2 * count : -1]
    arrive = [pltpu.make_async_copy(sources[n], holds[n], refs[-1].at[n]) for n in range(count)]
    leave = [pltpu.make_async_copy(holds[n], dests[n], refs[-1].at[n]) for n in range(count)]
    for copy in arrive:
        copy.start()
    for n in range(count):
        arrive[n].wait()
        leave[n].start()
    for copy in leave:
        copy.wait()


def on_device(
    groups,
    planes,
    query_hidden,
    passage_hidden,
    query_logits,
    passage_logits,
    head_weight,
    query_mask,
    passage_mask,
    positive,
    score_scale,
):
    width = query_hidden.shape[2]
    query_rows = query_hidden.shape[0] * query_hidden.shape[1]
    passage_rows = passage_hidden.shape[0] * passage_hidden.shape[1]
    rows = query_rows + passage_rows
    vocab_local, block = head_weight.shape
    chips = groups // 2
    half = planes // 2
    strip = 2 * block // chips
    sequences = 4 * groups
    main = pl.BlockSpec(memory_space=pltpu.HBM)
    units = 2 * half * UNITS
    span = rows * chips // UNITS
    dma = pltpu.SemaphoreType.DMA
    grad_query, grad_passage, grad_weight = pl.pallas_call(
        functools.partial(kernel, groups, planes),
        out_shape=(
            jax.ShapeDtypeStruct((query_rows, 2 * block), BF16),
            jax.ShapeDtypeStruct((passage_rows, 2 * block), BF16),
            jax.ShapeDtypeStruct((vocab_local, block), F32),
        ),
        in_specs=[main] * 8 + [pl.BlockSpec(memory_space=pltpu.SMEM)],
        out_specs=(main,) * 3,
        scratch_shapes=[
            pltpu.VMEM(query_logits.shape, F32),
            pltpu.VMEM(passage_logits.shape, F32),
            pltpu.VMEM(head_weight.shape, BF16),
            pltpu.VMEM(query_mask.shape, jnp.int32),
            pltpu.VMEM(passage_mask.shape, jnp.int32),
            pltpu.VMEM((1, positive.shape[0]), jnp.int32),
            pltpu.VMEM((groups, 8, vocab_local // 2), F32),
            pltpu.VMEM((groups, 8, vocab_local // 2), F32),
            pltpu.VMEM((sequences, vocab_local), F32),
            pltpu.VMEM((sequences, vocab_local), F32),
            pltpu.VMEM((chips, sequences), F32),
            pltpu.VMEM((planes, chips, sequences), F32),
            pltpu.VMEM((2, chips, sequences), F32),
            pltpu.VMEM((block, vocab_local), BF16),
            pltpu.VMEM((2 * block, vocab_local), BF16),
            pltpu.VMEM((groups * rows, block), BF16),
            pltpu.VMEM((groups * rows, vocab_local), BF16),
            pltpu.VMEM((2 * block, chips * rows), F32),
            pltpu.VMEM((units, strip, span), BF16),
            pltpu.VMEM((units, strip, span), BF16),
            pltpu.VMEM((strip, chips * rows), BF16),
            pltpu.VMEM((2 * block, rows), BF16),
            pltpu.VMEM((block, vocab_local), F32),
            pltpu.VMEM((query_rows, 2 * block), BF16),
            pltpu.VMEM((passage_rows, 2 * block), BF16),
            pltpu.VMEM((vocab_local, block), F32),
            dma((6,)),
            dma((11,)),
            dma,
            dma,
            dma,
            dma,
            dma,
            dma,
            dma,
            dma,
            dma((chips // 2,)),
            dma((units,)),
            dma,
            dma((3,)),
        ],
        compiler_params=pltpu.CompilerParams(
            collective_id=0, has_side_effects=True, vmem_limit_bytes=60 * 1024 * 1024
        ),
    )(
        query_hidden.reshape(query_rows, width),
        passage_hidden.reshape(passage_rows, width),
        query_logits,
        passage_logits,
        head_weight,
        query_mask,
        passage_mask,
        positive.reshape(1, -1),
        score_scale,
    )
    results = (grad_query, grad_passage, grad_weight)
    grad_query, grad_passage, grad_weight = pl.pallas_call(
        hand_over,
        out_shape=tuple(jax.ShapeDtypeStruct(r.shape, r.dtype) for r in results),
        in_specs=[main] * 3,
        out_specs=(main,) * 3,
        scratch_shapes=[pltpu.VMEM(r.shape, r.dtype) for r in results] + [dma((3,))],
        compiler_params=pltpu.CompilerParams(vmem_limit_bytes=60 * 1024 * 1024),
    )(*results)
    return (
        grad_query.reshape(query_hidden.shape[:2] + (2 * block,)),
        grad_passage.reshape(passage_hidden.shape[:2] + (2 * block,)),
        grad_weight,
    )


def solution(mesh):
    in_specs = (
        P("dp", None, None),
        P("dp", None, None),
        P("dp", None, "vocab"),
        P("dp", None, "vocab"),
        P("vocab", "dp"),
        P("dp", None),
        P("dp", None),
        P(),
        P(),
    )
    out_specs = (P("dp", None, "vocab"), P("dp", None, "vocab"), P("vocab", "dp"))
    return jax.shard_map(
        functools.partial(on_device, mesh.shape["dp"], mesh.shape["vocab"]),
        mesh=mesh,
        in_specs=in_specs,
        out_specs=out_specs,
        check_vma=False,
    )
```
